32 devices in a mesh: seq: 8 (over z, y), head: 4 (over x, core).
Axes of the slice: x: 2, y: 2, z: 4, core: 2. Of those that a mesh axis runs over, the one named last changes fastest.
Arguments:
- x_heads: bfloat16 [4096, 32768], P(('head', 'seq')), may hold values from -6 to 6
- b_proj: bfloat16 [32768, 128], P(('seq', 'head')), may hold values from -0.5 to 0.5
- c_proj: bfloat16 [32768, 128], P(('seq', 'head')), may hold values from -6 to 6
- log_gate: float32 [64, 32768], P('head', 'seq'), may hold values from -3 to 0, as said below
- step_size: float32 [64, 32768], P('head', 'seq'), may hold values from 0.003 to 0.03
- level_weight: float32 [64, 8, 32768], P('head', None, 'seq'), may hold values from 0.25 to 4
- skip: float32 [64], P('head'), may hold values from 0.5 to 1.5
Outputs:
- y_heads: bfloat16 [4096, 32768], P(('head', 'seq'))
The draws below stay inside these ranges and needn't reach their ends.
Inputs may be any that keep to these rules, and one draw needn't show every extreme that they name: log_gate holds no positive values.
All inputs are finite; a program needn't handle non-finite values.
Results may differ from the reference program's by a relative error of at most 0.0064.
Values may be sent and summed in bfloat16 or wider, within the bound.
No kernel may reach another device: no remote copies, remote signals or barrier semaphores. Data moves between devices by JAX's collectives and lax.ppermute only.
A program may use at most 192 MiB of HBM per device.

```python
import math
import jax
import jax.numpy as jnp
import numpy as np
from jax import lax

H = 64
P_SIZE = 64
N = 128
Q = 256
TOKEN_COUNT = 32768
LEVELS = 8


def draw_log_gate(key, part):
    sequence_lanes = jax.random.split(key, 6)
    fast_share = 0.5
    is_fast = jax.random.uniform(sequence_lanes[0], (H,)) < fast_share
    fast_rate = jax.random.uniform(sequence_lanes[1], (H,), minval=1.0 / 50.0, maxval=1.0 / 30.0)
    slow_rate = jax.random.uniform(sequence_lanes[2], (H,), minval=0.2, maxval=0.8) / TOKEN_COUNT
    head_decay_rate = jnp.where(is_fast, fast_rate, slow_rate)
    random_noise = jnp.exp(jax.random.uniform(sequence_lanes[3], (H, TOKEN_COUNT), minval=-math.log(2.0), maxval=math.log(2.0)))
    surge_position = jax.random.randint(sequence_lanes[4], (3,), 0, TOKEN_COUNT)
    surge_log_value = jax.random.uniform(sequence_lanes[5], (3,), minval=math.log(0.5), maxval=math.log(0.8))
    token_positions = jnp.arange(TOKEN_COUNT)
    surge_events = jnp.sum(jnp.where(token_positions[None, :] == surge_position[:, None], surge_log_value[:, None], 0.0), axis=0)
    return (-head_decay_rate[:, None] * random_noise + surge_events[None, :]).astype(jnp.float32)


def levels(stream_key, shape, pieces, smallest, high):
    loudness, own = 1.0, jax.random.fold_in(stream_key, 6)
    for position, blocks in pieces:
        steps = jnp.exp(jax.random.uniform(jax.random.fold_in(own, position), (blocks,), jnp.float32, smallest / len(pieces), high / len(pieces)))
        loudness = loudness * jnp.repeat(steps, shape[position] // blocks).reshape([-1 if axis == position else 1 for axis in range(len(shape))])
    return loudness


def noise(rng, dims, width, most, pieces=(), held_as=jnp.bfloat16):
    level = levels(rng, dims, pieces, -0.22, 0.18) if pieces else 1.0
    result = jax.random.normal(rng, dims, jnp.float32) * width * level
    return jnp.minimum(jnp.maximum(result, -most), most).astype(held_as)


def setup_inputs(seed: int = 0) -> dict:
    splits = jax.random.split(jax.random.key(seed), 8)
    return {
        "x_heads": noise(splits[0], (H * P_SIZE, TOKEN_COUNT), 1.0, 6.0, ((0, 32),)),
        "b_proj": noise(splits[1], (TOKEN_COUNT, N), N ** -0.5, 0.5, ((0, 32),)),
        "c_proj": noise(splits[2], (TOKEN_COUNT, N), 1.0, 6.0, ((0, 32),)),
        "log_gate": draw_log_gate(jax.random.fold_in(splits[7], 71), 0),
        "step_size": jnp.clip(jnp.exp(math.log(0.03) - 2.3025851 * jax.random.uniform(splits[4], (H, TOKEN_COUNT), jnp.float32) ** levels(splits[4], (H, TOKEN_COUNT), ((0, 4), (1, 8)), -0.2, 0.2)), 0.003, 0.03),
        "level_weight": jnp.clip(jnp.exp(math.log(4.0) - 2.7725887 * jax.random.uniform(splits[5], (H, LEVELS, TOKEN_COUNT), jnp.float32) ** levels(splits[5], (H, LEVELS, TOKEN_COUNT), ((0, 4), (2, 8)), -0.2, 0.2)), 0.25, 4.0),
        "skip": jnp.clip(0.5 + 1.0 * jax.random.uniform(splits[6], (H,), jnp.float32) ** levels(splits[6], (H,), ((0, 4),), -0.2, 0.2), 0.5, 1.5),
    }


very_negative = -1.0e30


def head_output(head_values, gate_row, step_row, weight_rows, skip_one, query_all, key_all, scores):
    span_total = TOKEN_COUNT // Q
    tree_levels = LEVELS - 1
    cumulative = jnp.cumsum(gate_row.reshape(span_total, Q), axis=1)
    step_blocks = step_row.reshape(span_total, Q)
    token_positions = jnp.arange(Q)
    causal = token_positions[:, None] >= token_positions[None, :]
    log_gaps = jnp.where(causal[None], cumulative[:, :, None] - cumulative[:, None, :], very_negative)
    mixing = (scores * jnp.exp(log_gaps) * step_blocks[:, None, :]).astype(jnp.bfloat16)
    values = head_values.reshape(P_SIZE, span_total, Q).astype(jnp.float32)
    local_part = jnp.einsum('cij,pcj->pci', mixing.astype(jnp.float32), values)
    local_part = local_part * weight_rows[0].reshape(span_total, Q)[None]
    span_log = cumulative[:, -1]
    weighted = (values * (jnp.exp(span_log[:, None] - cumulative) * step_blocks)[None]).astype(jnp.bfloat16)
    states = jnp.einsum('cjn,pcj->cnp', key_all, weighted.astype(jnp.float32))
    starts = jnp.concatenate([jnp.zeros((1,), jnp.float32), jnp.cumsum(span_log)])
    aggregate = states
    block_log = span_log
    level_part = jnp.zeros((P_SIZE, span_total, Q), jnp.float32)
    span_ids = np.arange(span_total)
    for depth_bit in range(tree_levels):
        blocks = span_ids >> depth_bit
        left_block = np.maximum(blocks - 1, 0)
        has_bit = ((blocks & 1) == 1).astype(np.float32)
        decays = jnp.exp(starts[span_ids] - starts[blocks << depth_bit]) * has_bit
        level_state = (aggregate[left_block] * decays[:, None, None]).astype(jnp.bfloat16)
        scaled = (weight_rows[depth_bit + 1].reshape(span_total, Q)[:, :, None] * query_all).astype(jnp.bfloat16)
        level_part = level_part + jnp.einsum('cin,cnp->pci', scaled.astype(jnp.float32), level_state.astype(jnp.float32))
        if depth_bit + 1 < tree_levels:
            pairs = aggregate.reshape(-1, 2, N, P_SIZE)
            pair_logs = block_log.reshape(-1, 2)
            aggregate = jnp.exp(pair_logs[:, 1])[:, None, None] * pairs[:, 0] + pairs[:, 1]
            block_log = pair_logs[:, 0] + pair_logs[:, 1]
    output_tile = local_part + jnp.exp(cumulative)[None] * level_part + skip_one * values
    return output_tile.reshape(P_SIZE, TOKEN_COUNT).astype(jnp.bfloat16)


def reference(x_heads, b_proj, c_proj, log_gate, step_size, level_weight, skip):
    span_total = TOKEN_COUNT // Q
    key_all = b_proj.astype(jnp.float32).reshape(span_total, Q, N)
    query_all = c_proj.astype(jnp.float32).reshape(span_total, Q, N)
    scores = jnp.einsum('cin,cjn->cij', query_all, key_all)
    head_rows = x_heads.reshape(H, P_SIZE, TOKEN_COUNT)

    def one_head(packed):
        head_values, gate_row, step_row, weight_rows, skip_one = packed
        return head_output(head_values, gate_row, step_row, weight_rows, skip_one, query_all, key_all, scores)

    outputs = lax.map(one_head, (head_rows, log_gate, step_size, level_weight, skip))
    return outputs.reshape(H * P_SIZE, TOKEN_COUNT)
```

```python
import functools
import math

import jax
import jax.numpy as jnp
from jax import lax
from jax.experimental import pallas as pl
from jax.experimental.pallas import tpu as pltpu
from jax.sharding import PartitionSpec as P

P_SIZE = 64
N = 128
Q = 256
HALF = Q // 2
GROUP = 8
LOG2E = math.log2(math.e)
VMEM_LIMIT = 48 * 1024 * 1024

f32 = jnp.float32
bf16 = jnp.bfloat16


def dot(a, b):
    return lax.dot_general(a, b, (((1,), (0,)), ((), ())), preferred_element_type=f32)


def dot_nt(a, b):
    return lax.dot_general(a, b, (((1,), (1,)), ((), ())), preferred_element_type=f32)


def exact_parts(value):
    high = value.astype(bf16)
    rest = value - high.astype(f32)
    middle = rest.astype(bf16)
    low = (rest - middle.astype(f32)).astype(bf16)
    return high, middle, low


def gates_kernel(heads, levels, padded, gates_ref, weight_ref, cum_ref, offset_ref, decay_ref, merge_ref,
                 log_scratch):
    shards, _, span_rows, _ = gates_ref.shape
    spans = shards * span_rows
    upper = (
        lax.broadcasted_iota(jnp.int32, (Q, Q), 0) <= lax.broadcasted_iota(jnp.int32, (Q, Q), 1)
    ).astype(f32).astype(bf16)
    chunk = min(spans, 64)
    for head in range(heads):
        for shard in range(shards):
            rows = pl.ds(shard * span_rows, span_rows)
            gate = gates_ref[shard, 2 * head]
            step = gates_ref[shard, 2 * head + 1]
            high, middle, low = exact_parts(gate)
            cumulative = (dot(high, upper) + dot(middle, upper) + dot(low, upper)) * LOG2E
            span_log = cumulative[:, Q - 1 :]
            cum_ref[head, rows, :] = cumulative
            offset_ref[head, rows, :] = cumulative - jnp.log2(step)
            weight_ref[head, rows, :] = jnp.exp2(span_log - cumulative) * step
            log_scratch[rows, :] = jnp.broadcast_to(span_log, (span_rows, N))
        high, middle, low = exact_parts(log_scratch[...])

        def some_spans(at, carry):
            first = at * chunk
            size = (chunk * padded, spans)
            row = lax.broadcasted_iota(jnp.int32, size, 0)
            span = first + row // padded
            level = row % padded
            other = lax.broadcasted_iota(jnp.int32, size, 1)
            out_rows = pl.ds(pl.multiple_of(first * padded, chunk * padded), chunk * padded)
            bit = jnp.maximum(level - 1, 0)
            before = (other >= (span >> bit) << bit) & (other < span)
            before = before.astype(f32).astype(bf16)
            decay_ref[head, out_rows, :] = dot(before, high) + dot(before, middle) + dot(before, low)
            right = (other > span - (1 << bit)) & (other <= span)
            right = right.astype(f32).astype(bf16)
            merge_ref[head, out_rows, :] = jnp.exp2(
                dot(right, high) + dot(right, middle) + dot(right, low)
            )
            return carry

        lax.fori_loop(0, spans // chunk, some_spans, 0)


def states_kernel(heads, width, group, bits, padded, x_ref, key_ref, weight_ref, merge_ref, tree_ref, high_ref):
    step = pl.program_id(0)
    low_bits = group.bit_length() - 1

    def factor(local, bit):
        row = local * padded + bit + 1
        return [merge_ref[head, row : row + 1, :] for head in range(heads)]

    def merge(left, right, scale):
        parts = []
        for head in range(heads):
            rows = slice(head * width, (head + 1) * width)
            parts.append(left[rows] * scale[head] + right[rows])
        return jnp.concatenate(parts, axis=0) if heads > 1 else parts[0]

    kept = {}
    for local in range(group):
        columns = slice(local * Q, (local + 1) * Q)
        parts = [
            (
                x_ref[head * width : (head + 1) * width, columns].astype(f32)
                * weight_ref[head, local : local + 1, :]
            ).astype(bf16)
            for head in range(heads)
        ]
        weighted = jnp.concatenate(parts, axis=0) if heads > 1 else parts[0]
        state = dot(weighted, key_ref[columns, :])
        bit = 0
        while bit < low_bits and local >> bit & 1:
            state = merge(kept[bit], state, factor(local, bit))
            bit += 1
        if bit < low_bits:
            kept[bit] = state
            tree_ref[local] = state.astype(bf16)
            continue
        high_count = bits - low_bits
        if high_count <= 0:
            tree_ref[local] = state.astype(bf16)
            continue
        tree_ref[local] = state.astype(bf16)
        for high in range(high_count):
            ones = (1 << high) - 1

            @pl.when((step & ones) == ones)
            def _(high=high, ones=ones):
                whole = state if high == 0 else high_ref[high_count]
                stays = ((step >> high) & 1) == 0

                @pl.when(stays)
                def _():
                    high_ref[high] = whole
                    tree_ref[local] = whole.astype(bf16)

                @pl.when(jnp.logical_not(stays))
                def _():
                    scale = factor(local, low_bits + high)
                    merged = merge(high_ref[high], whole, scale)
                    high_ref[high_count] = merged
                    tree_ref[local] = merged.astype(bf16)


def outputs_kernel(heads, width, group, bits, padded, skip_ref, x_ref, key_ref, query_ref, tree_ref, cum_ref,
                   offset_ref, decay_ref, level_ref, out_ref, total_ref, factor_ref):
    step = pl.program_id(0)
    low_bits = group.bit_length() - 1
    levels = bits + 1
    causal = lax.broadcasted_iota(jnp.int32, (HALF, HALF), 0) <= lax.broadcasted_iota(
        jnp.int32, (HALF, HALF), 1
    )
    total_ref[...] = jnp.zeros_like(total_ref)
    level_all = level_ref[0].astype(f32)
    for head in range(heads):
        for local in range(group):
            columns = slice(local * Q, (local + 1) * Q)
            decay = decay_ref[head, local * padded : local * padded + levels, :]
            decay = jnp.concatenate([decay] * (Q // N), axis=1)
            tile = jnp.exp2(cum_ref[head, local : local + 1, :] + decay)
            factor_ref[head, :levels, columns] = (
                level_all[head * levels : (head + 1) * levels, columns] * tile
            )

    for bit in range(low_bits, bits):
        place = bit - low_bits

        @pl.when(((step >> place) & 1) == 1)
        def _(bit=bit, place=place):
            slot = (step >> place << place) * group - 1
            part = dot_nt(tree_ref[slot], query_ref[...])
            for head in range(heads):
                rows = slice(head * width, (head + 1) * width)
                total_ref[rows, :] += part[rows] * factor_ref[head, bit + 1 : bit + 2, :]

    offsets = [jnp.transpose(offset_ref[head]) for head in range(heads)]
    for local in range(group):
        columns = slice(local * Q, (local + 1) * Q)
        keys = key_ref[columns, :]
        queries = query_ref[columns, :]
        scores = dot_nt(keys, queries)
        first = jnp.where(causal, scores[:HALF, :HALF], 0.0)
        cross = scores[:HALF, HALF:]
        second = jnp.where(causal, scores[HALF:, HALF:], 0.0)
        parts = []
        for bit in range(low_bits):
            if local >> bit & 1:
                slot = step * group + ((local >> bit) << bit) - 1
                parts.append((bit, dot_nt(tree_ref[slot], queries)))
        for head in range(heads):
            rows = slice(head * width, (head + 1) * width)
            cumulative = cum_ref[head, local : local + 1, :]
            offset = offsets[head][:, local : local + 1]
            upper = offset[:HALF]
            lower = offset[HALF:]
            left = cumulative[:, :HALF]
            right = cumulative[:, HALF:]
            mixing = jnp.concatenate(
                [
                    jnp.concatenate(
                        [
                            (first * jnp.exp2(jnp.minimum(left - upper, 64.0))).astype(bf16),
                            (cross * jnp.exp2(right - upper)).astype(bf16),
                        ],
                        axis=1,
                    ),
                    jnp.concatenate(
                        [
                            jnp.zeros((HALF, HALF), bf16),
                            (second * jnp.exp2(jnp.minimum(right - lower, 64.0))).astype(bf16),
                        ],
                        axis=1,
                    ),
                ],
                axis=0,
            )
            values = x_ref[rows, columns]
            own = level_all[head * levels : head * levels + 1, columns]
            result = dot(values, mixing) * own + total_ref[rows, columns]
            result += skip_ref[head] * values.astype(f32)
            for bit, part in parts:
                result += part[rows] * factor_ref[head, bit + 1 : bit + 2, columns]
            out_ref[rows, columns] = result.astype(bf16)


def on_device(x_heads, b_proj, c_proj, log_gate, step_size, level_weight, skip):
    rows, tokens = x_heads.shape
    head_count, tok_dev = log_gate.shape
    levels = level_weight.shape[1]
    bits = levels - 1
    shards = lax.axis_size("seq")
    span_rows = tok_dev // Q
    spans = tokens // Q
    heads = max(rows // P_SIZE, 1)
    width = rows // heads
    sharing = P_SIZE // width
    group = min(GROUP, span_rows)
    padded = -(-levels // 8) * 8
    steps = spans // group

    keys = lax.all_gather(b_proj, ("seq", "head"), axis=0, tiled=True)
    queries = lax.all_gather(c_proj, ("seq", "head"), axis=0, tiled=True)

    def to_owners(value):
        value = jnp.repeat(value, sharing, axis=0) if sharing > 1 else value
        value = value.reshape((shards, heads) + value.shape[1:])
        return value.reshape((shards, -1) + value.shape[3:])

    gates = jnp.stack(
        [log_gate.reshape(head_count, span_rows, Q), step_size.reshape(head_count, span_rows, Q)], axis=1
    )
    gates = lax.all_to_all(to_owners(gates), "seq", split_axis=0, concat_axis=0, tiled=True)
    level_rows = lax.all_to_all(
        to_owners(level_weight.astype(bf16)), "seq", split_axis=0, concat_axis=0, tiled=True
    )
    first_head = lax.axis_index("seq") * rows // P_SIZE
    own_skip = lax.dynamic_slice_in_dim(skip, first_head, heads, 0)

    params = functools.partial(pltpu.CompilerParams, vmem_limit_bytes=VMEM_LIMIT)
    weight, cumulative, offset, decay, merge = pl.pallas_call(
        functools.partial(gates_kernel, heads, levels, padded),
        out_shape=[jax.ShapeDtypeStruct((heads, spans, Q), f32)] * 3
        + [jax.ShapeDtypeStruct((heads, spans * padded, N), f32)] * 2,
        scratch_shapes=[pltpu.VMEM((spans, N), f32)],
        compiler_params=params(),
        name="gates",
    )(gates)

    x_spec = pl.BlockSpec((rows, group * Q), lambda g: (0, g))
    token_spec = pl.BlockSpec((group * Q, N), lambda g: (g, 0))
    span_spec = pl.BlockSpec((heads, group, Q), lambda g: (0, g, 0))
    level_spec = pl.BlockSpec((heads, group * padded, N), lambda g: (0, g, 0))
    tree = pl.pallas_call(
        functools.partial(states_kernel, heads, width, group, bits, padded),
        grid=(steps,),
        in_specs=[x_spec, token_spec, span_spec, level_spec],
        out_specs=pl.BlockSpec((group, rows, N), lambda g: (g, 0, 0)),
        out_shape=jax.ShapeDtypeStruct((spans, rows, N), bf16),
        scratch_shapes=[pltpu.VMEM((max(bits - group.bit_length() + 2, 1), rows, N), f32)],
        compiler_params=params(),
        cost_estimate=pl.CostEstimate(
            flops=2 * rows * tokens * N, bytes_accessed=2 * (rows * tokens + tokens * N), transcendentals=0
        ),
        name="states",
    )(x_heads, keys, weight, merge)

    per_shard = span_rows // group
    return pl.pallas_call(
        functools.partial(outputs_kernel, heads, width, group, bits, padded),
        grid=(steps,),
        in_specs=[
            pl.BlockSpec(memory_space=pltpu.SMEM),
            x_spec,
            token_spec,
            token_spec,
            pl.BlockSpec(memory_space=pltpu.VMEM),
            span_spec,
            span_spec,
            level_spec,
            pl.BlockSpec((1, heads * levels, group * Q), lambda g: (g // per_shard, 0, g % per_shard)),
        ],
        out_specs=x_spec,
        out_shape=jax.ShapeDtypeStruct((rows, tokens), bf16),
        scratch_shapes=[
            pltpu.VMEM((rows, group * Q), f32),
            pltpu.VMEM((heads, padded, group * Q), f32),
        ],
        compiler_params=params(),
        cost_estimate=pl.CostEstimate(
            flops=2 * tokens * (Q * N + rows * Q + bits * rows * N),
            bytes_accessed=4 * (rows * tokens + tokens * N),
            transcendentals=heads * tokens * Q,
        ),
        name="outputs",
    )(own_skip, x_heads, keys, queries, tree, cumulative, offset, decay, level_rows)


def solution(mesh):
    in_specs = (
        P(("head", "seq"), None),
        P(("seq", "head"), None),
        P(("seq", "head"), None),
        P("head", "seq"),
        P("head", "seq"),
        P("head", None, "seq"),
        P("head"),
    )
    out_specs = P(("head", "seq"), None)
    return jax.shard_map(
        on_device, mesh=mesh, in_specs=in_specs, out_specs=out_specs, check_vma=False
    )
```

```python
import functools
import math

import jax
import jax.numpy as jnp
from jax import lax
from jax.experimental import pallas as pl
from jax.experimental.pallas import tpu as pltpu
from jax.sharding import PartitionSpec as P

P_SIZE = 64
N = 128
Q = 256
HALF = Q // 2
CORES = 2
LOG2E = math.log2(math.e)
VMEM_LIMIT = 48 * 1024 * 1024

f32 = jnp.float32
bf16 = jnp.bfloat16


def dot(a, b):
    return lax.dot_general(a, b, (((1,), (0,)), ((), ())), preferred_element_type=f32)


def exact_parts(value):
    high = value.astype(bf16)
    rest = value - high.astype(f32)
    middle = rest.astype(bf16)
    low = (rest - middle.astype(f32)).astype(bf16)
    return high, middle, low


def gates_kernel(heads, levels, padded, gates_ref, weight_ref, cum_ref, offset_ref, decay_ref, merge_ref,
                 log_scratch):
    shards, _, span_rows, _ = gates_ref.shape
    spans = shards * span_rows
    upper = (
        lax.broadcasted_iota(jnp.int32, (Q, Q), 0) <= lax.broadcasted_iota(jnp.int32, (Q, Q), 1)
    ).astype(f32).astype(bf16)
    chunk = min(spans, 64)
    for head in range(heads):
        for shard in range(shards):
            rows = pl.ds(shard * span_rows, span_rows)
            gate = gates_ref[shard, 2 * head]
            step = gates_ref[shard, 2 * head + 1]
            high, middle, low = exact_parts(gate)
            cumulative = (dot(high, upper) + dot(middle, upper) + dot(low, upper)) * LOG2E
            span_log = cumulative[:, Q - 1 :]
            cum_ref[head, rows, :] = cumulative
            offset_ref[head, rows, :] = cumulative - jnp.log2(step)
            weight_ref[head, rows, :] = jnp.exp2(span_log - cumulative) * step
            log_scratch[rows, :] = jnp.broadcast_to(span_log, (span_rows, N))
        high, middle, low = exact_parts(log_scratch[...])

        def some_spans(at, carry):
            first = at * chunk
            size = (chunk * padded, spans)
            row = lax.broadcasted_iota(jnp.int32, size, 0)
            span = first + row // padded
            level = row % padded
            other = lax.broadcasted_iota(jnp.int32, size, 1)
            out_rows = pl.ds(pl.multiple_of(first * padded, chunk * padded), chunk * padded)
            bit = jnp.maximum(level - 1, 0)
            before = (other >= (span >> bit) << bit) & (other < span)
            before = before.astype(f32).astype(bf16)
            decay_ref[head, out_rows, :] = dot(before, high) + dot(before, middle) + dot(before, low)
            right = (other > span - (1 << bit)) & (other <= span)
            right = right.astype(f32).astype(bf16)
            merge_ref[head, out_rows, :] = jnp.exp2(
                dot(right, high) + dot(right, middle) + dot(right, low)
            )
            return carry

        lax.fori_loop(0, spans // chunk, some_spans, 0)


def pick(core, mine_ref, other_ref, local, group):
    half = group // CORES
    rows = slice(local % half * Q, (local % half + 1) * Q)
    return jnp.where(core == local // half, mine_ref[rows, :], other_ref[rows, :])


def states_kernel(heads, width, group, bits, padded, core_ref, x_ref, mine_ref, other_ref, weight_ref, merge_ref,
                  tree_ref, high_ref):
    step = pl.program_id(0)
    low_bits = group.bit_length() - 1

    def factor(local, bit):
        row = local * padded + bit + 1
        return [merge_ref[head, row : row + 1, :] for head in range(heads)]

    def merge(left, right, scale):
        parts = []
        for head in range(heads):
            rows = slice(head * width, (head + 1) * width)
            parts.append(left[rows] * scale[head] + right[rows])
        return jnp.concatenate(parts, axis=0) if heads > 1 else parts[0]

    kept = {}
    for local in range(group):
        columns = slice(local * Q, (local + 1) * Q)
        parts = [
            (
                x_ref[head * width : (head + 1) * width, columns].astype(f32)
                * weight_ref[head, local : local + 1, :]
            ).astype(bf16)
            for head in range(heads)
        ]
        weighted = jnp.concatenate(parts, axis=0) if heads > 1 else parts[0]
        state = dot(weighted, pick(core_ref[0], mine_ref, other_ref, local, group))
        bit = 0
        while bit < low_bits and local >> bit & 1:
            state = merge(kept[bit], state, factor(local, bit))
            bit += 1
        if bit < low_bits:
            kept[bit] = state
            tree_ref[local] = state.astype(bf16)
            continue
        high_count = bits - low_bits
        if high_count <= 0:
            tree_ref[local] = state.astype(bf16)
            continue
        tree_ref[local] = state.astype(bf16)
        for high in range(high_count):
            ones = (1 << high) - 1

            @pl.when((step & ones) == ones)
            def _(high=high, ones=ones):
                whole = state if high == 0 else high_ref[high_count]
                stays = ((step >> high) & 1) == 0

                @pl.when(stays)
                def _():
                    high_ref[high] = whole
                    tree_ref[local] = whole.astype(bf16)

                @pl.when(jnp.logical_not(stays))
                def _():
                    scale = factor(local, low_bits + high)
                    merged = merge(high_ref[high], whole, scale)
                    high_ref[high_count] = merged
                    tree_ref[local] = merged.astype(bf16)


def outputs_kernel(heads, width, group, bits, padded, core_ref, skip_ref, x_ref, my_key_ref,
                   other_key_ref, my_query_ref, other_query_ref, tree_ref, cum_ref, offset_ref, decay_ref, level_ref,
                   out_ref, total_ref, factor_ref, query_ref):
    step = pl.program_id(0)
    low_bits = group.bit_length() - 1
    levels = bits + 1
    causal = lax.broadcasted_iota(jnp.int32, (HALF, HALF), 0) <= lax.broadcasted_iota(
        jnp.int32, (HALF, HALF), 1
    )
    total_ref[...] = jnp.zeros_like(total_ref)
    for local in range(group):
        columns = slice(local * Q, (local + 1) * Q)
        query_ref[:, columns] = jnp.transpose(pick(core_ref[0], my_query_ref, other_query_ref, local, group))
    level_all = level_ref[0].astype(f32)
    for head in range(heads):
        for local in range(group):
            columns = slice(local * Q, (local + 1) * Q)
            decay = decay_ref[head, local * padded : local * padded + levels, :]
            decay = jnp.concatenate([decay] * (Q // N), axis=1)
            tile = jnp.exp2(cum_ref[head, local : local + 1, :] + decay)
            factor_ref[head, :levels, columns] = (
                level_all[head * levels : (head + 1) * levels, columns] * tile
            )

    for bit in range(low_bits, bits):
        place = bit - low_bits

        @pl.when(((step >> place) & 1) == 1)
        def _(bit=bit, place=place):
            slot = (step >> place << place) * group - 1
            part = dot(tree_ref[slot], query_ref[...])
            for head in range(heads):
                rows = slice(head * width, (head + 1) * width)
                total_ref[rows, :] += part[rows] * factor_ref[head, bit + 1 : bit + 2, :]

    offsets = [jnp.transpose(offset_ref[head]) for head in range(heads)]
    for local in range(group):
        columns = slice(local * Q, (local + 1) * Q)
        keys = pick(core_ref[0], my_key_ref, other_key_ref, local, group)
        queries = query_ref[:, columns]
        scores = dot(keys, queries)
        first = jnp.where(causal, scores[:HALF, :HALF], 0.0)
        cross = scores[:HALF, HALF:]
        second = jnp.where(causal, scores[HALF:, HALF:], 0.0)
        parts = []
        for bit in range(low_bits):
            if local >> bit & 1:
                slot = step * group + ((local >> bit) << bit) - 1
                parts.append((bit, dot(tree_ref[slot], queries)))
        for head in range(heads):
            rows = slice(head * width, (head + 1) * width)
            cumulative = cum_ref[head, local : local + 1, :]
            offset = offsets[head][:, local : local + 1]
            upper = offset[:HALF]
            lower = offset[HALF:]
            left = cumulative[:, :HALF]
            right = cumulative[:, HALF:]
            mixing = jnp.concatenate(
                [
                    jnp.concatenate(
                        [
                            (first * jnp.exp2(jnp.minimum(left - upper, 64.0))).astype(bf16),
                            (cross * jnp.exp2(right - upper)).astype(bf16),
                        ],
                        axis=1,
                    ),
                    jnp.concatenate(
                        [
                            jnp.zeros((HALF, HALF), bf16),
                            (second * jnp.exp2(jnp.minimum(right - lower, 64.0))).astype(bf16),
                        ],
                        axis=1,
                    ),
                ],
                axis=0,
            )
            values = x_ref[rows, columns]
            own = level_all[head * levels : head * levels + 1, columns]
            result = dot(values, mixing) * own + total_ref[rows, columns]
            result += skip_ref[head] * values.astype(f32)
            for bit, part in parts:
                result += part[rows] * factor_ref[head, bit + 1 : bit + 2, columns]
            out_ref[rows, columns] = result.astype(bf16)


def on_device(x_heads, b_proj, c_proj, log_gate, step_size, level_weight, skip):
    rows, tokens = x_heads.shape
    head_count, tok_dev = log_gate.shape
    levels = level_weight.shape[1]
    bits = levels - 1
    shards = lax.axis_size("seq")
    span_rows = tok_dev // Q
    spans = tokens // Q
    heads = max(rows // P_SIZE, 1)
    width = rows // heads
    sharing = P_SIZE // width
    group = CORES * b_proj.shape[0] // Q
    padded = -(-levels // 8) * 8
    steps = spans // group

    swap = [(core, 1 - core) for core in range(CORES)]
    my_keys = lax.all_gather(b_proj, ("seq", "x"), axis=0, tiled=True)
    my_queries = lax.all_gather(c_proj, ("seq", "x"), axis=0, tiled=True)
    other_keys = lax.ppermute(my_keys, "core", swap)
    other_queries = lax.ppermute(my_queries, "core", swap)
    core = lax.axis_index("core").astype(jnp.int32).reshape(1)

    def to_owners(value):
        value = jnp.repeat(value, sharing, axis=0) if sharing > 1 else value
        value = value.reshape((shards, heads) + value.shape[1:])
        return value.reshape((shards, -1) + value.shape[3:])

    gates = jnp.stack(
        [log_gate.reshape(head_count, span_rows, Q), step_size.reshape(head_count, span_rows, Q)], axis=1
    )
    gates = lax.all_to_all(to_owners(gates), "seq", split_axis=0, concat_axis=0, tiled=True)
    level_rows = lax.all_to_all(
        to_owners(level_weight.astype(bf16)), "seq", split_axis=0, concat_axis=0, tiled=True
    )
    first_head = lax.axis_index("seq") * rows // P_SIZE
    own_skip = lax.dynamic_slice_in_dim(skip, first_head, heads, 0)

    params = functools.partial(pltpu.CompilerParams, vmem_limit_bytes=VMEM_LIMIT)
    weight, cumulative, offset, decay, merge = pl.pallas_call(
        functools.partial(gates_kernel, heads, levels, padded),
        out_shape=[jax.ShapeDtypeStruct((heads, spans, Q), f32)] * 3
        + [jax.ShapeDtypeStruct((heads, spans * padded, N), f32)] * 2,
        scratch_shapes=[pltpu.VMEM((spans, N), f32)],
        compiler_params=params(),
        name="gates",
    )(gates)

    x_spec = pl.BlockSpec((rows, group * Q), lambda g: (0, g))
    token_spec = pl.BlockSpec((group // CORES * Q, N), lambda g: (g, 0))
    scalar_spec = pl.BlockSpec(memory_space=pltpu.SMEM)
    weight, cumulative, offset = [v.reshape(heads, steps, group, Q) for v in (weight, cumulative, offset)]
    span_spec = pl.BlockSpec((heads, None, group, Q), lambda g: (0, g, 0, 0))
    level_spec = pl.BlockSpec((heads, group * padded, N), lambda g: (0, g, 0))
    tree = pl.pallas_call(
        functools.partial(states_kernel, heads, width, group, bits, padded),
        grid=(steps,),
        in_specs=[scalar_spec, x_spec, token_spec, token_spec, span_spec, level_spec],
        out_specs=pl.BlockSpec((group, rows, N), lambda g: (g, 0, 0)),
        out_shape=jax.ShapeDtypeStruct((spans, rows, N), bf16),
        scratch_shapes=[pltpu.VMEM((max(bits - group.bit_length() + 2, 1), rows, N), f32)],
        compiler_params=params(),
        cost_estimate=pl.CostEstimate(
            flops=2 * rows * tokens * N, bytes_accessed=2 * (rows * tokens + tokens * N), transcendentals=0
        ),
        name="states",
    )(core, x_heads, my_keys, other_keys, weight, merge)

    per_shard = span_rows // group
    return pl.pallas_call(
        functools.partial(outputs_kernel, heads, width, group, bits, padded),
        grid=(steps,),
        in_specs=[
            scalar_spec,
            scalar_spec,
            x_spec,
            token_spec,
            token_spec,
            token_spec,
            token_spec,
            pl.BlockSpec(memory_space=pltpu.VMEM),
            span_spec,
            span_spec,
            level_spec,
            pl.BlockSpec((1, heads * levels, group * Q), lambda g: (g // per_shard, 0, g % per_shard)),
        ],
        out_specs=x_spec,
        out_shape=jax.ShapeDtypeStruct((rows, tokens), bf16),
        scratch_shapes=[
            pltpu.VMEM((rows, group * Q), f32),
            pltpu.VMEM((heads, padded, group * Q), f32),
            pltpu.VMEM((N, group * Q), bf16),
        ],
        compiler_params=params(),
        cost_estimate=pl.CostEstimate(
            flops=2 * tokens * (Q * N + rows * Q + bits * rows * N),
            bytes_accessed=4 * (rows * tokens + tokens * N),
            transcendentals=heads * tokens * Q,
        ),
        name="outputs",
    )(core, own_skip, x_heads, my_keys, other_keys, my_queries, other_queries, tree, cumulative, offset, decay,
      level_rows)


def solution(mesh):
    chips = mesh.shape["head"] // CORES
    devices = mesh.devices.reshape(mesh.shape["seq"], chips, CORES)
    split_mesh = jax.sharding.Mesh(devices, ("seq", "x", "core"))
    head = ("x", "core")
    in_specs = (
        P((*head, "seq"), None),
        P(("seq", *head), None),
        P(("seq", *head), None),
        P(head, "seq"),
        P(head, "seq"),
        P(head, None, "seq"),
        P(head),
    )
    out_specs = P((*head, "seq"), None)
    return jax.shard_map(
        on_device, mesh=split_mesh, in_specs=in_specs, out_specs=out_specs, check_vma=False
    )
```

```python
import functools
import math

import jax
import jax.numpy as jnp
from jax import lax
from jax.experimental import pallas as pl
from jax.experimental.pallas import tpu as pltpu
from jax.sharding import PartitionSpec as P

P_SIZE = 64
N = 128
Q = 256
HALF = Q // 2
CORES = 2
LOG2E = math.log2(math.e)
VMEM_LIMIT = 48 * 1024 * 1024

f32 = jnp.float32
bf16 = jnp.bfloat16


def dot(a, b):
    return lax.dot_general(a, b, (((1,), (0,)), ((), ())), preferred_element_type=f32)


def exact_parts(value):
    high = value.astype(bf16)
    rest = value - high.astype(f32)
    middle = rest.astype(bf16)
    low = (rest - middle.astype(f32)).astype(bf16)
    return high, middle, low


def gates_kernel(heads, levels, padded, gates_ref, weight_ref, cum_ref, offset_ref, decay_ref, merge_ref,
                 log_scratch):
    shards, _, span_rows, _ = gates_ref.shape
    spans = shards * span_rows
    upper = (
        lax.broadcasted_iota(jnp.int32, (Q, Q), 0) <= lax.broadcasted_iota(jnp.int32, (Q, Q), 1)
    ).astype(f32).astype(bf16)
    chunk = min(spans, 64)
    for head in range(heads):
        for shard in range(shards):
            rows = pl.ds(shard * span_rows, span_rows)
            gate = gates_ref[shard, 2 * head]
            step = gates_ref[shard, 2 * head + 1]
            high, middle, low = exact_parts(gate)
            cumulative = (dot(high, upper) + dot(middle, upper) + dot(low, upper)) * LOG2E
            span_log = cumulative[:, Q - 1 :]
            cum_ref[head, rows, :] = cumulative
            offset_ref[head, rows, :] = cumulative - jnp.log2(step)
            weight_ref[head, rows, :] = jnp.exp2(span_log - cumulative) * step
            log_scratch[rows, :] = jnp.broadcast_to(span_log, (span_rows, N))
        high, middle, low = exact_parts(log_scratch[...])

        def some_spans(at, carry):
            first = at * chunk
            size = (chunk * padded, spans)
            row = lax.broadcasted_iota(jnp.int32, size, 0)
            span = first + row // padded
            level = row % padded
            other = lax.broadcasted_iota(jnp.int32, size, 1)
            out_rows = pl.ds(pl.multiple_of(first * padded, chunk * padded), chunk * padded)
            bit = jnp.maximum(level - 1, 0)
            before = (other >= (span >> bit) << bit) & (other < span)
            before = before.astype(f32).astype(bf16)
            decay_ref[head, out_rows, :] = dot(before, high) + dot(before, middle) + dot(before, low)
            right = (other > span - (1 << bit)) & (other <= span)
            right = right.astype(f32).astype(bf16)
            merge_ref[head, out_rows, :] = jnp.exp2(
                dot(right, high) + dot(right, middle) + dot(right, low)
            )
            return carry

        lax.fori_loop(0, spans // chunk, some_spans, 0)


def pick(core, mine_ref, other_ref, local, group):
    half = group // CORES
    rows = slice(local % half * Q, (local % half + 1) * Q)
    return jnp.where(core == local // half, mine_ref[rows, :], other_ref[rows, :])


def merge_blocks(left, right, merge_ref, row, width):
    parts = []
    for head in range(merge_ref.shape[0]):
        rows = slice(head * width, (head + 1) * width)
        parts.append(left[rows] * merge_ref[head, row : row + 1, :] + right[rows])
    return jnp.concatenate(parts, axis=0) if len(parts) > 1 else parts[0]


def states_kernel(heads, width, group, padded, groups_ref, core_ref, x_ref, mine_ref, other_ref, weight_ref,
                  merge_ref, low_ref, total_ref):
    kept = {}
    for local in range(group):
        columns = slice(local * Q, (local + 1) * Q)
        parts = [
            (
                x_ref[head * width : (head + 1) * width, columns].astype(f32)
                * weight_ref[head, local : local + 1, :]
            ).astype(bf16)
            for head in range(heads)
        ]
        weighted = jnp.concatenate(parts, axis=0) if heads > 1 else parts[0]
        state = dot(weighted, pick(core_ref[0], mine_ref, other_ref, local, group))
        bit = 0
        while local >> bit & 1:
            state = merge_blocks(kept[bit], state, merge_ref, local * padded + bit + 1, width)
            bit += 1
        kept[bit] = state
        if local < group - 1:
            low_ref[local] = state.astype(bf16)
    total_ref[...] = state


def tree_kernel(width, group, padded, groups_ref, merge_ref, *refs):
    *total_refs, high_ref, order_ref = refs
    steps = order_ref.shape[0]
    low_bits = group.bit_length() - 1
    at = 0
    for total_ref in total_refs:
        for slot in range(total_ref.shape[0]):
            order_ref[groups_ref[at]] = total_ref[slot]
            at += 1
    kept = {}
    for step in range(steps):
        state = order_ref[step]
        bit = 0
        while step >> bit & 1:
            row = ((step + 1) * group - 1) * padded + low_bits + bit + 1
            state = merge_blocks(kept[bit], state, merge_ref, row, width)
            bit += 1
        kept[bit] = state
        high_ref[step] = state.astype(bf16)


def outputs_kernel(heads, width, group, bits, padded, groups_ref, core_ref, skip_ref, x_ref, my_key_ref,
                   other_key_ref, my_query_ref, other_query_ref, low_ref, high_ref, cum_ref, offset_ref, decay_ref,
                   level_ref, *refs):
    out_ref, total_ref, factor_ref, query_ref = refs[-4:]
    step = groups_ref[pl.program_id(0)]
    low_bits = group.bit_length() - 1
    levels = bits + 1
    causal = lax.broadcasted_iota(jnp.int32, (HALF, HALF), 0) <= lax.broadcasted_iota(
        jnp.int32, (HALF, HALF), 1
    )
    total_ref[...] = jnp.zeros_like(total_ref)
    for local in range(group):
        columns = slice(local * Q, (local + 1) * Q)
        query_ref[:, columns] = jnp.transpose(pick(core_ref[0], my_query_ref, other_query_ref, local, group))
    level_all = level_ref[0].astype(f32)
    for head in range(heads):
        for local in range(group):
            columns = slice(local * Q, (local + 1) * Q)
            decay = decay_ref[head, local * padded : local * padded + levels, :]
            decay = jnp.concatenate([decay] * (Q // N), axis=1)
            tile = jnp.exp2(cum_ref[head, local : local + 1, :] + decay)
            factor_ref[head, :levels, columns] = (
                level_all[head * levels : (head + 1) * levels, columns] * tile
            )

    for bit in range(low_bits, bits):
        place = bit - low_bits

        @pl.when(((step >> place) & 1) == 1)
        def _(bit=bit, place=place):
            part = dot(high_ref[(step >> place << place) - 1], query_ref[...])
            for head in range(heads):
                rows = slice(head * width, (head + 1) * width)
                total_ref[rows, :] += part[rows] * factor_ref[head, bit + 1 : bit + 2, :]

    offsets = [jnp.transpose(offset_ref[head]) for head in range(heads)]
    for local in range(group):
        columns = slice(local * Q, (local + 1) * Q)
        keys = pick(core_ref[0], my_key_ref, other_key_ref, local, group)
        queries = query_ref[:, columns]
        scores = dot(keys, queries)
        first = jnp.where(causal, scores[:HALF, :HALF], 0.0)
        cross = scores[:HALF, HALF:]
        second = jnp.where(causal, scores[HALF:, HALF:], 0.0)
        parts = []
        for bit in range(low_bits):
            if local >> bit & 1:
                slot = ((local >> bit) << bit) - 1
                parts.append((bit, dot(low_ref[slot], queries)))
        for head in range(heads):
            rows = slice(head * width, (head + 1) * width)
            cumulative = cum_ref[head, local : local + 1, :]
            offset = offsets[head][:, local : local + 1]
            upper = offset[:HALF]
            lower = offset[HALF:]
            left = cumulative[:, :HALF]
            right = cumulative[:, HALF:]
            mixing = jnp.concatenate(
                [
                    jnp.concatenate(
                        [
                            (first * jnp.exp2(jnp.minimum(left - upper, 64.0))).astype(bf16),
                            (cross * jnp.exp2(right - upper)).astype(bf16),
                        ],
                        axis=1,
                    ),
                    jnp.concatenate(
                        [
                            jnp.zeros((HALF, HALF), bf16),
                            (second * jnp.exp2(jnp.minimum(right - lower, 64.0))).astype(bf16),
                        ],
                        axis=1,
                    ),
                ],
                axis=0,
            )
            values = x_ref[rows, columns]
            own = level_all[head * levels : head * levels + 1, columns]
            result = dot(values, mixing) * own + total_ref[rows, columns]
            result += skip_ref[head] * values.astype(f32)
            for bit, part in parts:
                result += part[rows] * factor_ref[head, bit + 1 : bit + 2, columns]
            out_ref[rows, columns] = result.astype(bf16)


def exchange(value, axis, distance):
    pairs = [(place, place ^ distance) for place in range(lax.axis_size(axis))]
    return lax.ppermute(value, axis, pairs)


def along_z(own):
    pieces = [own]
    for distance in range(1, lax.axis_size("z")):
        low = distance & -distance
        pieces.append(exchange(pieces[distance ^ low], "z", low))
    return pieces


def in_plane(piece):
    half = piece.shape[0] // 2
    far = {}
    for distance in range(1, lax.axis_size("x")):
        far[0, distance] = exchange(piece, "x", distance)
    for distance in range(1, lax.axis_size("y")):
        far[distance, 0] = exchange(piece, "y", distance)
    for y in range(1, lax.axis_size("y")):
        for x in range(1, lax.axis_size("x")):
            first = exchange(far[0, x][:half], "y", y)
            second = exchange(far[y, 0][half:], "x", x)
            far[y, x] = jnp.concatenate([first, second], axis=0)
    return {(0, 0): piece, **far}


def both_cores(plane):
    return {place: (piece, exchange(piece, "core", 1)) for place, piece in plane.items()}


def gather(own):
    pieces = along_z(own)
    near = both_cores(in_plane(own))
    if len(pieces) == 1:
        return [near]
    return [near, both_cores(in_plane(jnp.concatenate(pieces[1:], axis=0)))]


def on_device(x_heads, b_proj, c_proj, log_gate, step_size, level_weight, skip):
    rows, tokens = x_heads.shape
    head_count, tok_dev = log_gate.shape
    levels = level_weight.shape[1]
    bits = levels - 1
    shards = lax.axis_size(("z", "y"))
    span_rows = tok_dev // Q
    spans = tokens // Q
    heads = max(rows // P_SIZE, 1)
    width = rows // heads
    sharing = P_SIZE // width
    block = b_proj.shape[0]
    group = CORES * block // Q
    padded = -(-levels // 8) * 8
    steps = spans // group
    per_shard = span_rows // group

    def to_owners(value):
        value = jnp.repeat(value, sharing, axis=0) if sharing > 1 else value
        value = value.reshape((shards, heads) + value.shape[1:])
        return value.reshape((shards, -1) + value.shape[3:])

    gates = jnp.stack(
        [log_gate.reshape(head_count, span_rows, Q), step_size.reshape(head_count, span_rows, Q)], axis=1
    )
    gates = lax.all_to_all(to_owners(gates), ("z", "y"), split_axis=0, concat_axis=0, tiled=True)
    key_sets = gather(b_proj)
    level_rows = lax.all_to_all(
        to_owners(level_weight.astype(bf16)), ("z", "y"), split_axis=0, concat_axis=0, tiled=True
    )
    query_sets = gather(c_proj)
    first_head = lax.axis_index(("z", "y")) * rows // P_SIZE
    own_skip = lax.dynamic_slice_in_dim(skip, first_head, heads, 0)
    core = lax.axis_index("core").astype(jnp.int32).reshape(1)

    def group_ids(batch, place):
        distances = jnp.arange(1) if batch == 0 else jnp.arange(1, lax.axis_size("z"))
        z = lax.axis_index("z") ^ distances
        y = lax.axis_index("y") ^ place[0]
        x = lax.axis_index("x") ^ place[1]
        return ((z * lax.axis_size("y") + y) * lax.axis_size("x") + x).astype(jnp.int32)

    params = pltpu.CompilerParams(vmem_limit_bytes=VMEM_LIMIT)
    weight, cumulative, offset, decay, merge = pl.pallas_call(
        functools.partial(gates_kernel, heads, levels, padded),
        out_shape=[jax.ShapeDtypeStruct((heads, spans, Q), f32)] * 3
        + [jax.ShapeDtypeStruct((heads, spans * padded, N), f32)] * 2,
        scratch_shapes=[pltpu.VMEM((spans, N), f32)],
        compiler_params=params,
        name="gates",
    )(gates)
    weight, cumulative, offset = [v.reshape(heads, steps, group, Q) for v in (weight, cumulative, offset)]

    x_spec = pl.BlockSpec((rows, group * Q), lambda i, ids, *_: (0, ids[i]))
    token_spec = pl.BlockSpec((block, N), lambda i, *_: (i, 0))
    span_spec = pl.BlockSpec((heads, None, group, Q), lambda i, ids, *_: (0, ids[i], 0, 0))
    level_spec = pl.BlockSpec((heads, group * padded, N), lambda i, ids, *_: (0, ids[i], 0))
    low_slots = max(group - 1, 1)
    low_spec = pl.BlockSpec((None, low_slots, rows, N), lambda i, *_: (i, 0, 0, 0))

    sets = [
        (group_ids(batch, place), key_sets[batch][place], query_sets[batch][place])
        for batch in range(len(key_sets))
        for place in sorted(key_sets[batch], key=lambda place: ((place[0] > 0) + (place[1] > 0), place))
    ]
    lows, totals = [], []
    for ids, keys, _ in sets:
        count = ids.shape[0]
        low, total = pl.pallas_call(
            functools.partial(states_kernel, heads, width, group, padded),
            grid_spec=pltpu.PrefetchScalarGridSpec(
                num_scalar_prefetch=2,
                grid=(count,),
                in_specs=[x_spec, token_spec, token_spec, span_spec, level_spec],
                out_specs=[low_spec, pl.BlockSpec((None, rows, N), lambda i, *_: (i, 0, 0))],
            ),
            out_shape=[
                jax.ShapeDtypeStruct((count, low_slots, rows, N), bf16),
                jax.ShapeDtypeStruct((count, rows, N), f32),
            ],
            compiler_params=params,
            cost_estimate=pl.CostEstimate(
                flops=2 * rows * count * group * Q * N,
                bytes_accessed=4 * count * group * Q * (rows + N),
                transcendentals=0,
            ),
            name="states",
        )(ids, core, x_heads, *keys, weight, merge)
        lows.append(low)
        totals.append(total)

    vmem = pl.BlockSpec(memory_space=pltpu.VMEM)
    high = pl.pallas_call(
        functools.partial(tree_kernel, width, group, padded),
        grid_spec=pltpu.PrefetchScalarGridSpec(
            num_scalar_prefetch=1,
            in_specs=[vmem] * (1 + len(totals)),
            out_specs=vmem,
            scratch_shapes=[pltpu.VMEM((steps, rows, N), f32)],
        ),
        out_shape=jax.ShapeDtypeStruct((steps, rows, N), bf16),
        compiler_params=params,
        name="tree",
    )(jnp.concatenate([ids for ids, _, _ in sets]), merge, *totals)

    out = None
    for (ids, keys, queries), low in zip(sets, lows):
        count = ids.shape[0]
        tokens_here = count * group * Q
        before = [] if out is None else [out]
        out = pl.pallas_call(
            functools.partial(outputs_kernel, heads, width, group, bits, padded),
            grid_spec=pltpu.PrefetchScalarGridSpec(
                num_scalar_prefetch=2,
                grid=(count,),
                in_specs=[
                    pl.BlockSpec(memory_space=pltpu.SMEM),
                    x_spec,
                    token_spec,
                    token_spec,
                    token_spec,
                    token_spec,
                    low_spec,
                    vmem,
                    span_spec,
                    span_spec,
                    level_spec,
                    pl.BlockSpec(
                        (1, heads * levels, group * Q),
                        lambda i, ids, *_: (ids[i] // per_shard, 0, ids[i] % per_shard),
                    ),
                ]
                + [pl.BlockSpec(memory_space=pl.ANY)] * len(before),
                out_specs=x_spec,
                scratch_shapes=[
                    pltpu.VMEM((rows, group * Q), f32),
                    pltpu.VMEM((heads, padded, group * Q), f32),
                    pltpu.VMEM((N, group * Q), bf16),
                ],
            ),
            out_shape=jax.ShapeDtypeStruct((rows, tokens), bf16),
            input_output_aliases={14: 0} if before else {},
            compiler_params=params,
            cost_estimate=pl.CostEstimate(
                flops=2 * tokens_here * (Q * N + rows * Q + bits * rows * N),
                bytes_accessed=4 * tokens_here * (rows + N),
                transcendentals=heads * tokens_here * Q,
            ),
            name="outputs",
        )(ids, core, own_skip, x_heads, *keys, *queries, low, high, cumulative, offset, decay, level_rows, *before)
    return out


def solution(mesh):
    x = mesh.shape["head"] // CORES
    y = math.gcd(mesh.shape["seq"], x)
    z = mesh.shape["seq"] // y
    split_mesh = jax.sharding.Mesh(mesh.devices.reshape(z, y, x, CORES), ("z", "y", "x", "core"))
    seq = ("z", "y")
    head = ("x", "core")
    in_specs = (
        P((*head, *seq), None),
        P((*seq, *head), None),
        P((*seq, *head), None),
        P(head, seq),
        P(head, seq),
        P(head, None, seq),
        P(head),
    )
    out_specs = P((*head, *seq), None)
    return jax.shard_map(
        on_device, mesh=split_mesh, in_specs=in_specs, out_specs=out_specs, check_vma=False
    )
```

```python
import functools
import math

import jax
import jax.numpy as jnp
from jax import lax
from jax.experimental import pallas as pl
from jax.experimental.pallas import tpu as pltpu
from jax.sharding import PartitionSpec as P

P_SIZE = 64
N = 128
Q = 256
HALF = Q // 2
CORES = 2
NEVER = -1e30
VMEM_LIMIT = 60 * 1024 * 1024

f32 = jnp.float32
bf16 = jnp.bfloat16


def dot(a, b):
    return lax.dot_general(a, b, (((1,), (0,)), ((), ())), preferred_element_type=f32)


def exact_parts(value):
    high = value.astype(bf16)
    rest = value - high.astype(f32)
    middle = rest.astype(bf16)
    low = (rest - middle.astype(f32)).astype(bf16)
    return high, middle, low


def gates_kernel(heads, levels, padded, gates_ref, weight_ref, cum_ref, offset_ref, decay_ref, merge_ref,
                 log_scratch):
    shards, _, span_rows, _ = gates_ref.shape
    spans = shards * span_rows
    upper = (
        lax.broadcasted_iota(jnp.int32, (Q, Q), 0) <= lax.broadcasted_iota(jnp.int32, (Q, Q), 1)
    ).astype(f32).astype(bf16)
    chunk = min(spans, 64)
    for head in range(heads):
        for shard in range(shards):
            rows = pl.ds(shard * span_rows, span_rows)
            gate = gates_ref[shard, 2 * head]
            step = gates_ref[shard, 2 * head + 1]
            high, middle, low = exact_parts(gate)
            cumulative = dot(high, upper) + dot(middle, upper) + dot(low, upper)
            span_log = cumulative[:, Q - 1 :]
            cum_ref[head, rows, :] = cumulative
            offset_ref[head, rows, :] = cumulative - jnp.log(step)
            weight_ref[head, rows, :] = jnp.exp(span_log - cumulative) * step
            log_scratch[rows, :] = jnp.broadcast_to(span_log, (span_rows, N))
        high, middle, low = exact_parts(log_scratch[...])

        def some_spans(at, carry):
            first = at * chunk
            size = (chunk * padded, spans)
            row = lax.broadcasted_iota(jnp.int32, size, 0)
            span = first + row // padded
            level = row % padded
            other = lax.broadcasted_iota(jnp.int32, size, 1)
            out_rows = pl.ds(pl.multiple_of(first * padded, chunk * padded), chunk * padded)
            bit = jnp.maximum(level - 1, 0)
            before = (other >= (span >> bit) << bit) & (other < span)
            before = before.astype(f32).astype(bf16)
            decay = dot(before, high) + dot(before, middle) + dot(before, low)
            has_bit = ((span >> bit) & 1)[:, :1] == 1
            decay_ref[head, out_rows, :] = jnp.where(has_bit, decay, NEVER)
            right = (other > span - (1 << bit)) & (other <= span)
            right = right.astype(f32).astype(bf16)
            merge_ref[head, out_rows, :] = jnp.exp(
                dot(right, high) + dot(right, middle) + dot(right, low)
            )
            return carry

        lax.fori_loop(0, spans // chunk, some_spans, 0)


def pick(core, mine_ref, other_ref, local, group):
    half = group // CORES
    rows = slice(local % half * Q, (local % half + 1) * Q)
    return jnp.where(core == local // half, mine_ref[rows, :], other_ref[rows, :])


def merge_blocks(left, right, merge_ref, row, width):
    parts = []
    for head in range(merge_ref.shape[0]):
        rows = slice(head * width, (head + 1) * width)
        parts.append(left[rows] * merge_ref[head, row : row + 1, :] + right[rows])
    return jnp.concatenate(parts, axis=0) if len(parts) > 1 else parts[0]


def states_kernel(heads, width, group, padded, groups_ref, core_ref, x_ref, mine_ref, other_ref, weight_ref,
                  merge_ref, low_ref, total_ref):
    kept = {}
    for local in range(group):
        columns = slice(local * Q, (local + 1) * Q)
        parts = [
            (
                x_ref[head * width : (head + 1) * width, columns].astype(f32)
                * weight_ref[head, local : local + 1, :]
            ).astype(bf16)
            for head in range(heads)
        ]
        weighted = jnp.concatenate(parts, axis=0) if heads > 1 else parts[0]
        state = dot(weighted, pick(core_ref[0], mine_ref, other_ref, local, group))
        bit = 0
        while local >> bit & 1:
            state = merge_blocks(kept[bit], state, merge_ref, local * padded + bit + 1, width)
            bit += 1
        kept[bit] = state
        if local < group - 1:
            low_ref[local] = state.astype(bf16)
    total_ref[...] = state


def tree_kernel(width, group, padded, groups_ref, merge_ref, *refs):
    *total_refs, high_ref, order_ref = refs
    steps = order_ref.shape[0]
    low_bits = group.bit_length() - 1
    at = 0
    for total_ref in total_refs:
        for slot in range(total_ref.shape[0]):
            order_ref[groups_ref[at]] = total_ref[slot]
            at += 1
    kept = {}
    for step in range(steps):
        state = order_ref[step]
        bit = 0
        while step >> bit & 1:
            row = ((step + 1) * group - 1) * padded + low_bits + bit + 1
            state = merge_blocks(kept[bit], state, merge_ref, row, width)
            bit += 1
        kept[bit] = state
        high_ref[step] = state.astype(bf16)


def outputs_kernel(heads, width, group, bits, padded, groups_ref, core_ref, skip_ref, x_ref, my_key_ref,
                   other_key_ref, my_query_ref, other_query_ref, low_ref, high_ref, cum_ref, offset_ref, decay_ref,
                   level_ref, *refs):
    out_ref, query_ref, score_ref, mixing_ref = refs[-4:]
    step = groups_ref[pl.program_id(0)]
    low_bits = group.bit_length() - 1
    levels = bits + 1
    causal = lax.broadcasted_iota(jnp.int32, (HALF, HALF), 0) <= lax.broadcasted_iota(
        jnp.int32, (HALF, HALF), 1
    )
    head_rows = [slice(head * width, (head + 1) * width) for head in range(heads)]
    high_slots = [
        jnp.maximum((step >> (bit - low_bits) << (bit - low_bits)) - 1, 0) for bit in range(low_bits, bits)
    ]
    offsets = [jnp.transpose(offset_ref[head]) for head in range(heads)]

    @pl.when(pl.program_id(0) == 0)
    def _():
        mixing_ref[:, :, HALF:, :HALF] = jnp.zeros((2, heads, HALF, HALF), bf16)

    def span_columns(local):
        return slice(local * Q, (local + 1) * Q)

    def score(local):
        slot = local % 2
        query_ref[slot] = jnp.transpose(pick(core_ref[0], my_query_ref, other_query_ref, local, group))
        keys = pick(core_ref[0], my_key_ref, other_key_ref, local, group)
        upper = dot(keys[:HALF], query_ref[slot])
        score_ref[slot, :HALF, :HALF] = jnp.where(causal, upper[:, :HALF], 0.0)
        score_ref[slot, :HALF, HALF:] = upper[:, HALF:]
        lower = dot(keys[HALF:], query_ref[slot, :, HALF:])
        score_ref[slot, HALF:, HALF:] = jnp.where(causal, lower, 0.0)

    def mix(local):
        slot = local % 2
        for head in range(heads):
            left = cum_ref[head, local : local + 1, :HALF]
            right = cum_ref[head, local : local + 1, HALF:]
            column = offsets[head][:, local : local + 1]
            upper = jnp.broadcast_to(column[:HALF], (HALF, HALF))
            lower = jnp.broadcast_to(column[HALF:], (HALF, HALF))
            mixing_ref[slot, head, :HALF, :HALF] = (
                score_ref[slot, :HALF, :HALF] * jnp.exp(jnp.minimum(left - upper, 64.0))
            ).astype(bf16)
            mixing_ref[slot, head, :HALF, HALF:] = (
                score_ref[slot, :HALF, HALF:] * jnp.exp(right - upper)
            ).astype(bf16)
            mixing_ref[slot, head, HALF:, HALF:] = (
                score_ref[slot, HALF:, HALF:] * jnp.exp(jnp.minimum(right - lower, 64.0))
            ).astype(bf16)

    def level_parts(local):
        slot = local % 2
        columns = span_columns(local)
        weights = level_ref[0, :, columns].astype(f32)
        factors = []
        for head in range(heads):
            decay = decay_ref[head, local * padded : local * padded + levels, :]
            decay = jnp.concatenate([decay] * (Q // N), axis=1)
            growth = jnp.exp(cum_ref[head, local : local + 1, :] + decay)
            factors.append(weights[head * levels : (head + 1) * levels] * growth)
        sums = [None] * heads
        for bit in range(bits):
            if bit < low_bits:
                if not local >> bit & 1:
                    continue
                state = low_ref[((local >> bit) << bit) - 1]
            else:
                state = high_ref[high_slots[bit - low_bits]]
            part = dot(state, query_ref[slot])
            for head in range(heads):
                term = part[head_rows[head]] * factors[head][bit + 1 : bit + 2]
                sums[head] = term if sums[head] is None else sums[head] + term
        return sums, [weights[head * levels : head * levels + 1] for head in range(heads)]

    def finish(local, parts):
        slot = local % 2
        columns = span_columns(local)
        sums, own = parts
        for head in range(heads):
            values = x_ref[head_rows[head], columns]
            result = dot(values, mixing_ref[slot, head]) * own[head] + skip_ref[head] * values.astype(f32)
            if sums[head] is not None:
                result += sums[head]
            out_ref[head_rows[head], columns] = result.astype(bf16)

    score(0)
    for local in range(group):
        parts = level_parts(local)
        if local + 1 < group:
            score(local + 1)
        mix(local)
        finish(local, parts)


def exchange(value, axis, distance):
    pairs = [(place, place ^ distance) for place in range(lax.axis_size(axis))]
    return lax.ppermute(value, axis, pairs)


def along_z(own):
    pieces = [own]
    for distance in range(1, lax.axis_size("z")):
        low = distance & -distance
        pieces.append(exchange(pieces[distance ^ low], "z", low))
    return jnp.concatenate(pieces, axis=0)


def in_plane(piece):
    half = piece.shape[0] // 2
    far = {}
    for distance in range(1, lax.axis_size("x")):
        far[0, distance] = exchange(piece, "x", distance)
    for distance in range(1, lax.axis_size("y")):
        far[distance, 0] = exchange(piece, "y", distance)
    for y in range(1, lax.axis_size("y")):
        for x in range(1, lax.axis_size("x")):
            first = exchange(far[0, x][:half], "y", y)
            second = exchange(far[y, 0][half:], "x", x)
            far[y, x] = jnp.concatenate([first, second], axis=0)
    return {(0, 0): piece, **far}


def both_cores(plane):
    return {place: (piece, exchange(piece, "core", 1)) for place, piece in plane.items()}


def after(value, *others):
    return lax.optimization_barrier((value, *others))[0]


def on_device(x_heads, b_proj, c_proj, log_gate, step_size, level_weight, skip):
    rows, tokens = x_heads.shape
    head_count, tok_dev = log_gate.shape
    levels = level_weight.shape[1]
    bits = levels - 1
    shards = lax.axis_size(("z", "y"))
    span_rows = tok_dev // Q
    spans = tokens // Q
    heads = max(rows // P_SIZE, 1)
    width = rows // heads
    sharing = P_SIZE // width
    block = b_proj.shape[0]
    group = CORES * block // Q
    padded = -(-levels // 8) * 8
    steps = spans // group
    per_shard = span_rows // group

    def to_owners(value):
        value = jnp.repeat(value, sharing, axis=0) if sharing > 1 else value
        value = value.reshape((shards, heads) + value.shape[1:])
        return value.reshape((shards, -1) + value.shape[3:])

    gates = jnp.stack(
        [log_gate.reshape(head_count, span_rows, Q), step_size.reshape(head_count, span_rows, Q)], axis=1
    )
    gates = lax.all_to_all(to_owners(gates), ("z", "y"), split_axis=0, concat_axis=0, tiled=True)
    key_line = along_z(b_proj)
    level_rows = lax.all_to_all(
        to_owners(after(level_weight, gates).astype(bf16)), ("z", "y"), split_axis=0, concat_axis=0, tiled=True
    )
    key_sets = both_cores(in_plane(key_line))
    query_sets = both_cores(in_plane(along_z(after(c_proj, key_line, gates))))
    first_head = lax.axis_index(("z", "y")) * rows // P_SIZE
    own_skip = lax.dynamic_slice_in_dim(skip, first_head, heads, 0)
    core = lax.axis_index("core").astype(jnp.int32).reshape(1)

    def group_ids(place):
        z = lax.axis_index("z") ^ jnp.arange(lax.axis_size("z"))
        y = lax.axis_index("y") ^ place[0]
        x = lax.axis_index("x") ^ place[1]
        return ((z * lax.axis_size("y") + y) * lax.axis_size("x") + x).astype(jnp.int32)

    params = pltpu.CompilerParams(vmem_limit_bytes=VMEM_LIMIT)
    weight, cumulative, offset, decay, merge = pl.pallas_call(
        functools.partial(gates_kernel, heads, levels, padded),
        out_shape=[jax.ShapeDtypeStruct((heads, spans, Q), f32)] * 3
        + [jax.ShapeDtypeStruct((heads, spans * padded, N), f32)] * 2,
        scratch_shapes=[pltpu.VMEM((spans, N), f32)],
        compiler_params=params,
        name="gates",
    )(gates)
    weight, cumulative, offset = [v.reshape(heads, steps, group, Q) for v in (weight, cumulative, offset)]

    x_spec = pl.BlockSpec((rows, group * Q), lambda i, ids, *_: (0, ids[i]))
    token_spec = pl.BlockSpec((block, N), lambda i, *_: (i, 0))
    span_spec = pl.BlockSpec((heads, None, group, Q), lambda i, ids, *_: (0, ids[i], 0, 0))
    level_spec = pl.BlockSpec((heads, group * padded, N), lambda i, ids, *_: (0, ids[i], 0))
    low_slots = max(group - 1, 1)
    low_spec = pl.BlockSpec((None, low_slots, rows, N), lambda i, *_: (i, 0, 0, 0))

    sets = [
        (group_ids(place), key_sets[place], query_sets[place])
        for place in sorted(key_sets, key=lambda place: ((place[0] > 0) + (place[1] > 0), place))
    ]
    lows, totals = [], []
    for ids, keys, _ in sets:
        count = ids.shape[0]
        low, total = pl.pallas_call(
            functools.partial(states_kernel, heads, width, group, padded),
            grid_spec=pltpu.PrefetchScalarGridSpec(
                num_scalar_prefetch=2,
                grid=(count,),
                in_specs=[x_spec, token_spec, token_spec, span_spec, level_spec],
                out_specs=[low_spec, pl.BlockSpec((None, rows, N), lambda i, *_: (i, 0, 0))],
            ),
            out_shape=[
                jax.ShapeDtypeStruct((count, low_slots, rows, N), bf16),
                jax.ShapeDtypeStruct((count, rows, N), f32),
            ],
            compiler_params=params,
            cost_estimate=pl.CostEstimate(
                flops=2 * rows * count * group * Q * N,
                bytes_accessed=4 * count * group * Q * (rows + N),
                transcendentals=0,
            ),
            name="states",
        )(ids, core, x_heads, *keys, weight, merge)
        lows.append(low)
        totals.append(total)

    vmem = pl.BlockSpec(memory_space=pltpu.VMEM)
    high = pl.pallas_call(
        functools.partial(tree_kernel, width, group, padded),
        grid_spec=pltpu.PrefetchScalarGridSpec(
            num_scalar_prefetch=1,
            in_specs=[vmem] * (1 + len(totals)),
            out_specs=vmem,
            scratch_shapes=[pltpu.VMEM((steps, rows, N), f32)],
        ),
        out_shape=jax.ShapeDtypeStruct((steps, rows, N), bf16),
        compiler_params=params,
        name="tree",
    )(jnp.concatenate([ids for ids, _, _ in sets]), merge, *totals)

    out = None
    for (ids, keys, queries), low in zip(sets, lows):
        count = ids.shape[0]
        tokens_here = count * group * Q
        before = [] if out is None else [out]
        out = pl.pallas_call(
            functools.partial(outputs_kernel, heads, width, group, bits, padded),
            grid_spec=pltpu.PrefetchScalarGridSpec(
                num_scalar_prefetch=2,
                grid=(count,),
                in_specs=[
                    pl.BlockSpec(memory_space=pltpu.SMEM),
                    x_spec,
                    token_spec,
                    token_spec,
                    token_spec,
                    token_spec,
                    low_spec,
                    vmem,
                    span_spec,
                    span_spec,
                    level_spec,
                    pl.BlockSpec(
                        (1, heads * levels, group * Q),
                        lambda i, ids, *_: (ids[i] // per_shard, 0, ids[i] % per_shard),
                    ),
                ]
                + [pl.BlockSpec(memory_space=pl.ANY)] * len(before),
                out_specs=x_spec,
                scratch_shapes=[
                    pltpu.VMEM((2, N, Q), bf16),
                    pltpu.VMEM((2, Q, Q), f32),
                    pltpu.VMEM((2, heads, Q, Q), bf16),
                ],
            ),
            out_shape=jax.ShapeDtypeStruct((rows, tokens), bf16),
            input_output_aliases={14: 0} if before else {},
            compiler_params=params,
            cost_estimate=pl.CostEstimate(
                flops=2 * tokens_here * (Q * N + rows * Q + bits * rows * N),
                bytes_accessed=4 * tokens_here * (rows + N),
                transcendentals=heads * tokens_here * Q,
            ),
            name="outputs",
        )(ids, core, own_skip, x_heads, *keys, *queries, low, high, cumulative, offset, decay, level_rows, *before)
    return out


def solution(mesh):
    x = mesh.shape["head"] // CORES
    y = math.gcd(mesh.shape["seq"], x)
    z = mesh.shape["seq"] // y
    split_mesh = jax.sharding.Mesh(mesh.devices.reshape(z, y, x, CORES), ("z", "y", "x", "core"))
    seq = ("z", "y")
    head = ("x", "core")
    in_specs = (
        P((*head, *seq), None),
        P((*seq, *head), None),
        P((*seq, *head), None),
        P(head, seq),
        P(head, seq),
        P(head, None, seq),
        P(head),
    )
    out_specs = P((*head, *seq), None)
    return jax.shard_map(
        on_device, mesh=split_mesh, in_specs=in_specs, out_specs=out_specs, check_vma=False
    )
```

```python
import functools
import math

import jax
import jax.numpy as jnp
from jax import lax
from jax.experimental import pallas as pl
from jax.experimental.pallas import tpu as pltpu
from jax.sharding import PartitionSpec as P

P_SIZE = 64
N = 128
Q = 256
HALF = Q // 2
CORES = 2
NEVER = -1e30
VMEM_LIMIT = 60 * 1024 * 1024

f32 = jnp.float32
bf16 = jnp.bfloat16


def dot(a, b):
    return lax.dot_general(a, b, (((1,), (0,)), ((), ())), preferred_element_type=f32)


def exact_parts(value):
    high = value.astype(bf16)
    rest = value - high.astype(f32)
    middle = rest.astype(bf16)
    low = (rest - middle.astype(f32)).astype(bf16)
    return high, middle, low


def gates_kernel(heads, levels, padded, gates_ref, weight_ref, cum_ref, offset_ref, half_ref, decay_ref,
                 merge_ref, log_scratch):
    shards, _, span_rows, _ = gates_ref.shape
    spans = shards * span_rows
    upper = (
        lax.broadcasted_iota(jnp.int32, (Q, Q), 0) <= lax.broadcasted_iota(jnp.int32, (Q, Q), 1)
    ).astype(f32).astype(bf16)
    chunk = min(spans, 64)
    for head in range(heads):
        for shard in range(shards):
            rows = pl.ds(shard * span_rows, span_rows)
            gate = gates_ref[shard, 2 * head]
            step = gates_ref[shard, 2 * head + 1]
            high, middle, low = exact_parts(gate)
            cumulative = dot(high, upper) + dot(middle, upper) + dot(low, upper)
            span_log = cumulative[:, Q - 1 :]
            cum_ref[head, rows, :] = cumulative
            offset_ref[head, rows, :] = cumulative - jnp.log(step)
            half_log = cumulative[:, HALF - 1 : HALF]
            weight_ref[head, rows, :HALF] = jnp.exp(half_log - cumulative[:, :HALF]) * step[:, :HALF]
            weight_ref[head, rows, HALF:] = jnp.exp(span_log - cumulative[:, HALF:]) * step[:, HALF:]
            half_ref[head, rows, :] = jnp.broadcast_to(jnp.exp(span_log - half_log), (span_rows, N))
            log_scratch[rows, :] = jnp.broadcast_to(span_log, (span_rows, N))
        high, middle, low = exact_parts(log_scratch[...])

        def some_spans(at, carry):
            first = at * chunk
            size = (chunk * padded, spans)
            row = lax.broadcasted_iota(jnp.int32, size, 0)
            span = first + row // padded
            level = row % padded
            other = lax.broadcasted_iota(jnp.int32, size, 1)
            out_rows = pl.ds(pl.multiple_of(first * padded, chunk * padded), chunk * padded)
            bit = jnp.maximum(level - 1, 0)
            before = (other >= (span >> bit) << bit) & (other < span)
            before = before.astype(f32).astype(bf16)
            decay = dot(before, high) + dot(before, middle) + dot(before, low)
            has_bit = ((span >> bit) & 1)[:, :1] == 1
            decay_ref[head, out_rows, :] = jnp.where(has_bit, decay, NEVER)
            right = (other > span - (1 << bit)) & (other <= span)
            right = right.astype(f32).astype(bf16)
            merge_ref[head, out_rows, :] = jnp.exp(
                dot(right, high) + dot(right, middle) + dot(right, low)
            )
            return carry

        lax.fori_loop(0, spans // chunk, some_spans, 0)


def pick(core, mine_ref, other_ref, local, group):
    half = group // CORES
    rows = slice(local % half * Q, (local % half + 1) * Q)
    return jnp.where(core == local // half, mine_ref[rows, :], other_ref[rows, :])


def scaled(value, rows, width):
    parts = [value[head * width : (head + 1) * width] * row for head, row in enumerate(rows)]
    return jnp.concatenate(parts, axis=0) if len(parts) > 1 else parts[0]


def merge_blocks(left, right, merge_ref, row, width):
    return scaled(left, [merge_ref[head, row : row + 1, :] for head in range(merge_ref.shape[0])], width) + right


def states_kernel(heads, width, group, padded, groups_ref, core_ref, x_ref, mine_ref, other_ref, weight_ref,
                  half_ref, merge_ref, low_ref, total_ref):
    kept = {}
    for local in range(group):
        columns = slice(local * Q, (local + 1) * Q)
        weights = [weight_ref[head, local : local + 1, :] for head in range(heads)]
        weighted = scaled(x_ref[:, columns].astype(f32), weights, width).astype(bf16)
        keys = pick(core_ref[0], mine_ref, other_ref, local, group)
        first = dot(weighted[:, :HALF], keys[:HALF])
        low_ref[group + local] = first.astype(bf16)
        halves = [half_ref[head, local : local + 1, :] for head in range(heads)]
        state = scaled(first, halves, width) + dot(weighted[:, HALF:], keys[HALF:])
        bit = 0
        while local >> bit & 1:
            state = merge_blocks(kept[bit], state, merge_ref, local * padded + bit + 1, width)
            bit += 1
        kept[bit] = state
        low_ref[local] = state.astype(bf16)
    total_ref[...] = state


def tree_kernel(width, group, padded, groups_ref, merge_ref, *refs):
    *total_refs, high_ref, order_ref = refs
    steps = order_ref.shape[0]
    low_bits = group.bit_length() - 1
    at = 0
    for total_ref in total_refs:
        for slot in range(total_ref.shape[0]):
            order_ref[groups_ref[at]] = total_ref[slot]
            at += 1
    kept = {}
    for step in range(steps):
        state = order_ref[step]
        bit = 0
        while step >> bit & 1:
            row = ((step + 1) * group - 1) * padded + low_bits + bit + 1
            state = merge_blocks(kept[bit], state, merge_ref, row, width)
            bit += 1
        kept[bit] = state
        high_ref[step] = state.astype(bf16)


def outputs_kernel(heads, width, group, bits, padded, groups_ref, core_ref, skip_ref, x_ref, my_key_ref,
                   other_key_ref, my_query_ref, other_query_ref, low_ref, high_ref, cum_ref, offset_ref, decay_ref,
                   level_ref, *refs):
    out_ref, query_ref, score_ref, side_ref = refs[-4:]
    step = groups_ref[pl.program_id(0)]
    low_bits = group.bit_length() - 1
    levels = bits + 1
    causal = lax.broadcasted_iota(jnp.int32, (HALF, HALF), 0) <= lax.broadcasted_iota(
        jnp.int32, (HALF, HALF), 1
    )
    head_rows = [slice(head * width, (head + 1) * width) for head in range(heads)]
    high_slots = [
        jnp.maximum((step >> (bit - low_bits) << (bit - low_bits)) - 1, 0) for bit in range(low_bits, bits)
    ]
    offsets = [jnp.transpose(offset_ref[head]) for head in range(heads)]

    @pl.when(pl.program_id(0) == 0)
    def _():
        side_ref[:, :, :HALF, HALF:] = jnp.zeros((2, heads, HALF, HALF), bf16)
        side_ref[:, :, HALF:Q, :HALF] = jnp.zeros((2, heads, HALF, HALF), bf16)
        side_ref[:, :, Q : Q + N, :HALF] = jnp.zeros((2, heads, N, HALF), bf16)

    def active(local):
        return [bit for bit in range(bits) if bit >= low_bits or local >> bit & 1]

    def score(local):
        slot = local % 2
        query_ref[slot] = jnp.transpose(pick(core_ref[0], my_query_ref, other_query_ref, local, group))
        keys = pick(core_ref[0], my_key_ref, other_key_ref, local, group)
        for half in (slice(0, HALF), slice(HALF, Q)):
            score_ref[slot, half] = jnp.where(causal, dot(keys[half], query_ref[slot, :, half]), 0.0)

    def prepare(local):
        slot = local % 2
        columns = slice(local * Q, (local + 1) * Q)
        weights = level_ref[0, :, columns].astype(f32)
        for head in range(heads):
            cumulative = cum_ref[head, local : local + 1, :]
            weight = weights[head * levels : (head + 1) * levels]
            own = cumulative + jnp.log(weight[:1])
            column = offsets[head][:, local : local + 1]
            for half in (slice(0, HALF), slice(HALF, Q)):
                gaps = jnp.minimum(own[:, half] - column[half], 64.0)
                side_ref[slot, head, half, half] = (score_ref[slot, half] * jnp.exp(gaps)).astype(bf16)
            across = jnp.exp(own[:, HALF:] - cumulative[:, HALF - 1 : HALF]).astype(bf16)
            side_ref[slot, head, Q : Q + N, HALF:] = query_ref[slot, :, HALF:] * across
            decay = decay_ref[head, local * padded : local * padded + levels, :]
            decay = jnp.concatenate([decay] * (Q // N), axis=1)
            factors = weight * jnp.exp(cumulative + decay)
            for place, bit in enumerate(active(local)):
                rows = slice(Q + (place + 1) * N, Q + (place + 2) * N)
                side_ref[slot, head, rows, :] = query_ref[slot] * factors[bit + 1 : bit + 2].astype(bf16)

    def finish(local):
        slot = local % 2
        columns = slice(local * Q, (local + 1) * Q)
        states = [low_ref[group + local]]
        for bit in active(local):
            if bit < low_bits:
                states.append(low_ref[((local >> bit) << bit) - 1])
            else:
                states.append(high_ref[high_slots[bit - low_bits]])
        for head in range(heads):
            values = x_ref[head_rows[head], columns]
            left = jnp.concatenate([values] + [state[head_rows[head]] for state in states], axis=1)
            result = dot(left, side_ref[slot, head, : Q + len(states) * N, :])
            out_ref[head_rows[head], columns] = (result + skip_ref[head] * values.astype(f32)).astype(bf16)

    score(0)
    for local in range(group):
        if local + 1 < group:
            score(local + 1)
        prepare(local)
        if local:
            finish(local - 1)
    finish(group - 1)


def exchange(value, axis, distance):
    pairs = [(place, place ^ distance) for place in range(lax.axis_size(axis))]
    return lax.ppermute(value, axis, pairs)


def along_z(own):
    pieces = [own]
    for distance in range(1, lax.axis_size("z")):
        low = distance & -distance
        pieces.append(exchange(pieces[distance ^ low], "z", low))
    return pieces[1:]


def places():
    both = [(y, x) for y in range(lax.axis_size("y")) for x in range(lax.axis_size("x"))]
    return sorted(both, key=lambda place: ((place[0] > 0) + (place[1] > 0), place))


def straight(piece):
    near = {(0, 0): piece}
    for y, x in places():
        if (y > 0) != (x > 0):
            near[y, x] = exchange(piece, "x", x) if x else exchange(piece, "y", y)
    return near


def diagonal(near, by_x, by_y):
    far = {}
    for y, x in places():
        if y and x:
            parts = []
            if by_x is not None:
                parts.append(exchange(near[0, x][by_x], "y", y))
            if by_y is not None:
                parts.append(exchange(near[y, 0][by_y], "x", x))
            far[y, x] = parts
    return far


def join(parts):
    return jnp.concatenate(parts, axis=0) if len(parts) > 1 else parts[0]


def with_core(piece):
    return piece, exchange(piece, "core", 1)


def after(value, *others):
    return lax.optimization_barrier((value, *others))[0]


def on_device(x_heads, b_proj, c_proj, log_gate, step_size, level_weight, skip):
    rows, tokens = x_heads.shape
    head_count, tok_dev = log_gate.shape
    levels = level_weight.shape[1]
    bits = levels - 1
    shards = lax.axis_size(("z", "y"))
    span_rows = tok_dev // Q
    spans = tokens // Q
    heads = max(rows // P_SIZE, 1)
    width = rows // heads
    sharing = P_SIZE // width
    block = b_proj.shape[0]
    group = CORES * block // Q
    padded = -(-levels // 8) * 8
    steps = spans // group
    per_shard = span_rows // group

    def to_owners(value):
        value = jnp.repeat(value, sharing, axis=0) if sharing > 1 else value
        value = value.reshape((shards, heads) + value.shape[1:])
        return value.reshape((shards, -1) + value.shape[3:])

    gates = jnp.stack(
        [log_gate.reshape(head_count, span_rows, Q), step_size.reshape(head_count, span_rows, Q)], axis=1
    )
    gates = lax.all_to_all(to_owners(gates), ("z", "y"), split_axis=0, concat_axis=0, tiled=True)
    everything = slice(None)
    key_near = straight(b_proj)
    key_line = along_z(b_proj)
    query_near = straight(c_proj)
    query_line = along_z(c_proj)
    key_near.update({place: join(parts) for place, parts in diagonal(key_near, everything, None).items()})
    query_near.update({place: join(parts) for place, parts in diagonal(query_near, None, everything).items()})
    level_rows = lax.all_to_all(
        to_owners(after(level_weight, gates).astype(bf16)), ("z", "y"), split_axis=0, concat_axis=0, tiled=True
    )
    keys_here = with_core(jnp.concatenate([key_near[place] for place in places()], axis=0))
    queries_here = with_core(jnp.concatenate([query_near[place] for place in places()], axis=0))
    first_head = lax.axis_index(("z", "y")) * rows // P_SIZE
    own_skip = lax.dynamic_slice_in_dim(skip, first_head, heads, 0)
    core = lax.axis_index("core").astype(jnp.int32).reshape(1)

    def group_ids(place, z=None):
        z = lax.axis_index("z") ^ jnp.arange(1, lax.axis_size("z")) if z is None else z
        y = lax.axis_index("y") ^ place[0]
        x = lax.axis_index("x") ^ place[1]
        return ((z * lax.axis_size("y") + y) * lax.axis_size("x") + x).astype(jnp.int32)

    params = pltpu.CompilerParams(vmem_limit_bytes=VMEM_LIMIT)
    weight, cumulative, offset, half, decay, merge = pl.pallas_call(
        functools.partial(gates_kernel, heads, levels, padded),
        out_shape=[jax.ShapeDtypeStruct((heads, spans, Q), f32)] * 3
        + [jax.ShapeDtypeStruct((heads, spans, N), f32)]
        + [jax.ShapeDtypeStruct((heads, spans * padded, N), f32)] * 2,
        scratch_shapes=[pltpu.VMEM((spans, N), f32)],
        compiler_params=params,
        name="gates",
    )(gates)
    weight, cumulative, offset = [v.reshape(heads, steps, group, Q) for v in (weight, cumulative, offset)]
    half = half.reshape(heads, steps, group, N)

    x_spec = pl.BlockSpec((rows, group * Q), lambda i, ids, *_: (0, ids[i]))
    token_spec = pl.BlockSpec((block, N), lambda i, *_: (i, 0))
    span_spec = pl.BlockSpec((heads, None, group, Q), lambda i, ids, *_: (0, ids[i], 0, 0))
    level_spec = pl.BlockSpec((heads, group * padded, N), lambda i, ids, *_: (0, ids[i], 0))
    half_spec = pl.BlockSpec((heads, None, group, N), lambda i, ids, *_: (0, ids[i], 0, 0))
    low_slots = 2 * group
    low_spec = pl.BlockSpec((None, low_slots, rows, N), lambda i, *_: (i, 0, 0, 0))

    lows, totals, all_ids = [], [], []

    def states(ids, keys):
        count = ids.shape[0]
        low, total = pl.pallas_call(
            functools.partial(states_kernel, heads, width, group, padded),
            grid_spec=pltpu.PrefetchScalarGridSpec(
                num_scalar_prefetch=2,
                grid=(count,),
                in_specs=[x_spec, token_spec, token_spec, span_spec, half_spec, level_spec],
                out_specs=[low_spec, pl.BlockSpec((None, rows, N), lambda i, *_: (i, 0, 0))],
            ),
            out_shape=[
                jax.ShapeDtypeStruct((count, low_slots, rows, N), bf16),
                jax.ShapeDtypeStruct((count, rows, N), f32),
            ],
            compiler_params=params,
            cost_estimate=pl.CostEstimate(
                flops=2 * rows * count * group * Q * N,
                bytes_accessed=4 * count * group * Q * (rows + N),
                transcendentals=0,
            ),
            name="states",
        )(ids, core, x_heads, *keys, weight, half, merge)
        lows.append(low)
        totals.append(total)
        all_ids.append(ids)
        return total

    here = jnp.concatenate([group_ids(place, lax.axis_index("z").reshape(1)) for place in places()])
    total = states(here, keys_here)
    if key_line:
        halves = slice(0, block * len(key_line) // 2), slice(block * len(key_line) // 2, None)
        key_far = straight(jnp.concatenate(key_line, axis=0))
        query_far = straight(after(jnp.concatenate(query_line, axis=0), weight))
        key_far.update({place: join(parts) for place, parts in diagonal(key_far, *halves).items()})
        keys_far = {place: with_core(key_far[place]) for place in places()}
        for place in places():
            states(group_ids(place), keys_far[place])

    vmem = pl.BlockSpec(memory_space=pltpu.VMEM)
    high = pl.pallas_call(
        functools.partial(tree_kernel, width, group, padded),
        grid_spec=pltpu.PrefetchScalarGridSpec(
            num_scalar_prefetch=1,
            in_specs=[vmem] * (1 + len(totals)),
            out_specs=vmem,
            scratch_shapes=[pltpu.VMEM((steps, rows, N), f32)],
        ),
        out_shape=jax.ShapeDtypeStruct((steps, rows, N), bf16),
        compiler_params=params,
        name="tree",
    )(jnp.concatenate(all_ids), merge, *totals)

    def outputs(ids, keys, queries, low, out):
        count = ids.shape[0]
        tokens_here = count * group * Q
        before = [] if out is None else [out]
        return pl.pallas_call(
            functools.partial(outputs_kernel, heads, width, group, bits, padded),
            grid_spec=pltpu.PrefetchScalarGridSpec(
                num_scalar_prefetch=2,
                grid=(count,),
                in_specs=[
                    pl.BlockSpec(memory_space=pltpu.SMEM),
                    x_spec,
                    token_spec,
                    token_spec,
                    token_spec,
                    token_spec,
                    low_spec,
                    vmem,
                    span_spec,
                    span_spec,
                    level_spec,
                    pl.BlockSpec(
                        (1, heads * levels, group * Q),
                        lambda i, ids, *_: (ids[i] // per_shard, 0, ids[i] % per_shard),
                    ),
                ]
                + [pl.BlockSpec(memory_space=pl.ANY)] * len(before),
                out_specs=x_spec,
                scratch_shapes=[
                    pltpu.VMEM((2, N, Q), bf16),
                    pltpu.VMEM((2, Q, HALF), f32),
                    pltpu.VMEM((2, heads, Q + levels * N, Q), bf16),
                ],
            ),
            out_shape=jax.ShapeDtypeStruct((rows, tokens), bf16),
            input_output_aliases={14: 0} if before else {},
            compiler_params=params,
            cost_estimate=pl.CostEstimate(
                flops=2 * tokens_here * (Q * N + rows * Q + bits * rows * N),
                bytes_accessed=4 * tokens_here * (rows + N),
                transcendentals=heads * tokens_here * Q,
            ),
            name="outputs",
        )(ids, core, own_skip, x_heads, *keys, *queries, low, high, cumulative, offset, decay, level_rows, *before)
    out = outputs(here, keys_here, queries_here, lows[0], None)
    if key_line:
        query_far = {place: after(piece, out) if any(place) else piece for place, piece in query_far.items()}
        corners = diagonal(query_far, *halves)
        queries_far = {place: with_core(piece) for place, piece in query_far.items()}
        for at, place in enumerate(places()):
            if at + 2 == len(query_far):
                for corner, parts in corners.items():
                    queries_far[corner] = with_core(join([after(part, out) for part in parts]))
                out = after(out, *[queries_far[corner][0] for corner in corners])
            out = outputs(group_ids(place), keys_far[place], queries_far[place], lows[1 + at], out)
    return out


def solution(mesh):
    x = mesh.shape["head"] // CORES
    y = math.gcd(mesh.shape["seq"], x)
    z = mesh.shape["seq"] // y
    split_mesh = jax.sharding.Mesh(mesh.devices.reshape(z, y, x, CORES), ("z", "y", "x", "core"))
    seq = ("z", "y")
    head = ("x", "core")
    in_specs = (
        P((*head, *seq), None),
        P((*seq, *head), None),
        P((*seq, *head), None),
        P(head, seq),
        P(head, seq),
        P(head, None, seq),
        P(head),
    )
    out_specs = P((*head, *seq), None)
    return jax.shard_map(
        on_device, mesh=split_mesh, in_specs=in_specs, out_specs=out_specs, check_vma=False
    )
```

```python
import functools
import math

import jax
import jax.numpy as jnp
from jax import lax
from jax.experimental import pallas as pl
from jax.experimental.pallas import tpu as pltpu
from jax.sharding import PartitionSpec as P

P_SIZE = 64
N = 128
Q = 256
HALF = Q // 2
CORES = 2
NEVER = -1e30
VMEM_LIMIT = 60 * 1024 * 1024

f32 = jnp.float32
bf16 = jnp.bfloat16


def dot(a, b):
    return lax.dot_general(a, b, (((1,), (0,)), ((), ())), preferred_element_type=f32)


def exact_parts(value):
    high = value.astype(bf16)
    rest = value - high.astype(f32)
    middle = rest.astype(bf16)
    low = (rest - middle.astype(f32)).astype(bf16)
    return high, middle, low


def gates_kernel(heads, levels, padded, gates_ref, weight_ref, cum_ref, offset_ref, decay_ref, merge_ref,
                 log_scratch):
    shards, _, span_rows, _ = gates_ref.shape
    spans = shards * span_rows
    upper = (
        lax.broadcasted_iota(jnp.int32, (Q, Q), 0) <= lax.broadcasted_iota(jnp.int32, (Q, Q), 1)
    ).astype(f32).astype(bf16)
    chunk = min(spans, 64)
    for head in range(heads):
        for shard in range(shards):
            rows = pl.ds(shard * span_rows, span_rows)
            gate = gates_ref[shard, 2 * head]
            step = gates_ref[shard, 2 * head + 1]
            high, middle, low = exact_parts(gate)
            cumulative = dot(high, upper) + dot(middle, upper) + dot(low, upper)
            span_log = cumulative[:, Q - 1 :]
            cum_ref[head, rows, :] = cumulative
            offset_ref[head, rows, :] = cumulative - jnp.log(step)
            weight_ref[head, rows, :] = jnp.exp(span_log - cumulative) * step
            log_scratch[rows, :] = jnp.broadcast_to(span_log, (span_rows, N))
        high, middle, low = exact_parts(log_scratch[...])

        def some_spans(at, carry):
            first = at * chunk
            size = (chunk * padded, spans)
            row = lax.broadcasted_iota(jnp.int32, size, 0)
            span = first + row // padded
            level = row % padded
            other = lax.broadcasted_iota(jnp.int32, size, 1)
            out_rows = pl.ds(pl.multiple_of(first * padded, chunk * padded), chunk * padded)
            bit = jnp.maximum(level - 1, 0)
            before = (other >= (span >> bit) << bit) & (other < span)
            before = before.astype(f32).astype(bf16)
            decay = dot(before, high) + dot(before, middle) + dot(before, low)
            has_bit = ((span >> bit) & 1)[:, :1] == 1
            decay_ref[head, out_rows, :] = jnp.where(has_bit, decay, NEVER)
            right = (other > span - (1 << bit)) & (other <= span)
            right = right.astype(f32).astype(bf16)
            merge_ref[head, out_rows, :] = jnp.exp(
                dot(right, high) + dot(right, middle) + dot(right, low)
            )
            return carry

        lax.fori_loop(0, spans // chunk, some_spans, 0)


def pick_set(step, starts, values):
    value = values[0]
    for start, other in zip(starts[1:], values[1:]):
        value = jnp.where(step >= start, other, value)
    return value


def pick(core, step, starts, pairs, local, group):
    half = group // CORES
    rows = slice(local % half * Q, (local % half + 1) * Q)
    mine = core == local // half
    return pick_set(step, starts, [jnp.where(mine, my_ref[rows, :], other_ref[rows, :]) for my_ref, other_ref in pairs])


def scaled(value, rows, width):
    parts = [value[head * width : (head + 1) * width] * row for head, row in enumerate(rows)]
    return jnp.concatenate(parts, axis=0) if len(parts) > 1 else parts[0]


def merge_blocks(left, right, merge_ref, row, width):
    return scaled(left, [merge_ref[head, row : row + 1, :] for head in range(merge_ref.shape[0])], width) + right


def states_kernel(heads, width, group, padded, starts, groups_ref, core_ref, x_ref, weight_ref, merge_ref, *refs):
    *key_refs, low_ref, total_ref = refs
    pairs = list(zip(key_refs[::2], key_refs[1::2]))
    kept = {}
    for local in range(group):
        columns = slice(local * Q, (local + 1) * Q)
        weights = [weight_ref[head, local : local + 1, :] for head in range(heads)]
        weighted = scaled(x_ref[:, columns].astype(f32), weights, width).astype(bf16)
        state = dot(weighted, pick(core_ref[0], pl.program_id(0), starts, pairs, local, group))
        bit = 0
        while local >> bit & 1:
            state = merge_blocks(kept[bit], state, merge_ref, local * padded + bit + 1, width)
            bit += 1
        kept[bit] = state
        if local < group - 1:
            low_ref[local] = state.astype(bf16)
    total_ref[...] = state


def tree_kernel(width, group, padded, groups_ref, merge_ref, *refs):
    *total_refs, high_ref, order_ref = refs
    steps = order_ref.shape[0]
    low_bits = group.bit_length() - 1
    at = 0
    for total_ref in total_refs:
        for slot in range(total_ref.shape[0]):
            order_ref[groups_ref[at]] = total_ref[slot]
            at += 1
    kept = {}
    for step in range(steps):
        state = order_ref[step]
        bit = 0
        while step >> bit & 1:
            row = ((step + 1) * group - 1) * padded + low_bits + bit + 1
            state = merge_blocks(kept[bit], state, merge_ref, row, width)
            bit += 1
        kept[bit] = state
        high_ref[step] = state.astype(bf16)


def outputs_kernel(heads, width, group, bits, padded, starts, groups_ref, core_ref, skip_ref, x_ref, high_ref,
                   cum_ref, offset_ref, decay_ref, level_ref, *refs):
    *set_refs, out_ref, query_ref, total_ref, factor_ref, score_ref, mixing_ref = refs
    set_refs = [set_refs[5 * at : 5 * at + 5] for at in range(len(starts))]
    key_pairs = [refs[0:2] for refs in set_refs]
    query_pairs = [refs[2:4] for refs in set_refs]
    low_refs = [refs[4] for refs in set_refs]
    at = pl.program_id(0)
    step = groups_ref[at]
    low_bits = group.bit_length() - 1
    levels = bits + 1
    causal = lax.broadcasted_iota(jnp.int32, (HALF, HALF), 0) <= lax.broadcasted_iota(
        jnp.int32, (HALF, HALF), 1
    )
    head_rows = [slice(head * width, (head + 1) * width) for head in range(heads)]
    offsets = [jnp.transpose(offset_ref[head]) for head in range(heads)]

    @pl.when(at == 0)
    def _():
        mixing_ref[:, :, HALF:, :HALF] = jnp.zeros((2, heads, HALF, HALF), bf16)

    def span_columns(local):
        return slice(local * Q, (local + 1) * Q)

    for local in range(group):
        columns = span_columns(local)
        query_ref[:, columns] = jnp.transpose(pick(core_ref[0], at, starts, query_pairs, local, group))
        weights = level_ref[0, :, columns].astype(f32)
        for head in range(heads):
            decay = decay_ref[head, local * padded : local * padded + levels, :]
            decay = jnp.concatenate([decay] * (Q // N), axis=1)
            growth = jnp.exp(cum_ref[head, local : local + 1, :] + decay)
            factor_ref[head, :levels, columns] = weights[head * levels : (head + 1) * levels] * growth
    total_ref[...] = jnp.zeros_like(total_ref)

    def weigh(part, bit, columns):
        return [part[rows] * factor_ref[head, bit + 1 : bit + 2, columns] for head, rows in enumerate(head_rows)]

    for bit in range(low_bits, bits):
        place = bit - low_bits

        @pl.when(((step >> place) & 1) == 1)
        def _(bit=bit, place=place):
            state = high_ref[(step >> place << place) - 1]
            for local in range(group):
                columns = span_columns(local)
                terms = weigh(dot(state, query_ref[:, columns]), bit, columns)
                for rows, term in zip(head_rows, terms):
                    total_ref[rows, columns] += term

    def score(local):
        slot = local % 2
        columns = span_columns(local)
        keys = pick(core_ref[0], at, starts, key_pairs, local, group)
        upper = dot(keys[:HALF], query_ref[:, columns])
        score_ref[slot, :HALF, :HALF] = jnp.where(causal, upper[:, :HALF], 0.0)
        score_ref[slot, :HALF, HALF:] = upper[:, HALF:]
        lower = dot(keys[HALF:], query_ref[:, columns][:, HALF:])
        score_ref[slot, HALF:, HALF:] = jnp.where(causal, lower, 0.0)

    def mix(local):
        slot = local % 2
        for head in range(heads):
            left = cum_ref[head, local : local + 1, :HALF]
            right = cum_ref[head, local : local + 1, HALF:]
            column = offsets[head][:, local : local + 1]
            upper = jnp.broadcast_to(column[:HALF], (HALF, HALF))
            lower = jnp.broadcast_to(column[HALF:], (HALF, HALF))
            mixing_ref[slot, head, :HALF, :HALF] = (
                score_ref[slot, :HALF, :HALF] * jnp.exp(jnp.minimum(left - upper, 64.0))
            ).astype(bf16)
            mixing_ref[slot, head, :HALF, HALF:] = (
                score_ref[slot, :HALF, HALF:] * jnp.exp(right - upper)
            ).astype(bf16)
            mixing_ref[slot, head, HALF:, HALF:] = (
                score_ref[slot, HALF:, HALF:] * jnp.exp(jnp.minimum(right - lower, 64.0))
            ).astype(bf16)

    def level_parts(local):
        columns = span_columns(local)
        sums = [total_ref[rows, columns] for rows in head_rows]
        for bit in range(low_bits):
            if local >> bit & 1:
                slot = ((local >> bit) << bit) - 1
                state = pick_set(at, starts, [low_ref[slot] for low_ref in low_refs])
                terms = weigh(dot(state, query_ref[:, columns]), bit, columns)
                sums = [left + right for left, right in zip(sums, terms)]
        return sums

    def finish(local, sums):
        slot = local % 2
        columns = span_columns(local)
        own = level_ref[0, :, columns].astype(f32)
        for head, rows in enumerate(head_rows):
            values = x_ref[rows, columns]
            result = dot(values, mixing_ref[slot, head]) * own[head * levels : head * levels + 1]
            result += skip_ref[head] * values.astype(f32) + sums[head]
            out_ref[rows, columns] = result.astype(bf16)

    score(0)
    for local in range(group):
        sums = level_parts(local)
        if local + 1 < group:
            score(local + 1)
        mix(local)
        finish(local, sums)


def exchange(value, axis, distance):
    pairs = [(place, place ^ distance) for place in range(lax.axis_size(axis))]
    return lax.ppermute(value, axis, pairs)


def along_z(own):
    pieces = [own]
    for distance in range(1, lax.axis_size("z")):
        low = distance & -distance
        pieces.append(exchange(pieces[distance ^ low], "z", low))
    return pieces[1:]


def places():
    both = [(y, x) for y in range(lax.axis_size("y")) for x in range(lax.axis_size("x"))]
    return sorted(both, key=lambda place: ((place[0] > 0) + (place[1] > 0), place))


def straight(piece):
    near = {(0, 0): piece}
    for y, x in places():
        if (y > 0) != (x > 0):
            near[y, x] = exchange(piece, "x", x) if x else exchange(piece, "y", y)
    return near


def diagonal(near, by_x, by_y):
    far = {}
    for y, x in places():
        if y and x:
            parts = []
            if by_x is not None:
                parts.append(exchange(near[0, x][by_x], "y", y))
            if by_y is not None:
                parts.append(exchange(near[y, 0][by_y], "x", x))
            far[y, x] = parts
    return far


def join(parts):
    return jnp.concatenate(parts, axis=0) if len(parts) > 1 else parts[0]


def with_core(piece):
    return piece, exchange(piece, "core", 1)


def after(value, *others):
    return lax.optimization_barrier((value, *others))[0]


def on_device(x_heads, b_proj, c_proj, log_gate, step_size, level_weight, skip):
    rows, tokens = x_heads.shape
    head_count, tok_dev = log_gate.shape
    levels = level_weight.shape[1]
    bits = levels - 1
    shards = lax.axis_size(("z", "y"))
    span_rows = tok_dev // Q
    spans = tokens // Q
    heads = max(rows // P_SIZE, 1)
    width = rows // heads
    sharing = P_SIZE // width
    block = b_proj.shape[0]
    group = CORES * block // Q
    padded = -(-levels // 8) * 8
    steps = spans // group
    per_shard = span_rows // group

    def to_owners(value):
        value = jnp.repeat(value, sharing, axis=0) if sharing > 1 else value
        value = value.reshape((shards, heads) + value.shape[1:])
        return value.reshape((shards, -1) + value.shape[3:])

    gates = jnp.stack(
        [log_gate.reshape(head_count, span_rows, Q), step_size.reshape(head_count, span_rows, Q)], axis=1
    )
    gates = lax.all_to_all(to_owners(gates), ("z", "y"), split_axis=0, concat_axis=0, tiled=True)
    first_head = lax.axis_index(("z", "y")) * rows // P_SIZE
    own_skip = lax.dynamic_slice_in_dim(skip, first_head, heads, 0)
    core = lax.axis_index("core").astype(jnp.int32).reshape(1)

    def group_ids(place, z=None):
        z = lax.axis_index("z") ^ jnp.arange(1, lax.axis_size("z")) if z is None else z
        y = lax.axis_index("y") ^ place[0]
        x = lax.axis_index("x") ^ place[1]
        return ((z * lax.axis_size("y") + y) * lax.axis_size("x") + x).astype(jnp.int32)

    params = pltpu.CompilerParams(vmem_limit_bytes=VMEM_LIMIT)
    key_near = straight(b_proj)
    key_line = along_z(b_proj)
    query_near = straight(c_proj)
    crossed = [near[place] for near in (key_near, query_near) for place in places() if place in near and any(place)]
    everything = slice(None)
    key_near.update({place: join(parts) for place, parts in diagonal(key_near, everything, None).items()})
    query_near.update({place: join(parts) for place, parts in diagonal(query_near, None, everything).items()})
    query_line = along_z(after(c_proj, *key_line))
    keys_here = with_core(join([key_near[place] for place in places()]))
    queries_here = with_core(join([query_near[place] for place in places()]))

    params = pltpu.CompilerParams(vmem_limit_bytes=VMEM_LIMIT)
    weight, cumulative, offset, decay, merge = pl.pallas_call(
        functools.partial(gates_kernel, heads, levels, padded),
        out_shape=[jax.ShapeDtypeStruct((heads, spans, Q), f32)] * 3
        + [jax.ShapeDtypeStruct((heads, spans * padded, N), f32)] * 2,
        scratch_shapes=[pltpu.VMEM((spans, N), f32)],
        compiler_params=params,
        name="gates",
    )(gates)
    weight, cumulative, offset = [v.reshape(heads, steps, group, Q) for v in (weight, cumulative, offset)]
    level_rows = lax.all_to_all(
        to_owners(after(level_weight, gates).astype(bf16)), ("z", "y"), split_axis=0, concat_axis=0, tiled=True
    )

    x_spec = pl.BlockSpec((rows, group * Q), lambda i, ids, *_: (0, ids[i]))
    span_spec = pl.BlockSpec((heads, None, group, Q), lambda i, ids, *_: (0, ids[i], 0, 0))
    level_spec = pl.BlockSpec((heads, group * padded, N), lambda i, ids, *_: (0, ids[i], 0))
    low_slots = max(group - 1, 1)
    vmem = pl.BlockSpec(memory_space=pltpu.VMEM)

    def within(start, count, base, trailing):
        return lambda i, *_: (jnp.clip(i - start, 0, count - 1) + base,) + (0,) * trailing

    def first_steps(id_lists):
        return [sum(ids.shape[0] for ids in id_lists[:at]) for at in range(len(id_lists))]

    totals, all_ids = [], []

    def states(sets):
        starts = first_steps([ids for ids, _ in sets])
        ids = join([ids for ids, _ in sets])
        count = ids.shape[0]
        key_specs = [
            pl.BlockSpec((block, N), within(start, own.shape[0], 0, 1)) for start, (own, _) in zip(starts, sets)
        ]
        low, total = pl.pallas_call(
            functools.partial(states_kernel, heads, width, group, padded, starts),
            grid_spec=pltpu.PrefetchScalarGridSpec(
                num_scalar_prefetch=2,
                grid=(count,),
                in_specs=[x_spec, span_spec, level_spec] + [spec for spec in key_specs for _ in range(CORES)],
                out_specs=[
                    pl.BlockSpec((None, low_slots, rows, N), lambda i, *_: (i, 0, 0, 0)),
                    pl.BlockSpec((None, rows, N), lambda i, *_: (i, 0, 0)),
                ],
            ),
            out_shape=[
                jax.ShapeDtypeStruct((count, low_slots, rows, N), bf16),
                jax.ShapeDtypeStruct((count, rows, N), f32),
            ],
            compiler_params=params,
            cost_estimate=pl.CostEstimate(
                flops=2 * rows * count * group * Q * N,
                bytes_accessed=4 * count * group * Q * (rows + N),
                transcendentals=0,
            ),
            name="states",
        )(ids, core, x_heads, weight, merge, *[key for _, keys in sets for key in keys])
        totals.append(total)
        all_ids.append(ids)
        return [(low, start) for start in starts]

    def outputs(sets, out):
        starts = first_steps([ids for ids, *_ in sets])
        ids = join([ids for ids, *_ in sets])
        count = ids.shape[0]
        tokens_here = count * group * Q
        set_specs, operands = [], []
        for start, (own, keys, queries, (low, base)) in zip(starts, sets):
            set_specs += [pl.BlockSpec((block, N), within(start, own.shape[0], 0, 1))] * (2 * CORES)
            set_specs.append(pl.BlockSpec((None, low_slots, rows, N), within(start, own.shape[0], base, 3)))
            operands += [*keys, *queries, low]
        before = [] if out is None else [out]
        fixed = [
            pl.BlockSpec(memory_space=pltpu.SMEM),
            x_spec,
            vmem,
            span_spec,
            span_spec,
            level_spec,
            pl.BlockSpec(
                (1, heads * levels, group * Q),
                lambda i, ids, *_: (ids[i] // per_shard, 0, ids[i] % per_shard),
            ),
        ]

        def kernel(*refs):
            last = 2 + len(fixed) + len(set_specs)
            outputs_kernel(
                heads, width, group, bits, padded, starts, *refs[:last], *refs[last + len(before) :]
            )

        return pl.pallas_call(
            kernel,
            grid_spec=pltpu.PrefetchScalarGridSpec(
                num_scalar_prefetch=2,
                grid=(count,),
                in_specs=fixed + set_specs + [pl.BlockSpec(memory_space=pl.ANY)] * len(before),
                out_specs=x_spec,
                scratch_shapes=[
                    pltpu.VMEM((N, group * Q), bf16),
                    pltpu.VMEM((rows, group * Q), f32),
                    pltpu.VMEM((heads, padded, group * Q), f32),
                    pltpu.VMEM((2, Q, Q), f32),
                    pltpu.VMEM((2, heads, Q, Q), bf16),
                ],
            ),
            out_shape=jax.ShapeDtypeStruct((rows, tokens), bf16),
            input_output_aliases={2 + len(fixed) + len(set_specs): 0} if before else {},
            compiler_params=params,
            cost_estimate=pl.CostEstimate(
                flops=2 * tokens_here * (Q * N + rows * Q + bits * rows * N),
                bytes_accessed=4 * tokens_here * (rows + N),
                transcendentals=heads * tokens_here * Q,
            ),
            name="outputs",
        )(ids, core, own_skip, x_heads, high, cumulative, offset, decay, level_rows, *operands, *before)

    here = join([group_ids(place, lax.axis_index("z").reshape(1)) for place in places()])
    one = (0, 0)
    sides = [place for place in places() if (place[0] > 0) != (place[1] > 0)]
    corners = [place for place in places() if place[0] and place[1]]
    far_ids = {place: group_ids(place) for place in places()}
    lows = {}
    if key_line:
        cut = block * ((len(key_line) + 1) // 3)
        by_x, by_y = slice(0, cut), slice(cut, None)
        key_far = straight(after(join(key_line), *crossed))
        keys_far = {one: with_core(key_far[one])}
        low_here, lows[one] = states([(here, keys_here), (far_ids[one], keys_far[one])])
        query_own = join(query_line)
        ready = (totals[0], query_own, queries_here[0])
        query_far = straight(after(query_own, *[key_far[place] for place in sides]))
        if sides:
            tied = {place: after(key_far[place], *ready) for place in sides}
            parts = diagonal(tied, by_x, by_y)
            keys_far.update({place: with_core(key_far[place]) for place in sides})
            lows.update(zip(sides, states([(far_ids[place], keys_far[place]) for place in sides])))
            if corners:
                joined = {place: join([after(part, totals[1]) for part in parts[place]]) for place in corners}
                keys_far.update({place: with_core(joined[place]) for place in corners})
                lows.update(zip(corners, states([(far_ids[place], keys_far[place]) for place in corners])))
    else:
        (low_here,) = states([(here, keys_here)])

    high = pl.pallas_call(
        functools.partial(tree_kernel, width, group, padded),
        grid_spec=pltpu.PrefetchScalarGridSpec(
            num_scalar_prefetch=1,
            in_specs=[vmem] * (1 + len(totals)),
            out_specs=vmem,
            scratch_shapes=[pltpu.VMEM((steps, rows, N), f32)],
        ),
        out_shape=jax.ShapeDtypeStruct((steps, rows, N), bf16),
        compiler_params=params,
        name="tree",
    )(join(all_ids), merge, *totals)

    out = outputs([(here, keys_here, queries_here, low_here)], None)
    if key_line:
        tied = {place: after(query_far[place], out) for place in sides}
        parts = diagonal(tied, by_x, by_y)
        queries_far = {place: with_core(query_far[place] if place == one else tied[place]) for place in [one] + sides}

        def far_sets(some):
            return [(far_ids[place], keys_far[place], queries_far[place], lows[place]) for place in some]

        early = [one] + sides[: len(sides) // 2]
        late = sides[len(sides) // 2 :]
        out = outputs(far_sets(early), out)
        for place in corners:
            queries_far[place] = with_core(join([after(part, out) for part in parts[place]]))
        if late or corners:
            out = outputs(far_sets(late + corners), out)
    return out


def solution(mesh):
    x = mesh.shape["head"] // CORES
    y = math.gcd(mesh.shape["seq"], x)
    z = mesh.shape["seq"] // y
    split_mesh = jax.sharding.Mesh(mesh.devices.reshape(z, y, x, CORES), ("z", "y", "x", "core"))
    seq = ("z", "y")
    head = ("x", "core")
    in_specs = (
        P((*head, *seq), None),
        P((*seq, *head), None),
        P((*seq, *head), None),
        P(head, seq),
        P(head, seq),
        P(head, None, seq),
        P(head),
    )
    out_specs = P((*head, *seq), None)
    return jax.shard_map(
        on_device, mesh=split_mesh, in_specs=in_specs, out_specs=out_specs, check_vma=False
    )
```

```python
import functools
import math

import jax
import jax.numpy as jnp
from jax import lax
from jax.experimental import pallas as pl
from jax.experimental.pallas import tpu as pltpu
from jax.sharding import PartitionSpec as P

P_SIZE = 64
N = 128
Q = 256
HALF = Q // 2
CORES = 2
NEVER = -1e30
VMEM_LIMIT = 60 * 1024 * 1024

f32 = jnp.float32
bf16 = jnp.bfloat16


def dot(a, b):
    return lax.dot_general(a, b, (((1,), (0,)), ((), ())), preferred_element_type=f32)


def exact_parts(value):
    high = value.astype(bf16)
    rest = value - high.astype(f32)
    middle = rest.astype(bf16)
    low = (rest - middle.astype(f32)).astype(bf16)
    return high, middle, low


def gates_kernel(heads, levels, padded, gates_ref, weight_ref, cum_ref, offset_ref, half_ref, decay_ref,
                 merge_ref, log_scratch):
    shards, _, span_rows, _ = gates_ref.shape
    spans = shards * span_rows
    upper = (
        lax.broadcasted_iota(jnp.int32, (Q, Q), 0) <= lax.broadcasted_iota(jnp.int32, (Q, Q), 1)
    ).astype(f32).astype(bf16)
    chunk = min(spans, 64)
    for head in range(heads):
        for shard in range(shards):
            rows = pl.ds(shard * span_rows, span_rows)
            gate = gates_ref[shard, 2 * head]
            step = gates_ref[shard, 2 * head + 1]
            high, middle, low = exact_parts(gate)
            cumulative = dot(high, upper) + dot(middle, upper) + dot(low, upper)
            span_log = cumulative[:, Q - 1 :]
            cum_ref[head, rows, :] = cumulative
            offset_ref[head, rows, :] = cumulative - jnp.log(step)
            half_log = cumulative[:, HALF - 1 : HALF]
            weight_ref[head, rows, :HALF] = jnp.exp(half_log - cumulative[:, :HALF]) * step[:, :HALF]
            weight_ref[head, rows, HALF:] = jnp.exp(span_log - cumulative[:, HALF:]) * step[:, HALF:]
            half_ref[head, rows, :] = jnp.broadcast_to(jnp.exp(span_log - half_log), (span_rows, N))
            log_scratch[rows, :] = jnp.broadcast_to(span_log, (span_rows, N))
        high, middle, low = exact_parts(log_scratch[...])

        def some_spans(at, carry):
            first = at * chunk
            size = (chunk * padded, spans)
            row = lax.broadcasted_iota(jnp.int32, size, 0)
            span = first + row // padded
            level = row % padded
            other = lax.broadcasted_iota(jnp.int32, size, 1)
            out_rows = pl.ds(pl.multiple_of(first * padded, chunk * padded), chunk * padded)
            bit = jnp.maximum(level - 1, 0)
            before = (other >= (span >> bit) << bit) & (other < span)
            before = before.astype(f32).astype(bf16)
            decay = dot(before, high) + dot(before, middle) + dot(before, low)
            has_bit = ((span >> bit) & 1)[:, :1] == 1
            decay_ref[head, out_rows, :] = jnp.where(has_bit, decay, NEVER)
            right = (other > span - (1 << bit)) & (other <= span)
            right = right.astype(f32).astype(bf16)
            merge_ref[head, out_rows, :] = jnp.exp(
                dot(right, high) + dot(right, middle) + dot(right, low)
            )
            return carry

        lax.fori_loop(0, spans // chunk, some_spans, 0)


def pick_set(step, starts, values):
    value = values[0]
    for start, other in zip(starts[1:], values[1:]):
        value = jnp.where(step >= start, other, value)
    return value


def pick(core, step, starts, pairs, local, group):
    half = group // CORES
    rows = slice(local % half * Q, (local % half + 1) * Q)
    mine = core == local // half
    return pick_set(step, starts, [jnp.where(mine, my_ref[rows, :], other_ref[rows, :]) for my_ref, other_ref in pairs])


def scaled(value, rows, width):
    parts = [value[head * width : (head + 1) * width] * row for head, row in enumerate(rows)]
    return jnp.concatenate(parts, axis=0) if len(parts) > 1 else parts[0]


def merge_blocks(left, right, merge_ref, row, width):
    return scaled(left, [merge_ref[head, row : row + 1, :] for head in range(merge_ref.shape[0])], width) + right


def states_kernel(heads, width, group, padded, starts, groups_ref, core_ref, x_ref, weight_ref, half_ref, merge_ref,
                  *refs):
    *key_refs, low_ref, total_ref = refs
    pairs = list(zip(key_refs[::2], key_refs[1::2]))
    kept = {}
    for local in range(group):
        columns = slice(local * Q, (local + 1) * Q)
        weights = [weight_ref[head, local : local + 1, :] for head in range(heads)]
        weighted = scaled(x_ref[:, columns].astype(f32), weights, width).astype(bf16)
        keys = pick(core_ref[0], pl.program_id(0), starts, pairs, local, group)
        first = dot(weighted[:, :HALF], keys[:HALF])
        low_ref[group + local] = first.astype(bf16)
        halves = [half_ref[head, local : local + 1, :] for head in range(heads)]
        state = scaled(first, halves, width) + dot(weighted[:, HALF:], keys[HALF:])
        bit = 0
        while local >> bit & 1:
            state = merge_blocks(kept[bit], state, merge_ref, local * padded + bit + 1, width)
            bit += 1
        kept[bit] = state
        low_ref[local] = state.astype(bf16)
    total_ref[...] = state


def tree_kernel(width, group, padded, groups_ref, merge_ref, *refs):
    *total_refs, high_ref, order_ref = refs
    steps = order_ref.shape[0]
    low_bits = group.bit_length() - 1
    at = 0
    for total_ref in total_refs:
        for slot in range(total_ref.shape[0]):
            order_ref[groups_ref[at]] = total_ref[slot]
            at += 1
    kept = {}
    for step in range(steps):
        state = order_ref[step]
        bit = 0
        while step >> bit & 1:
            row = step * padded + low_bits + bit + 1
            state = merge_blocks(kept[bit], state, merge_ref, row, width)
            bit += 1
        kept[bit] = state
        high_ref[step] = state.astype(bf16)


def outputs_kernel(heads, width, group, bits, padded, starts, groups_ref, core_ref, skip_ref, x_ref, high_ref,
                   cum_ref, offset_ref, decay_ref, level_ref, *refs):
    *set_refs, out_ref, query_ref, score_ref, sum_ref, mixing_ref = refs
    set_refs = [set_refs[5 * at : 5 * at + 5] for at in range(len(starts))]
    key_pairs = [refs[0:2] for refs in set_refs]
    query_pairs = [refs[2:4] for refs in set_refs]
    low_refs = [refs[4] for refs in set_refs]
    at = pl.program_id(0)
    step = groups_ref[at]
    low_bits = group.bit_length() - 1
    levels = bits + 1
    causal = lax.broadcasted_iota(jnp.int32, (HALF, HALF), 0) <= lax.broadcasted_iota(
        jnp.int32, (HALF, HALF), 1
    )
    halves = slice(0, HALF), slice(HALF, Q)
    head_rows = [slice(head * width, (head + 1) * width) for head in range(heads)]
    high_slots = [
        jnp.maximum((step >> (bit - low_bits) << (bit - low_bits)) - 1, 0) for bit in range(low_bits, bits)
    ]
    offsets = [jnp.transpose(offset_ref[head]) for head in range(heads)]

    def span_columns(local):
        return slice(local * Q, (local + 1) * Q)

    def low_state(slot):
        return pick_set(at, starts, [low_ref[slot] for low_ref in low_refs])

    def own_sums(local, head):
        weight = level_ref[0, :, span_columns(local)].astype(f32)[head * levels : head * levels + 1]
        return cum_ref[head, local : local + 1, :] + jnp.log(weight)

    def products(local):
        slot = local % 2
        columns = span_columns(local)
        query_ref[slot] = jnp.transpose(pick(core_ref[0], at, starts, query_pairs, local, group))
        keys = pick(core_ref[0], at, starts, key_pairs, local, group)
        active = [bit for bit in range(bits) if bit >= low_bits or local >> bit & 1]
        states = [
            low_state(((local >> bit) << bit) - 1) if bit < low_bits else high_ref[high_slots[bit - low_bits]]
            for bit in active
        ]
        result = dot(jnp.concatenate([keys, low_state(group + local)] + states, axis=0), query_ref[slot])
        for half in halves:
            score_ref[slot, half] = jnp.where(causal, result[half, half], 0.0)
        weights = level_ref[0, :, columns].astype(f32)
        for head, rows in enumerate(head_rows):
            cumulative = cum_ref[head, local : local + 1, :]
            decay = decay_ref[head, local * padded : local * padded + levels, :]
            decay = jnp.concatenate([decay] * (Q // N), axis=1)
            factors = weights[head * levels : (head + 1) * levels] * jnp.exp(cumulative + decay)
            total = None
            for place, bit in enumerate(active):
                first_row = Q + (place + 1) * heads * width + rows.start
                term = result[first_row : first_row + width] * factors[bit + 1 : bit + 2]
                total = term if total is None else total + term
            across = jnp.exp(own_sums(local, head)[:, HALF:] - cumulative[:, HALF - 1 : HALF])
            across = result[Q + rows.start : Q + rows.stop, HALF:] * across
            if total is None:
                sum_ref[slot, rows, :HALF] = jnp.zeros((width, HALF), f32)
                sum_ref[slot, rows, HALF:] = across
            else:
                sum_ref[slot, rows, :HALF] = total[:, :HALF]
                sum_ref[slot, rows, HALF:] = total[:, HALF:] + across

    def mix(local):
        slot = local % 2
        for head in range(heads):
            own = own_sums(local, head)
            column = offsets[head][:, local : local + 1]
            for half in halves:
                gaps = jnp.minimum(own[:, half] - column[half], 64.0)
                mixing_ref[slot, head, half] = (score_ref[slot, half] * jnp.exp(gaps)).astype(bf16)

    def finish(local):
        slot = local % 2
        for head, rows in enumerate(head_rows):
            for half in halves:
                columns = slice(local * Q + half.start, local * Q + half.stop)
                values = x_ref[rows, columns]
                result = dot(values, mixing_ref[slot, head, half]) + sum_ref[slot, rows, half]
                out_ref[rows, columns] = (result + skip_ref[head] * values.astype(f32)).astype(bf16)

    products(0)
    for local in range(group):
        if local + 1 < group:
            products(local + 1)
        mix(local)
        finish(local)


def exchange(value, axis, distance):
    pairs = [(place, place ^ distance) for place in range(lax.axis_size(axis))]
    return lax.ppermute(value, axis, pairs)


def along_z(own):
    pieces = [own]
    for distance in range(1, lax.axis_size("z")):
        low = distance & -distance
        pieces.append(exchange(pieces[distance ^ low], "z", low))
    return pieces[1:]


def places():
    both = [(y, x) for y in range(lax.axis_size("y")) for x in range(lax.axis_size("x"))]
    return sorted(both, key=lambda place: ((place[0] > 0) + (place[1] > 0), place))


def straight(piece):
    near = {(0, 0): piece}
    for y, x in places():
        if (y > 0) != (x > 0):
            near[y, x] = exchange(piece, "x", x) if x else exchange(piece, "y", y)
    return near


def diagonal(near, by_x, by_y):
    far = {}
    for y, x in places():
        if y and x:
            parts = []
            if by_x is not None:
                parts.append(exchange(near[0, x][by_x], "y", y))
            if by_y is not None:
                parts.append(exchange(near[y, 0][by_y], "x", x))
            far[y, x] = parts
    return far


def join(parts):
    return jnp.concatenate(parts, axis=0) if len(parts) > 1 else parts[0]


def with_core(piece):
    return piece, exchange(piece, "core", 1)


def after(value, *others):
    return lax.optimization_barrier((value, *others))[0]


def on_device(x_heads, b_proj, c_proj, log_gate, step_size, level_weight, skip):
    rows, tokens = x_heads.shape
    head_count, tok_dev = log_gate.shape
    levels = level_weight.shape[1]
    bits = levels - 1
    shards = lax.axis_size(("z", "y"))
    span_rows = tok_dev // Q
    spans = tokens // Q
    heads = max(rows // P_SIZE, 1)
    width = rows // heads
    sharing = P_SIZE // width
    block = b_proj.shape[0]
    group = CORES * block // Q
    padded = -(-levels // 8) * 8
    steps = spans // group
    per_shard = span_rows // group

    def to_owners(value):
        value = jnp.repeat(value, sharing, axis=0) if sharing > 1 else value
        value = value.reshape((shards, heads) + value.shape[1:])
        return value.reshape((shards, -1) + value.shape[3:])

    first_head = lax.axis_index(("z", "y")) * rows // P_SIZE
    own_skip = lax.dynamic_slice_in_dim(skip, first_head, heads, 0)
    core = lax.axis_index("core").astype(jnp.int32).reshape(1)

    def group_ids(place, z=None):
        z = lax.axis_index("z") ^ jnp.arange(1, lax.axis_size("z")) if z is None else z
        y = lax.axis_index("y") ^ place[0]
        x = lax.axis_index("x") ^ place[1]
        return ((z * lax.axis_size("y") + y) * lax.axis_size("x") + x).astype(jnp.int32)

    params = pltpu.CompilerParams(vmem_limit_bytes=VMEM_LIMIT)
    key_near = straight(b_proj)
    key_line = along_z(b_proj)
    log_gate = after(log_gate, *key_line)
    gates = jnp.stack(
        [log_gate.reshape(head_count, span_rows, Q), step_size.reshape(head_count, span_rows, Q)], axis=1
    )
    gates = lax.all_to_all(to_owners(gates), ("z", "y"), split_axis=0, concat_axis=0, tiled=True)
    query_near = straight(c_proj)
    crossed = [near[place] for near in (key_near, query_near) for place in places() if place in near and any(place)]
    everything = slice(None)
    key_near.update({place: join(parts) for place, parts in diagonal(key_near, everything, None).items()})
    query_near.update({place: join(parts) for place, parts in diagonal(query_near, None, everything).items()})
    query_line = along_z(after(c_proj, gates))
    keys_here = with_core(join([key_near[place] for place in places()]))
    queries_here = with_core(join([query_near[place] for place in places()]))

    params = pltpu.CompilerParams(vmem_limit_bytes=VMEM_LIMIT)
    weight, cumulative, offset, half, decay, merge = pl.pallas_call(
        functools.partial(gates_kernel, heads, levels, padded),
        out_shape=[jax.ShapeDtypeStruct((heads, spans, Q), f32)] * 3
        + [jax.ShapeDtypeStruct((heads, spans, N), f32)]
        + [jax.ShapeDtypeStruct((heads, spans * padded, N), f32)] * 2,
        scratch_shapes=[pltpu.VMEM((spans, N), f32)],
        compiler_params=params,
        name="gates",
    )(gates)
    weight, cumulative, offset = [v.reshape(heads, steps, group, Q) for v in (weight, cumulative, offset)]
    half = half.reshape(heads, steps, group, N)
    last_merge = merge.reshape(heads, steps, group * padded, N)[:, :, -padded:].reshape(heads, steps * padded, N)
    level_rows = lax.all_to_all(
        to_owners(after(level_weight, gates).astype(bf16)), ("z", "y"), split_axis=0, concat_axis=0, tiled=True
    )

    x_spec = pl.BlockSpec((rows, group * Q), lambda i, ids, *_: (0, ids[i]))
    span_spec = pl.BlockSpec((heads, None, group, Q), lambda i, ids, *_: (0, ids[i], 0, 0))
    level_spec = pl.BlockSpec((heads, group * padded, N), lambda i, ids, *_: (0, ids[i], 0))
    half_spec = pl.BlockSpec((heads, None, group, N), lambda i, ids, *_: (0, ids[i], 0, 0))
    low_slots = 2 * group
    vmem = pl.BlockSpec(memory_space=pltpu.VMEM)

    def within(start, count, base, trailing):
        return lambda i, *_: (jnp.clip(i - start, 0, count - 1) + base,) + (0,) * trailing

    def first_steps(id_lists):
        return [sum(ids.shape[0] for ids in id_lists[:at]) for at in range(len(id_lists))]

    totals, all_ids = [], []

    def states(sets):
        starts = first_steps([ids for ids, _ in sets])
        ids = join([ids for ids, _ in sets])
        count = ids.shape[0]
        key_specs = [
            pl.BlockSpec((block, N), within(start, own.shape[0], 0, 1)) for start, (own, _) in zip(starts, sets)
        ]
        low, total = pl.pallas_call(
            functools.partial(states_kernel, heads, width, group, padded, starts),
            grid_spec=pltpu.PrefetchScalarGridSpec(
                num_scalar_prefetch=2,
                grid=(count,),
                in_specs=[x_spec, span_spec, half_spec, level_spec] + [spec for spec in key_specs for _ in range(CORES)],
                out_specs=[
                    pl.BlockSpec((None, low_slots, rows, N), lambda i, *_: (i, 0, 0, 0)),
                    pl.BlockSpec((None, rows, N), lambda i, *_: (i, 0, 0)),
                ],
            ),
            out_shape=[
                jax.ShapeDtypeStruct((count, low_slots, rows, N), bf16),
                jax.ShapeDtypeStruct((count, rows, N), f32),
            ],
            compiler_params=params,
            cost_estimate=pl.CostEstimate(
                flops=2 * rows * count * group * Q * N,
                bytes_accessed=4 * count * group * Q * (rows + N),
                transcendentals=0,
            ),
            name="states",
        )(ids, core, x_heads, weight, half, merge, *[key for _, keys in sets for key in keys])
        totals.append(total)
        all_ids.append(ids)
        return [(low, start) for start in starts]

    def outputs(sets, out):
        starts = first_steps([ids for ids, *_ in sets])
        ids = join([ids for ids, *_ in sets])
        count = ids.shape[0]
        tokens_here = count * group * Q
        set_specs, operands = [], []
        for start, (own, keys, queries, (low, base)) in zip(starts, sets):
            set_specs += [pl.BlockSpec((block, N), within(start, own.shape[0], 0, 1))] * (2 * CORES)
            set_specs.append(pl.BlockSpec((None, low_slots, rows, N), within(start, own.shape[0], base, 3)))
            operands += [*keys, *queries, low]
        before = [] if out is None else [out]
        fixed = [
            pl.BlockSpec(memory_space=pltpu.SMEM),
            x_spec,
            vmem,
            span_spec,
            span_spec,
            level_spec,
            pl.BlockSpec(
                (1, heads * levels, group * Q),
                lambda i, ids, *_: (ids[i] // per_shard, 0, ids[i] % per_shard),
            ),
        ]

        def kernel(*refs):
            last = 2 + len(fixed) + len(set_specs)
            outputs_kernel(
                heads, width, group, bits, padded, starts, *refs[:last], *refs[last + len(before) :]
            )

        return pl.pallas_call(
            kernel,
            grid_spec=pltpu.PrefetchScalarGridSpec(
                num_scalar_prefetch=2,
                grid=(count,),
                in_specs=fixed + set_specs + [pl.BlockSpec(memory_space=pl.ANY)] * len(before),
                out_specs=x_spec,
                scratch_shapes=[
                    pltpu.VMEM((2, N, Q), bf16),
                    pltpu.VMEM((2, Q, HALF), f32),
                    pltpu.VMEM((2, rows, Q), f32),
                    pltpu.VMEM((2, heads, Q, HALF), bf16),
                ],
            ),
            out_shape=jax.ShapeDtypeStruct((rows, tokens), bf16),
            input_output_aliases={2 + len(fixed) + len(set_specs): 0} if before else {},
            compiler_params=params,
            cost_estimate=pl.CostEstimate(
                flops=2 * tokens_here * (Q * N + rows * Q + bits * rows * N),
                bytes_accessed=4 * tokens_here * (rows + N),
                transcendentals=heads * tokens_here * Q,
            ),
            name="outputs",
        )(ids, core, own_skip, x_heads, high, cumulative, offset, decay, level_rows, *operands, *before)

    here = join([group_ids(place, lax.axis_index("z").reshape(1)) for place in places()])
    one = (0, 0)
    sides = [place for place in places() if (place[0] > 0) != (place[1] > 0)]
    corners = [place for place in places() if place[0] and place[1]]
    far_ids = {place: group_ids(place) for place in places()}
    lows = {}
    if key_line:
        cut = block * ((len(key_line) + 1) // 3)
        by_x, by_y = slice(0, cut), slice(cut, None)
        key_far = straight(after(join(key_line), *crossed))
        keys_far = {one: with_core(key_far[one])}
        low_here, lows[one] = states([(here, keys_here), (far_ids[one], keys_far[one])])
        query_own = join(query_line)
        query_far = straight(after(query_own, *[key_far[place] for place in sides]))
        if sides:
            tied = {place: after(key_far[place], weight) for place in sides}
            parts = diagonal(tied, by_x, by_y)
            keys_far.update({place: with_core(key_far[place]) for place in sides})
            lows.update(zip(sides, states([(far_ids[place], keys_far[place]) for place in sides])))
            if corners:
                joined = {place: join([after(part, *totals[:2]) for part in parts[place]]) for place in corners}
                keys_far.update({place: with_core(joined[place]) for place in corners})
                lows.update(zip(corners, states([(far_ids[place], keys_far[place]) for place in corners])))
    else:
        (low_here,) = states([(here, keys_here)])

    high = pl.pallas_call(
        functools.partial(tree_kernel, width, group, padded),
        grid_spec=pltpu.PrefetchScalarGridSpec(
            num_scalar_prefetch=1,
            in_specs=[vmem] * (1 + len(totals)),
            out_specs=vmem,
            scratch_shapes=[pltpu.VMEM((steps, rows, N), f32)],
        ),
        out_shape=jax.ShapeDtypeStruct((steps, rows, N), bf16),
        compiler_params=params,
        name="tree",
    )(join(all_ids), last_merge, *totals)

    out = outputs([(here, keys_here, queries_here, low_here)], None)
    if key_line:
        tied = {place: after(query_far[place], out) for place in sides}
        parts = diagonal(tied, by_x, by_y)
        queries_far = {place: with_core(query_far[place] if place == one else tied[place]) for place in [one] + sides}

        def far_sets(some):
            return [(far_ids[place], keys_far[place], queries_far[place], lows[place]) for place in some]

        early = [one] + sides[: len(sides) // 2]
        late = sides[len(sides) // 2 :]
        out = outputs(far_sets(early), out)
        for place in corners:
            queries_far[place] = with_core(join([after(part, out) for part in parts[place]]))
        if late or corners:
            out = outputs(far_sets(late + corners), out)
    return out


def solution(mesh):
    x = mesh.shape["head"] // CORES
    y = math.gcd(mesh.shape["seq"], x)
    z = mesh.shape["seq"] // y
    split_mesh = jax.sharding.Mesh(mesh.devices.reshape(z, y, x, CORES), ("z", "y", "x", "core"))
    seq = ("z", "y")
    head = ("x", "core")
    in_specs = (
        P((*head, *seq), None),
        P((*seq, *head), None),
        P((*seq, *head), None),
        P(head, seq),
        P(head, seq),
        P(head, None, seq),
        P(head),
    )
    out_specs = P((*head, *seq), None)
    return jax.shard_map(
        on_device, mesh=split_mesh, in_specs=in_specs, out_specs=out_specs, check_vma=False
    )
```

```python
import functools
import math

import jax
import jax.numpy as jnp
from jax import lax
from jax.experimental import pallas as pl
from jax.experimental.pallas import tpu as pltpu
from jax.sharding import PartitionSpec as P

P_SIZE = 64
N = 128
Q = 256
HALF = Q // 2
CORES = 2
NEVER = -1e30
VMEM_LIMIT = 60 * 1024 * 1024

f32 = jnp.float32
bf16 = jnp.bfloat16


def dot(a, b):
    return lax.dot_general(a, b, (((1,), (0,)), ((), ())), preferred_element_type=f32)


def dot_nt(a, b):
    return lax.dot_general(a, b, (((1,), (1,)), ((), ())), preferred_element_type=f32)


def exact_parts(value):
    high = value.astype(bf16)
    rest = value - high.astype(f32)
    middle = rest.astype(bf16)
    low = (rest - middle.astype(f32)).astype(bf16)
    return high, middle, low


def gates_kernel(heads, levels, padded, gates_ref, weight_ref, cum_ref, offset_ref, half_ref, decay_ref,
                 merge_ref, log_scratch):
    shards, _, span_rows, _ = gates_ref.shape
    spans = shards * span_rows
    upper = (
        lax.broadcasted_iota(jnp.int32, (Q, Q), 0) <= lax.broadcasted_iota(jnp.int32, (Q, Q), 1)
    ).astype(f32).astype(bf16)
    chunk = min(spans, 64)
    for head in range(heads):
        for shard in range(shards):
            rows = pl.ds(shard * span_rows, span_rows)
            gate = gates_ref[shard, 2 * head]
            step = gates_ref[shard, 2 * head + 1]
            high, middle, low = exact_parts(gate)
            cumulative = dot(high, upper) + dot(middle, upper) + dot(low, upper)
            span_log = cumulative[:, Q - 1 :]
            cum_ref[head, rows, :] = cumulative
            offset_ref[head, rows, :] = cumulative - jnp.log(step)
            half_log = cumulative[:, HALF - 1 : HALF]
            weight_ref[head, rows, :HALF] = jnp.exp(half_log - cumulative[:, :HALF]) * step[:, :HALF]
            weight_ref[head, rows, HALF:] = jnp.exp(span_log - cumulative[:, HALF:]) * step[:, HALF:]
            half_ref[head, rows, :] = jnp.broadcast_to(jnp.exp(span_log - half_log), (span_rows, N))
            log_scratch[rows, :] = jnp.broadcast_to(span_log, (span_rows, N))
        high, middle, low = exact_parts(log_scratch[...])

        def some_spans(at, carry):
            first = at * chunk
            size = (chunk * padded, spans)
            row = lax.broadcasted_iota(jnp.int32, size, 0)
            span = first + row // padded
            level = row % padded
            other = lax.broadcasted_iota(jnp.int32, size, 1)
            out_rows = pl.ds(pl.multiple_of(first * padded, chunk * padded), chunk * padded)
            bit = jnp.maximum(level - 1, 0)
            before = (other >= (span >> bit) << bit) & (other < span)
            before = before.astype(f32).astype(bf16)
            decay = dot(before, high) + dot(before, middle) + dot(before, low)
            has_bit = ((span >> bit) & 1)[:, :1] == 1
            decay_ref[head, out_rows, :] = jnp.where(has_bit, decay, NEVER)
            right = (other > span - (1 << bit)) & (other <= span)
            right = right.astype(f32).astype(bf16)
            merge_ref[head, out_rows, :] = jnp.exp(
                dot(right, high) + dot(right, middle) + dot(right, low)
            )
            return carry

        lax.fori_loop(0, spans // chunk, some_spans, 0)


def pick_set(step, starts, values):
    value = values[0]
    for start, other in zip(starts[1:], values[1:]):
        value = jnp.where(step >= start, other, value)
    return value


def pick(core, step, starts, pairs, local, group):
    half = group // CORES
    rows = slice(local % half * Q, (local % half + 1) * Q)
    mine = core == local // half
    return pick_set(step, starts, [jnp.where(mine, my_ref[rows, :], other_ref[rows, :]) for my_ref, other_ref in pairs])


def scaled(value, rows, width):
    parts = [value[head * width : (head + 1) * width] * row for head, row in enumerate(rows)]
    return jnp.concatenate(parts, axis=0) if len(parts) > 1 else parts[0]


def merge_blocks(left, right, merge_ref, row, width):
    return scaled(left, [merge_ref[head, row : row + 1, :] for head in range(merge_ref.shape[0])], width) + right


def states_kernel(heads, width, group, padded, starts, groups_ref, core_ref, x_ref, weight_ref, half_ref, merge_ref,
                  *refs):
    *key_refs, low_ref, total_ref = refs
    pairs = list(zip(key_refs[::2], key_refs[1::2]))
    kept = {}
    for local in range(group):
        columns = slice(local * Q, (local + 1) * Q)
        weights = [weight_ref[head, local : local + 1, :] for head in range(heads)]
        weighted = scaled(x_ref[:, columns].astype(f32), weights, width).astype(bf16)
        keys = pick(core_ref[0], pl.program_id(0), starts, pairs, local, group)
        first = dot(weighted[:, :HALF], keys[:HALF])
        low_ref[group + local] = first.astype(bf16)
        halves = [half_ref[head, local : local + 1, :] for head in range(heads)]
        state = scaled(first, halves, width) + dot(weighted[:, HALF:], keys[HALF:])
        bit = 0
        while local >> bit & 1:
            state = merge_blocks(kept[bit], state, merge_ref, local * padded + bit + 1, width)
            bit += 1
        kept[bit] = state
        low_ref[local] = state.astype(bf16)
    total_ref[...] = state


def tree_kernel(width, group, padded, groups_ref, merge_ref, *refs):
    *total_refs, high_ref, order_ref = refs
    steps = order_ref.shape[0]
    low_bits = group.bit_length() - 1
    at = 0
    for total_ref in total_refs:
        for slot in range(total_ref.shape[0]):
            order_ref[groups_ref[at]] = total_ref[slot]
            at += 1
    kept = {}
    for step in range(steps):
        state = order_ref[step]
        bit = 0
        while step >> bit & 1:
            row = step * padded + low_bits + bit + 1
            state = merge_blocks(kept[bit], state, merge_ref, row, width)
            bit += 1
        kept[bit] = state
        high_ref[step] = state.astype(bf16)


def outputs_kernel(heads, width, group, bits, padded, starts, groups_ref, core_ref, skip_ref, x_ref, high_ref,
                   cum_ref, offset_ref, decay_ref, level_ref, *refs):
    *set_refs, out_ref, score_ref, sum_ref, factor_ref, select_ref = refs
    set_refs = [set_refs[5 * at : 5 * at + 5] for at in range(len(starts))]
    key_pairs = [refs[0:2] for refs in set_refs]
    query_pairs = [refs[2:4] for refs in set_refs]
    low_refs = [refs[4] for refs in set_refs]
    at = pl.program_id(0)
    step = groups_ref[at]
    low_bits = group.bit_length() - 1
    levels = bits + 1
    size = (HALF, Q)
    causal = lax.broadcasted_iota(jnp.int32, size, 0) <= lax.broadcasted_iota(jnp.int32, size, 1) % HALF
    halves = slice(0, HALF), slice(HALF, Q)
    head_rows = [slice(head * width, (head + 1) * width) for head in range(heads)]
    high_slots = [
        jnp.maximum((step >> (bit - low_bits) << (bit - low_bits)) - 1, 0) for bit in range(low_bits, bits)
    ]
    part_rows = 3 * len(halves) * group
    pad_rows = -part_rows % 16 + 16
    offsets = []
    for head in range(heads):
        parts = exact_parts(offset_ref[head])
        tiles = [part.astype(f32)[:, half] for part in parts for half in halves]
        tiles.append(jnp.ones((pad_rows, HALF), f32))
        offsets.append(jnp.transpose(jnp.concatenate(tiles, axis=0)).astype(bf16))

    @pl.when(at == 0)
    def _():
        size = (part_rows, Q)
        row = lax.broadcasted_iota(jnp.int32, size, 0)
        same_half = (row // group) % len(halves) == lax.broadcasted_iota(jnp.int32, size, 1) // HALF
        for local in range(group):
            chosen = same_half & (row % group == local)
            select_ref[local, :part_rows] = jnp.where(chosen, -1.0, 0.0).astype(bf16)

    def low_state(slot):
        return pick_set(at, starts, [low_ref[slot] for low_ref in low_refs])

    def products(local):
        slot = local % 2
        columns = slice(local * Q, (local + 1) * Q)
        queries = pick(core_ref[0], at, starts, query_pairs, local, group)
        keys = pick(core_ref[0], at, starts, key_pairs, local, group)
        nothing = jnp.zeros((HALF, N), bf16)
        apart = jnp.concatenate(
            [
                jnp.concatenate([queries[:HALF], nothing], axis=1),
                jnp.concatenate([nothing, queries[HALF:]], axis=1),
            ],
            axis=0,
        )
        score = dot_nt(jnp.concatenate([keys[:HALF], keys[HALF:]], axis=1), apart)
        score_ref[slot] = jnp.where(causal, score, 0.0)
        active = [bit for bit in range(bits) if bit >= low_bits or local >> bit & 1]
        states = [
            low_state(((local >> bit) << bit) - 1) if bit < low_bits else high_ref[high_slots[bit - low_bits]]
            for bit in active
        ]
        result = dot_nt(jnp.concatenate([low_state(group + local)] + states, axis=0), queries)
        weights = level_ref[0, :, columns].astype(f32)
        right = lax.broadcasted_iota(jnp.int32, (1, Q), 1) >= HALF
        for head, rows in enumerate(head_rows):
            cumulative = cum_ref[head, local : local + 1, :]
            weight = weights[head * levels : (head + 1) * levels]
            decay = decay_ref[head, local * padded : local * padded + levels, :]
            decay = jnp.concatenate([decay] * (Q // N), axis=1)
            factor_ref[slot, head, :levels] = weight * jnp.exp(cumulative + decay)
            own = cumulative + jnp.log(weight[:1])
            across = jnp.where(right, jnp.exp(own - cumulative[:, HALF - 1 : HALF]), 0.0)
            total = result[rows] * across
            for place, bit in enumerate(active):
                first_row = (place + 1) * heads * width + rows.start
                total += result[first_row : first_row + width] * factor_ref[slot, head, bit + 1 : bit + 2]
            sum_ref[slot, rows] = total

    def finish(local):
        slot = local % 2
        columns = slice(local * Q, (local + 1) * Q)
        weights = level_ref[0, :, columns].astype(f32)
        for head, rows in enumerate(head_rows):
            own = cum_ref[head, local : local + 1, :] + jnp.log(weights[head * levels : head * levels + 1])
            row = lax.broadcasted_iota(jnp.int32, (pad_rows, Q), 0)
            tail = jnp.zeros((pad_rows, Q), f32)
            for place, part in enumerate(exact_parts(own)):
                tail = jnp.where(row == place, part.astype(f32), tail)
            side = jnp.concatenate([select_ref[local, :part_rows], tail.astype(bf16)], axis=0)
            gaps = jnp.minimum(dot(offsets[head], side), 64.0)
            mixing = (score_ref[slot] * jnp.exp(gaps)).astype(bf16)
            for half in halves:
                here = slice(local * Q + half.start, local * Q + half.stop)
                values = x_ref[rows, here]
                result = dot(values, mixing[:, half]) + sum_ref[slot, rows, half]
                out_ref[rows, here] = (result + skip_ref[head] * values.astype(f32)).astype(bf16)

    products(0)
    for local in range(group):
        if local + 1 < group:
            products(local + 1)
        finish(local)


def exchange(value, axis, distance):
    pairs = [(place, place ^ distance) for place in range(lax.axis_size(axis))]
    return lax.ppermute(value, axis, pairs)


def along_z(own):
    pieces = [own]
    for distance in range(1, lax.axis_size("z")):
        low = distance & -distance
        pieces.append(exchange(pieces[distance ^ low], "z", low))
    return pieces[1:]


def places():
    both = [(y, x) for y in range(lax.axis_size("y")) for x in range(lax.axis_size("x"))]
    return sorted(both, key=lambda place: ((place[0] > 0) + (place[1] > 0), place))


def straight(piece):
    near = {(0, 0): piece}
    for y, x in places():
        if (y > 0) != (x > 0):
            near[y, x] = exchange(piece, "x", x) if x else exchange(piece, "y", y)
    return near


def diagonal(near, by_x, by_y):
    far = {}
    for y, x in places():
        if y and x:
            parts = []
            if by_x is not None:
                parts.append(exchange(near[0, x][by_x], "y", y))
            if by_y is not None:
                parts.append(exchange(near[y, 0][by_y], "x", x))
            far[y, x] = parts
    return far


def join(parts):
    return jnp.concatenate(parts, axis=0) if len(parts) > 1 else parts[0]


def with_core(piece):
    return piece, exchange(piece, "core", 1)


def after(value, *others):
    return lax.optimization_barrier((value, *others))[0]


def on_device(x_heads, b_proj, c_proj, log_gate, step_size, level_weight, skip):
    rows, tokens = x_heads.shape
    head_count, tok_dev = log_gate.shape
    levels = level_weight.shape[1]
    bits = levels - 1
    shards = lax.axis_size(("z", "y"))
    span_rows = tok_dev // Q
    spans = tokens // Q
    heads = max(rows // P_SIZE, 1)
    width = rows // heads
    sharing = P_SIZE // width
    block = b_proj.shape[0]
    group = CORES * block // Q
    padded = -(-levels // 8) * 8
    steps = spans // group
    per_shard = span_rows // group

    def to_owners(value):
        value = jnp.repeat(value, sharing, axis=0) if sharing > 1 else value
        value = value.reshape((shards, heads) + value.shape[1:])
        return value.reshape((shards, -1) + value.shape[3:])

    first_head = lax.axis_index(("z", "y")) * rows // P_SIZE
    own_skip = lax.dynamic_slice_in_dim(skip, first_head, heads, 0)
    core = lax.axis_index("core").astype(jnp.int32).reshape(1)

    def group_ids(place, z=None):
        z = lax.axis_index("z") ^ jnp.arange(1, lax.axis_size("z")) if z is None else z
        y = lax.axis_index("y") ^ place[0]
        x = lax.axis_index("x") ^ place[1]
        return ((z * lax.axis_size("y") + y) * lax.axis_size("x") + x).astype(jnp.int32)

    params = pltpu.CompilerParams(vmem_limit_bytes=VMEM_LIMIT)
    key_near = straight(b_proj)
    key_line = along_z(b_proj)
    gates = jnp.stack(
        [log_gate.reshape(head_count, span_rows, Q), step_size.reshape(head_count, span_rows, Q)], axis=1
    )
    gates = lax.all_to_all(to_owners(gates), ("z", "y"), split_axis=0, concat_axis=0, tiled=True)
    query_near = straight(c_proj)
    crossed = [near[place] for near in (key_near, query_near) for place in places() if place in near and any(place)]
    everything = slice(None)
    key_near.update({place: join(parts) for place, parts in diagonal(key_near, everything, None).items()})
    query_near.update({place: join(parts) for place, parts in diagonal(query_near, None, everything).items()})
    query_line = along_z(after(c_proj, *key_line))
    keys_here = with_core(join([key_near[place] for place in places()]))

    params = pltpu.CompilerParams(vmem_limit_bytes=VMEM_LIMIT)
    weight, cumulative, offset, half, decay, merge = pl.pallas_call(
        functools.partial(gates_kernel, heads, levels, padded),
        out_shape=[jax.ShapeDtypeStruct((heads, spans, Q), f32)] * 3
        + [jax.ShapeDtypeStruct((heads, spans, N), f32)]
        + [jax.ShapeDtypeStruct((heads, spans * padded, N), f32)] * 2,
        scratch_shapes=[pltpu.VMEM((spans, N), f32)],
        compiler_params=params,
        name="gates",
    )(gates)
    weight, cumulative, offset = [v.reshape(heads, steps, group, Q) for v in (weight, cumulative, offset)]
    half = half.reshape(heads, steps, group, N)
    last_merge = merge.reshape(heads, steps, group * padded, N)[:, :, -padded:].reshape(heads, steps * padded, N)
    x_spec = pl.BlockSpec((rows, group * Q), lambda i, ids, *_: (0, ids[i]))
    span_spec = pl.BlockSpec((heads, None, group, Q), lambda i, ids, *_: (0, ids[i], 0, 0))
    level_spec = pl.BlockSpec((heads, group * padded, N), lambda i, ids, *_: (0, ids[i], 0))
    half_spec = pl.BlockSpec((heads, None, group, N), lambda i, ids, *_: (0, ids[i], 0, 0))
    low_slots = 2 * group
    vmem = pl.BlockSpec(memory_space=pltpu.VMEM)

    def within(start, count, base, trailing):
        return lambda i, *_: (jnp.clip(i - start, 0, count - 1) + base,) + (0,) * trailing

    def first_steps(id_lists):
        return [sum(ids.shape[0] for ids in id_lists[:at]) for at in range(len(id_lists))]

    totals, all_ids = [], []

    def states(sets):
        starts = first_steps([ids for ids, _ in sets])
        ids = join([ids for ids, _ in sets])
        count = ids.shape[0]
        key_specs = [
            pl.BlockSpec((block, N), within(start, own.shape[0], 0, 1)) for start, (own, _) in zip(starts, sets)
        ]
        low, total = pl.pallas_call(
            functools.partial(states_kernel, heads, width, group, padded, starts),
            grid_spec=pltpu.PrefetchScalarGridSpec(
                num_scalar_prefetch=2,
                grid=(count,),
                in_specs=[x_spec, span_spec, half_spec, level_spec] + [spec for spec in key_specs for _ in range(CORES)],
                out_specs=[
                    pl.BlockSpec((None, low_slots, rows, N), lambda i, *_: (i, 0, 0, 0)),
                    pl.BlockSpec((None, rows, N), lambda i, *_: (i, 0, 0)),
                ],
            ),
            out_shape=[
                jax.ShapeDtypeStruct((count, low_slots, rows, N), bf16),
                jax.ShapeDtypeStruct((count, rows, N), f32),
            ],
            compiler_params=params,
            cost_estimate=pl.CostEstimate(
                flops=2 * rows * count * group * Q * N,
                bytes_accessed=4 * count * group * Q * (rows + N),
                transcendentals=0,
            ),
            name="states",
        )(ids, core, x_heads, weight, half, merge, *[key for _, keys in sets for key in keys])
        totals.append(total)
        all_ids.append(ids)
        return [(low, start) for start in starts]

    def outputs(sets, out):
        starts = first_steps([ids for ids, *_ in sets])
        ids = join([ids for ids, *_ in sets])
        count = ids.shape[0]
        tokens_here = count * group * Q
        set_specs, operands = [], []
        for start, (own, keys, queries, (low, base)) in zip(starts, sets):
            set_specs += [pl.BlockSpec((block, N), within(start, own.shape[0], 0, 1))] * (2 * CORES)
            set_specs.append(pl.BlockSpec((None, low_slots, rows, N), within(start, own.shape[0], base, 3)))
            operands += [*keys, *queries, low]
        before = [] if out is None else [out]
        fixed = [
            pl.BlockSpec(memory_space=pltpu.SMEM),
            x_spec,
            vmem,
            span_spec,
            span_spec,
            level_spec,
            pl.BlockSpec(
                (1, heads * levels, group * Q),
                lambda i, ids, *_: (ids[i] // per_shard, 0, ids[i] % per_shard),
            ),
        ]

        def kernel(*refs):
            last = 2 + len(fixed) + len(set_specs)
            outputs_kernel(
                heads, width, group, bits, padded, starts, *refs[:last], *refs[last + len(before) :]
            )

        return pl.pallas_call(
            kernel,
            grid_spec=pltpu.PrefetchScalarGridSpec(
                num_scalar_prefetch=2,
                grid=(count,),
                in_specs=fixed + set_specs + [pl.BlockSpec(memory_space=pl.ANY)] * len(before),
                out_specs=x_spec,
                scratch_shapes=[
                    pltpu.VMEM((2, HALF, Q), f32),
                    pltpu.VMEM((2, rows, Q), f32),
                    pltpu.VMEM((2, heads, padded, Q), f32),
                    pltpu.VMEM((group, 8 * group, Q), bf16),
                ],
            ),
            out_shape=jax.ShapeDtypeStruct((rows, tokens), bf16),
            input_output_aliases={2 + len(fixed) + len(set_specs): 0} if before else {},
            compiler_params=params,
            cost_estimate=pl.CostEstimate(
                flops=2 * tokens_here * (Q * N + rows * Q + bits * rows * N),
                bytes_accessed=4 * tokens_here * (rows + N),
                transcendentals=heads * tokens_here * Q,
            ),
            name="outputs",
        )(ids, core, own_skip, x_heads, high, cumulative, offset, decay, level_rows, *operands, *before)

    here = join([group_ids(place, lax.axis_index("z").reshape(1)) for place in places()])
    one = (0, 0)
    sides = [place for place in places() if (place[0] > 0) != (place[1] > 0)]
    corners = [place for place in places() if place[0] and place[1]]
    far_ids = {place: group_ids(place) for place in places()}
    lows = {}
    if key_line:
        cut = block * ((len(key_line) + 1) // 3)
        by_x, by_y = slice(0, cut), slice(cut, None)
        key_far = straight(after(join(key_line), *crossed))
        keys_far = {one: with_core(key_far[one])}
        low_here, lows[one] = states([(here, keys_here), (far_ids[one], keys_far[one])])
        query_own = join([after(piece, totals[0]) for piece in query_line])
        query_far = straight(after(query_own, *[key_far[place] for place in sides]))
        if sides:
            tied = {place: after(key_far[place], weight) for place in sides}
            parts = diagonal(tied, by_x, by_y)
            keys_far.update({place: with_core(key_far[place]) for place in sides})
            lows.update(zip(sides, states([(far_ids[place], keys_far[place]) for place in sides])))
            if corners:
                joined = {place: join([after(part, *totals[:2]) for part in parts[place]]) for place in corners}
                keys_far.update({place: with_core(joined[place]) for place in corners})
                lows.update(zip(corners, states([(far_ids[place], keys_far[place]) for place in corners])))
    else:
        (low_here,) = states([(here, keys_here)])

    level_rows = lax.all_to_all(
        to_owners(after(level_weight, totals[0]).astype(bf16)), ("z", "y"), split_axis=0, concat_axis=0, tiled=True
    )
    queries_here = with_core(join([after(query_near[place], totals[0]) for place in places()]))
    high = pl.pallas_call(
        functools.partial(tree_kernel, width, group, padded),
        grid_spec=pltpu.PrefetchScalarGridSpec(
            num_scalar_prefetch=1,
            in_specs=[vmem] * (1 + len(totals)),
            out_specs=vmem,
            scratch_shapes=[pltpu.VMEM((steps, rows, N), f32)],
        ),
        out_shape=jax.ShapeDtypeStruct((steps, rows, N), bf16),
        compiler_params=params,
        name="tree",
    )(join(all_ids), last_merge, *totals)

    out = outputs([(here, keys_here, queries_here, low_here)], None)
    if key_line:
        tied = {place: after(query_far[place], out) for place in sides}
        parts = diagonal(tied, by_x, by_y)
        queries_far = {place: with_core(query_far[place] if place == one else tied[place]) for place in [one] + sides}

        def far_sets(some):
            return [(far_ids[place], keys_far[place], queries_far[place], lows[place]) for place in some]

        early = [one] + sides[: len(sides) // 2]
        late = sides[len(sides) // 2 :]
        out = outputs(far_sets(early), out)
        for place in corners:
            queries_far[place] = with_core(join([after(part, out) for part in parts[place]]))
        if late or corners:
            out = outputs(far_sets(late + corners), out)
    return out


def solution(mesh):
    x = mesh.shape["head"] // CORES
    y = math.gcd(mesh.shape["seq"], x)
    z = mesh.shape["seq"] // y
    split_mesh = jax.sharding.Mesh(mesh.devices.reshape(z, y, x, CORES), ("z", "y", "x", "core"))
    seq = ("z", "y")
    head = ("x", "core")
    in_specs = (
        P((*head, *seq), None),
        P((*seq, *head), None),
        P((*seq, *head), None),
        P(head, seq),
        P(head, seq),
        P(head, None, seq),
        P(head),
    )
    out_specs = P((*head, *seq), None)
    return jax.shard_map(
        on_device, mesh=split_mesh, in_specs=in_specs, out_specs=out_specs, check_vma=False
    )
```

```python
import functools
import math

import jax
import jax.numpy as jnp
from jax import lax
from jax.experimental import pallas as pl
from jax.experimental.pallas import tpu as pltpu
from jax.sharding import PartitionSpec as P

P_SIZE = 64
N = 128
Q = 256
HALF = Q // 2
CORES = 2
NEVER = -1e30
VMEM_LIMIT = 60 * 1024 * 1024

f32 = jnp.float32
bf16 = jnp.bfloat16


def dot(a, b):
    return lax.dot_general(a, b, (((1,), (0,)), ((), ())), preferred_element_type=f32)


def exact_parts(value):
    high = value.astype(bf16)
    rest = value - high.astype(f32)
    middle = rest.astype(bf16)
    low = (rest - middle.astype(f32)).astype(bf16)
    return high, middle, low


def gates_kernel(heads, levels, padded, gates_ref, weight_ref, cum_ref, offset_ref, half_ref, decay_ref,
                 merge_ref, log_scratch):
    shards, _, span_rows, _ = gates_ref.shape
    spans = shards * span_rows
    upper = (
        lax.broadcasted_iota(jnp.int32, (Q, Q), 0) <= lax.broadcasted_iota(jnp.int32, (Q, Q), 1)
    ).astype(f32).astype(bf16)
    chunk = min(spans, 64)
    for head in range(heads):
        for shard in range(shards):
            rows = pl.ds(shard * span_rows, span_rows)
            gate = gates_ref[shard, 2 * head]
            step = gates_ref[shard, 2 * head + 1]
            high, middle, low = exact_parts(gate)
            cumulative = dot(high, upper) + dot(middle, upper) + dot(low, upper)
            span_log = cumulative[:, Q - 1 :]
            cum_ref[head, rows, :] = cumulative
            offset_ref[head, rows, :] = cumulative - jnp.log(step)
            half_log = cumulative[:, HALF - 1 : HALF]
            weight_ref[head, rows, :HALF] = jnp.exp(half_log - cumulative[:, :HALF]) * step[:, :HALF]
            weight_ref[head, rows, HALF:] = jnp.exp(span_log - cumulative[:, HALF:]) * step[:, HALF:]
            half_ref[head, rows, :] = jnp.broadcast_to(jnp.exp(span_log - half_log), (span_rows, N))
            log_scratch[rows, :] = jnp.broadcast_to(span_log, (span_rows, N))
        high, middle, low = exact_parts(log_scratch[...])

        def some_spans(at, carry):
            first = at * chunk
            size = (chunk * padded, spans)
            row = lax.broadcasted_iota(jnp.int32, size, 0)
            span = first + row // padded
            level = row % padded
            other = lax.broadcasted_iota(jnp.int32, size, 1)
            out_rows = pl.ds(pl.multiple_of(first * padded, chunk * padded), chunk * padded)
            bit = jnp.maximum(level - 1, 0)
            before = (other >= (span >> bit) << bit) & (other < span)
            before = before.astype(f32).astype(bf16)
            decay = dot(before, high) + dot(before, middle) + dot(before, low)
            has_bit = ((span >> bit) & 1)[:, :1] == 1
            decay_ref[head, out_rows, :] = jnp.where(has_bit, decay, NEVER)
            right = (other > span - (1 << bit)) & (other <= span)
            right = right.astype(f32).astype(bf16)
            merge_ref[head, out_rows, :] = jnp.exp(
                dot(right, high) + dot(right, middle) + dot(right, low)
            )
            return carry

        lax.fori_loop(0, spans // chunk, some_spans, 0)


def pick_set(step, starts, values):
    value = values[0]
    for start, other in zip(starts[1:], values[1:]):
        value = jnp.where(step >= start, other, value)
    return value


def pick(core, step, starts, pairs, local, group):
    half = group // CORES
    rows = slice(local % half * Q, (local % half + 1) * Q)
    mine = core == local // half
    return pick_set(step, starts, [jnp.where(mine, my_ref[rows, :], other_ref[rows, :]) for my_ref, other_ref in pairs])


def scaled(value, rows, width):
    parts = [value[head * width : (head + 1) * width] * row for head, row in enumerate(rows)]
    return jnp.concatenate(parts, axis=0) if len(parts) > 1 else parts[0]


def merge_blocks(left, right, merge_ref, row, width):
    return scaled(left, [merge_ref[head, row : row + 1, :] for head in range(merge_ref.shape[0])], width) + right


def states_kernel(heads, width, group, padded, starts, groups_ref, core_ref, x_ref, weight_ref, half_ref, merge_ref,
                  *refs):
    *key_refs, low_ref, total_ref = refs
    pairs = list(zip(key_refs[::2], key_refs[1::2]))
    kept = {}
    for local in range(group):
        columns = slice(local * Q, (local + 1) * Q)
        weights = [weight_ref[head, local : local + 1, :] for head in range(heads)]
        weighted = scaled(x_ref[:, columns].astype(f32), weights, width).astype(bf16)
        keys = pick(core_ref[0], pl.program_id(0), starts, pairs, local, group)
        first = dot(weighted[:, :HALF], keys[:HALF])
        low_ref[group + local] = first.astype(bf16)
        halves = [half_ref[head, local : local + 1, :] for head in range(heads)]
        state = scaled(first, halves, width) + dot(weighted[:, HALF:], keys[HALF:])
        bit = 0
        while local >> bit & 1:
            state = merge_blocks(kept[bit], state, merge_ref, local * padded + bit + 1, width)
            bit += 1
        kept[bit] = state
        low_ref[local] = state.astype(bf16)
    total_ref[...] = state


def tree_kernel(width, group, padded, groups_ref, merge_ref, *refs):
    *total_refs, high_ref, order_ref = refs
    steps = order_ref.shape[0]
    low_bits = group.bit_length() - 1
    at = 0
    for total_ref in total_refs:
        for slot in range(total_ref.shape[0]):
            order_ref[groups_ref[at]] = total_ref[slot]
            at += 1
    kept = {}
    for step in range(steps):
        state = order_ref[step]
        bit = 0
        while step >> bit & 1:
            row = step * padded + low_bits + bit + 1
            state = merge_blocks(kept[bit], state, merge_ref, row, width)
            bit += 1
        kept[bit] = state
        high_ref[step] = state.astype(bf16)


def outputs_kernel(heads, width, group, bits, padded, starts, groups_ref, core_ref, skip_ref, x_ref, high_ref,
                   cum_ref, offset_ref, decay_ref, level_ref, *refs):
    *set_refs, out_ref, query_ref, score_ref, sum_ref, factor_ref, own_ref, mixing_ref = refs
    set_refs = [set_refs[5 * at : 5 * at + 5] for at in range(len(starts))]
    key_pairs = [refs[0:2] for refs in set_refs]
    query_pairs = [refs[2:4] for refs in set_refs]
    low_refs = [refs[4] for refs in set_refs]
    at = pl.program_id(0)
    step = groups_ref[at]
    low_bits = group.bit_length() - 1
    levels = bits + 1
    causal = lax.broadcasted_iota(jnp.int32, (HALF, HALF), 0) <= lax.broadcasted_iota(
        jnp.int32, (HALF, HALF), 1
    )
    halves = slice(0, HALF), slice(HALF, Q)
    spans = [slice(local * Q, (local + 1) * Q) for local in range(group)]
    head_rows = [slice(head * width, (head + 1) * width) for head in range(heads)]
    high_slots = [
        jnp.maximum((step >> (bit - low_bits) << (bit - low_bits)) - 1, 0) for bit in range(low_bits, bits)
    ]
    offsets = [jnp.transpose(offset_ref[head]) for head in range(heads)]

    def low_state(slot):
        return pick_set(at, starts, [low_ref[slot] for low_ref in low_refs])

    for local, columns in enumerate(spans):
        query_ref[:, columns] = jnp.transpose(pick(core_ref[0], at, starts, query_pairs, local, group))
    right = lax.broadcasted_iota(jnp.int32, (1, Q), 1) >= HALF
    for local, columns in enumerate(spans):
        weights = level_ref[0, :, columns].astype(f32)
        for head in range(heads):
            cumulative = cum_ref[head, local : local + 1, :]
            weight = weights[head * levels : (head + 1) * levels]
            decay = decay_ref[head, local * padded : local * padded + levels, :]
            decay = jnp.concatenate([decay] * (Q // N), axis=1)
            factor_ref[head, :levels, columns] = weight * jnp.exp(cumulative + decay)
            own = cumulative + jnp.log(weight[:1])
            own_ref[head, :1, columns] = own
            across = jnp.exp(own - cumulative[:, HALF - 1 : HALF])
            factor_ref[head, :1, columns] = jnp.where(right, across, 0.0)

    for local, columns in enumerate(spans):
        keys = pick(core_ref[0], at, starts, key_pairs, local, group)
        active = [bit for bit in range(bits) if bit >= low_bits or local >> bit & 1]
        states = [low_state(group + local)]
        for bit in active:
            if bit < low_bits:
                states.append(low_state(((local >> bit) << bit) - 1))
            else:
                states.append(high_ref[high_slots[bit - low_bits]])
        result = dot(jnp.concatenate([keys] + states, axis=0), query_ref[:, columns])
        for half in halves:
            score_ref[local, half] = jnp.where(causal, result[half, half], 0.0)
        for head, rows in enumerate(head_rows):
            total = None
            for place, row in enumerate([0] + [bit + 1 for bit in active]):
                first_row = Q + place * heads * width + rows.start
                term = result[first_row : first_row + width] * factor_ref[head, row : row + 1, columns]
                total = term if total is None else total + term
            sum_ref[rows, columns] = total

    for local, columns in enumerate(spans):
        for head in range(heads):
            own = own_ref[head, :1, columns]
            column = offsets[head][:, local : local + 1]
            for half in halves:
                gaps = jnp.minimum(own[:, half] - column[half], 64.0)
                mixing_ref[local, head, half] = (score_ref[local, half] * jnp.exp(gaps)).astype(bf16)

    for local, columns in enumerate(spans):
        for head, rows in enumerate(head_rows):
            for half in halves:
                here = slice(columns.start + half.start, columns.start + half.stop)
                values = x_ref[rows, here]
                result = dot(values, mixing_ref[local, head, half]) + sum_ref[rows, here]
                out_ref[rows, here] = (result + skip_ref[head] * values.astype(f32)).astype(bf16)


def exchange(value, axis, distance):
    pairs = [(place, place ^ distance) for place in range(lax.axis_size(axis))]
    return lax.ppermute(value, axis, pairs)


def along_z(own):
    pieces = [own]
    for distance in range(1, lax.axis_size("z")):
        low = distance & -distance
        pieces.append(exchange(pieces[distance ^ low], "z", low))
    return pieces[1:]


def places():
    both = [(y, x) for y in range(lax.axis_size("y")) for x in range(lax.axis_size("x"))]
    return sorted(both, key=lambda place: ((place[0] > 0) + (place[1] > 0), place))


def straight(piece):
    near = {(0, 0): piece}
    for y, x in places():
        if (y > 0) != (x > 0):
            near[y, x] = exchange(piece, "x", x) if x else exchange(piece, "y", y)
    return near


def diagonal(near, by_x, by_y):
    far = {}
    for y, x in places():
        if y and x:
            parts = []
            if by_x is not None:
                parts.append(exchange(near[0, x][by_x], "y", y))
            if by_y is not None:
                parts.append(exchange(near[y, 0][by_y], "x", x))
            far[y, x] = parts
    return far


def join(parts):
    return jnp.concatenate(parts, axis=0) if len(parts) > 1 else parts[0]


def with_core(piece):
    return piece, exchange(piece, "core", 1)


def after(value, *others):
    return lax.optimization_barrier((value, *others))[0]


def on_device(x_heads, b_proj, c_proj, log_gate, step_size, level_weight, skip):
    rows, tokens = x_heads.shape
    head_count, tok_dev = log_gate.shape
    levels = level_weight.shape[1]
    bits = levels - 1
    shards = lax.axis_size(("z", "y"))
    span_rows = tok_dev // Q
    spans = tokens // Q
    heads = max(rows // P_SIZE, 1)
    width = rows // heads
    sharing = P_SIZE // width
    block = b_proj.shape[0]
    group = CORES * block // Q
    padded = -(-levels // 8) * 8
    steps = spans // group
    per_shard = span_rows // group

    def to_owners(value):
        value = jnp.repeat(value, sharing, axis=0) if sharing > 1 else value
        value = value.reshape((shards, heads) + value.shape[1:])
        return value.reshape((shards, -1) + value.shape[3:])

    first_head = lax.axis_index(("z", "y")) * rows // P_SIZE
    own_skip = lax.dynamic_slice_in_dim(skip, first_head, heads, 0)
    core = lax.axis_index("core").astype(jnp.int32).reshape(1)

    def group_ids(place, z=None):
        z = lax.axis_index("z") ^ jnp.arange(1, lax.axis_size("z")) if z is None else z
        y = lax.axis_index("y") ^ place[0]
        x = lax.axis_index("x") ^ place[1]
        return ((z * lax.axis_size("y") + y) * lax.axis_size("x") + x).astype(jnp.int32)

    params = pltpu.CompilerParams(vmem_limit_bytes=VMEM_LIMIT)
    key_near = straight(b_proj)
    key_line = along_z(b_proj)
    gates = jnp.stack(
        [log_gate.reshape(head_count, span_rows, Q), step_size.reshape(head_count, span_rows, Q)], axis=1
    )
    gates = lax.all_to_all(to_owners(gates), ("z", "y"), split_axis=0, concat_axis=0, tiled=True)
    query_near = straight(c_proj)
    crossed = [near[place] for near in (key_near, query_near) for place in places() if place in near and any(place)]
    everything = slice(None)
    key_near.update({place: join(parts) for place, parts in diagonal(key_near, everything, None).items()})
    query_near.update({place: join(parts) for place, parts in diagonal(query_near, None, everything).items()})
    query_line = along_z(after(c_proj, *key_line))
    keys_here = with_core(join([key_near[place] for place in places()]))

    params = pltpu.CompilerParams(vmem_limit_bytes=VMEM_LIMIT)
    weight, cumulative, offset, half, decay, merge = pl.pallas_call(
        functools.partial(gates_kernel, heads, levels, padded),
        out_shape=[jax.ShapeDtypeStruct((heads, spans, Q), f32)] * 3
        + [jax.ShapeDtypeStruct((heads, spans, N), f32)]
        + [jax.ShapeDtypeStruct((heads, spans * padded, N), f32)] * 2,
        scratch_shapes=[pltpu.VMEM((spans, N), f32)],
        compiler_params=params,
        name="gates",
    )(gates)
    weight, cumulative, offset = [v.reshape(heads, steps, group, Q) for v in (weight, cumulative, offset)]
    half = half.reshape(heads, steps, group, N)
    last_merge = merge.reshape(heads, steps, group * padded, N)[:, :, -padded:].reshape(heads, steps * padded, N)
    x_spec = pl.BlockSpec((rows, group * Q), lambda i, ids, *_: (0, ids[i]))
    span_spec = pl.BlockSpec((heads, None, group, Q), lambda i, ids, *_: (0, ids[i], 0, 0))
    level_spec = pl.BlockSpec((heads, group * padded, N), lambda i, ids, *_: (0, ids[i], 0))
    half_spec = pl.BlockSpec((heads, None, group, N), lambda i, ids, *_: (0, ids[i], 0, 0))
    low_slots = 2 * group
    vmem = pl.BlockSpec(memory_space=pltpu.VMEM)

    def within(start, count, base, trailing):
        return lambda i, *_: (jnp.clip(i - start, 0, count - 1) + base,) + (0,) * trailing

    def first_steps(id_lists):
        return [sum(ids.shape[0] for ids in id_lists[:at]) for at in range(len(id_lists))]

    totals, all_ids = [], []

    def states(sets):
        starts = first_steps([ids for ids, _ in sets])
        ids = join([ids for ids, _ in sets])
        count = ids.shape[0]
        key_specs = [
            pl.BlockSpec((block, N), within(start, own.shape[0], 0, 1)) for start, (own, _) in zip(starts, sets)
        ]
        low, total = pl.pallas_call(
            functools.partial(states_kernel, heads, width, group, padded, starts),
            grid_spec=pltpu.PrefetchScalarGridSpec(
                num_scalar_prefetch=2,
                grid=(count,),
                in_specs=[x_spec, span_spec, half_spec, level_spec] + [spec for spec in key_specs for _ in range(CORES)],
                out_specs=[
                    pl.BlockSpec((None, low_slots, rows, N), lambda i, *_: (i, 0, 0, 0)),
                    pl.BlockSpec((None, rows, N), lambda i, *_: (i, 0, 0)),
                ],
            ),
            out_shape=[
                jax.ShapeDtypeStruct((count, low_slots, rows, N), bf16),
                jax.ShapeDtypeStruct((count, rows, N), f32),
            ],
            compiler_params=params,
            cost_estimate=pl.CostEstimate(
                flops=2 * rows * count * group * Q * N,
                bytes_accessed=4 * count * group * Q * (rows + N),
                transcendentals=0,
            ),
            name="states",
        )(ids, core, x_heads, weight, half, merge, *[key for _, keys in sets for key in keys])
        totals.append(total)
        all_ids.append(ids)
        return [(low, start) for start in starts]

    def outputs(sets, out):
        starts = first_steps([ids for ids, *_ in sets])
        ids = join([ids for ids, *_ in sets])
        count = ids.shape[0]
        tokens_here = count * group * Q
        set_specs, operands = [], []
        for start, (own, keys, queries, (low, base)) in zip(starts, sets):
            set_specs += [pl.BlockSpec((block, N), within(start, own.shape[0], 0, 1))] * (2 * CORES)
            set_specs.append(pl.BlockSpec((None, low_slots, rows, N), within(start, own.shape[0], base, 3)))
            operands += [*keys, *queries, low]
        before = [] if out is None else [out]
        fixed = [
            pl.BlockSpec(memory_space=pltpu.SMEM),
            x_spec,
            vmem,
            span_spec,
            span_spec,
            level_spec,
            pl.BlockSpec(
                (1, heads * levels, group * Q),
                lambda i, ids, *_: (ids[i] // per_shard, 0, ids[i] % per_shard),
            ),
        ]

        def kernel(*refs):
            last = 2 + len(fixed) + len(set_specs)
            outputs_kernel(
                heads, width, group, bits, padded, starts, *refs[:last], *refs[last + len(before) :]
            )

        return pl.pallas_call(
            kernel,
            grid_spec=pltpu.PrefetchScalarGridSpec(
                num_scalar_prefetch=2,
                grid=(count,),
                in_specs=fixed + set_specs + [pl.BlockSpec(memory_space=pl.ANY)] * len(before),
                out_specs=x_spec,
                scratch_shapes=[
                    pltpu.VMEM((N, group * Q), bf16),
                    pltpu.VMEM((group, Q, HALF), f32),
                    pltpu.VMEM((rows, group * Q), f32),
                    pltpu.VMEM((heads, padded, group * Q), f32),
                    pltpu.VMEM((heads, 8, group * Q), f32),
                    pltpu.VMEM((group, heads, Q, HALF), bf16),
                ],
            ),
            out_shape=jax.ShapeDtypeStruct((rows, tokens), bf16),
            input_output_aliases={2 + len(fixed) + len(set_specs): 0} if before else {},
            compiler_params=params,
            cost_estimate=pl.CostEstimate(
                flops=2 * tokens_here * (Q * N + rows * Q + bits * rows * N),
                bytes_accessed=4 * tokens_here * (rows + N),
                transcendentals=heads * tokens_here * Q,
            ),
            name="outputs",
        )(ids, core, own_skip, x_heads, high, cumulative, offset, decay, level_rows, *operands, *before)

    here = join([group_ids(place, lax.axis_index("z").reshape(1)) for place in places()])
    one = (0, 0)
    sides = [place for place in places() if (place[0] > 0) != (place[1] > 0)]
    corners = [place for place in places() if place[0] and place[1]]
    far_ids = {place: group_ids(place) for place in places()}
    lows = {}
    if key_line:
        cut = block * ((len(key_line) + 1) // 3)
        by_x, by_y = slice(0, cut), slice(cut, None)
        key_far = straight(after(join(key_line), *crossed))
        keys_far = {one: with_core(key_far[one])}
        low_here, lows[one] = states([(here, keys_here), (far_ids[one], keys_far[one])])
        query_own = join(query_line)
        query_far = straight(after(query_own, *[key_far[place] for place in sides]))
        if sides:
            parts = diagonal(key_far, by_x, by_y)
            keys_far.update({place: with_core(key_far[place]) for place in sides})
            lows.update(zip(sides, states([(far_ids[place], keys_far[place]) for place in sides])))
            if corners:
                joined = {place: join([after(part, *totals[:2]) for part in parts[place]]) for place in corners}
                keys_far.update({place: with_core(joined[place]) for place in corners})
                lows.update(zip(corners, states([(far_ids[place], keys_far[place]) for place in corners])))
    else:
        (low_here,) = states([(here, keys_here)])

    level_rows = lax.all_to_all(
        to_owners(after(level_weight, weight).astype(bf16)), ("z", "y"), split_axis=0, concat_axis=0, tiled=True
    )
    queries_here = with_core(join([after(query_near[place], totals[0]) for place in places()]))
    if key_line:
        last_merge = after(last_merge, *[query_far[place] for place in sides])
    high = pl.pallas_call(
        functools.partial(tree_kernel, width, group, padded),
        grid_spec=pltpu.PrefetchScalarGridSpec(
            num_scalar_prefetch=1,
            in_specs=[vmem] * (1 + len(totals)),
            out_specs=vmem,
            scratch_shapes=[pltpu.VMEM((steps, rows, N), f32)],
        ),
        out_shape=jax.ShapeDtypeStruct((steps, rows, N), bf16),
        compiler_params=params,
        name="tree",
    )(join(all_ids), last_merge, *totals)

    out = outputs([(here, keys_here, queries_here, low_here)], None)
    if key_line:
        parts = diagonal(query_far, by_x, by_y)
        queries_far = {place: with_core(query_far[place]) for place in [one] + sides}

        def far_sets(some):
            return [(far_ids[place], keys_far[place], queries_far[place], lows[place]) for place in some]

        early = [one] + sides[: len(sides) // 2]
        late = sides[len(sides) // 2 :]
        for place in corners:
            queries_far[place] = with_core(join([after(part, out) for part in parts[place]]))
        out = outputs(far_sets(early), after(out, *[queries_far[place][0] for place in corners]))
        if late or corners:
            out = outputs(far_sets(late + corners), out)
    return out


def solution(mesh):
    x = mesh.shape["head"] // CORES
    y = math.gcd(mesh.shape["seq"], x)
    z = mesh.shape["seq"] // y
    split_mesh = jax.sharding.Mesh(mesh.devices.reshape(z, y, x, CORES), ("z", "y", "x", "core"))
    seq = ("z", "y")
    head = ("x", "core")
    in_specs = (
        P((*head, *seq), None),
        P((*seq, *head), None),
        P((*seq, *head), None),
        P(head, seq),
        P(head, seq),
        P(head, None, seq),
        P(head),
    )
    out_specs = P((*head, *seq), None)
    return jax.shard_map(
        on_device, mesh=split_mesh, in_specs=in_specs, out_specs=out_specs, check_vma=False
    )
```

```python
import functools
import math

import jax
import jax.numpy as jnp
from jax import lax
from jax.experimental import pallas as pl
from jax.experimental.pallas import tpu as pltpu
from jax.sharding import PartitionSpec as P

P_SIZE = 64
N = 128
Q = 256
HALF = Q // 2
CORES = 2
NEVER = -1e30
VMEM_LIMIT = 60 * 1024 * 1024

f32 = jnp.float32
bf16 = jnp.bfloat16


def dot(a, b):
    return lax.dot_general(a, b, (((1,), (0,)), ((), ())), preferred_element_type=f32)


def exact_parts(value):
    high = value.astype(bf16)
    rest = value - high.astype(f32)
    middle = rest.astype(bf16)
    low = (rest - middle.astype(f32)).astype(bf16)
    return high, middle, low


def gates_kernel(heads, levels, padded, gates_ref, weight_ref, cum_ref, offset_ref, half_ref, decay_ref,
                 merge_ref, log_scratch):
    shards, _, span_rows, _ = gates_ref.shape
    spans = shards * span_rows
    upper = (
        lax.broadcasted_iota(jnp.int32, (Q, Q), 0) <= lax.broadcasted_iota(jnp.int32, (Q, Q), 1)
    ).astype(f32).astype(bf16)
    chunk = min(spans, 64)
    for head in range(heads):
        for shard in range(shards):
            rows = pl.ds(shard * span_rows, span_rows)
            gate = gates_ref[shard, 2 * head]
            step = gates_ref[shard, 2 * head + 1]
            high, middle, low = exact_parts(gate)
            cumulative = dot(high, upper) + dot(middle, upper) + dot(low, upper)
            span_log = cumulative[:, Q - 1 :]
            cum_ref[head, rows, :] = cumulative
            offset_ref[head, rows, :] = cumulative - jnp.log(step)
            half_log = cumulative[:, HALF - 1 : HALF]
            weight_ref[head, rows, :HALF] = jnp.exp(half_log - cumulative[:, :HALF]) * step[:, :HALF]
            weight_ref[head, rows, HALF:] = jnp.exp(span_log - cumulative[:, HALF:]) * step[:, HALF:]
            half_ref[head, rows, :] = jnp.broadcast_to(jnp.exp(span_log - half_log), (span_rows, N))
            log_scratch[rows, :] = jnp.broadcast_to(span_log, (span_rows, N))
        high, middle, low = exact_parts(log_scratch[...])

        def some_spans(at, carry):
            first = at * chunk
            size = (chunk * padded, spans)
            row = lax.broadcasted_iota(jnp.int32, size, 0)
            span = first + row // padded
            level = row % padded
            other = lax.broadcasted_iota(jnp.int32, size, 1)
            out_rows = pl.ds(pl.multiple_of(first * padded, chunk * padded), chunk * padded)
            bit = jnp.maximum(level - 1, 0)
            before = (other >= (span >> bit) << bit) & (other < span)
            before = before.astype(f32).astype(bf16)
            decay = dot(before, high) + dot(before, middle) + dot(before, low)
            has_bit = ((span >> bit) & 1)[:, :1] == 1
            decay_ref[head, out_rows, :] = jnp.where(has_bit, decay, NEVER)
            right = (other > span - (1 << bit)) & (other <= span)
            right = right.astype(f32).astype(bf16)
            merge_ref[head, out_rows, :] = jnp.exp(
                dot(right, high) + dot(right, middle) + dot(right, low)
            )
            return carry

        lax.fori_loop(0, spans // chunk, some_spans, 0)


def pick_set(step, starts, values):
    value = values[0]
    for start, other in zip(starts[1:], values[1:]):
        value = jnp.where(step >= start, other, value)
    return value


def pick(core, step, starts, pairs, local, group):
    half = group // CORES
    rows = slice(local % half * Q, (local % half + 1) * Q)
    mine = core == local // half
    return pick_set(step, starts, [jnp.where(mine, my_ref[rows, :], other_ref[rows, :]) for my_ref, other_ref in pairs])


def scaled(value, rows, width):
    parts = [value[head * width : (head + 1) * width] * row for head, row in enumerate(rows)]
    return jnp.concatenate(parts, axis=0) if len(parts) > 1 else parts[0]


def merge_blocks(left, right, merge_ref, row, width):
    return scaled(left, [merge_ref[head, row : row + 1, :] for head in range(merge_ref.shape[0])], width) + right


def states_kernel(heads, width, group, padded, starts, groups_ref, core_ref, x_ref, weight_ref, half_ref, merge_ref,
                  *refs):
    *key_refs, low_ref, total_ref = refs
    pairs = list(zip(key_refs[::2], key_refs[1::2]))
    kept = {}
    for local in range(group):
        columns = slice(local * Q, (local + 1) * Q)
        weights = [weight_ref[head, local : local + 1, :] for head in range(heads)]
        weighted = scaled(x_ref[:, columns].astype(f32), weights, width).astype(bf16)
        keys = pick(core_ref[0], pl.program_id(0), starts, pairs, local, group)
        first = dot(weighted[:, :HALF], keys[:HALF])
        low_ref[group + local] = first.astype(bf16)
        halves = [half_ref[head, local : local + 1, :] for head in range(heads)]
        state = scaled(first, halves, width) + dot(weighted[:, HALF:], keys[HALF:])
        bit = 0
        while local >> bit & 1:
            state = merge_blocks(kept[bit], state, merge_ref, local * padded + bit + 1, width)
            bit += 1
        kept[bit] = state
        low_ref[local] = state.astype(bf16)
    total_ref[...] = state


def tree_kernel(width, group, padded, groups_ref, merge_ref, *refs):
    *total_refs, high_ref, order_ref = refs
    steps = order_ref.shape[0]
    low_bits = group.bit_length() - 1
    at = 0
    for total_ref in total_refs:
        for slot in range(total_ref.shape[0]):
            order_ref[groups_ref[at]] = total_ref[slot]
            at += 1
    kept = {}
    for step in range(steps):
        state = order_ref[step]
        bit = 0
        while step >> bit & 1:
            row = step * padded + low_bits + bit + 1
            state = merge_blocks(kept[bit], state, merge_ref, row, width)
            bit += 1
        kept[bit] = state
        high_ref[step] = state.astype(bf16)


def outputs_kernel(heads, width, group, bits, padded, starts, groups_ref, core_ref, skip_ref, x_ref, high_ref,
                   cum_ref, offset_ref, decay_ref, level_ref, *refs):
    *set_refs, out_ref, query_ref, score_ref, sum_ref, factor_ref, own_ref, mixing_ref = refs
    set_refs = [set_refs[5 * at : 5 * at + 5] for at in range(len(starts))]
    key_pairs = [refs[0:2] for refs in set_refs]
    query_pairs = [refs[2:4] for refs in set_refs]
    low_refs = [refs[4] for refs in set_refs]
    at = pl.program_id(0)
    step = groups_ref[at]
    low_bits = group.bit_length() - 1
    levels = bits + 1
    causal = lax.broadcasted_iota(jnp.int32, (HALF, HALF), 0) <= lax.broadcasted_iota(
        jnp.int32, (HALF, HALF), 1
    )
    halves = slice(0, HALF), slice(HALF, Q)
    spans = [slice(local * Q, (local + 1) * Q) for local in range(group)]
    head_rows = [slice(head * width, (head + 1) * width) for head in range(heads)]
    high_slots = [
        jnp.maximum((step >> (bit - low_bits) << (bit - low_bits)) - 1, 0) for bit in range(low_bits, bits)
    ]
    offsets = [jnp.transpose(offset_ref[head]) for head in range(heads)]

    def low_state(slot):
        return pick_set(at, starts, [low_ref[slot] for low_ref in low_refs])

    for local, columns in enumerate(spans):
        query_ref[:, columns] = jnp.transpose(pick(core_ref[0], at, starts, query_pairs, local, group))
    right = lax.broadcasted_iota(jnp.int32, (1, Q), 1) >= HALF
    for local, columns in enumerate(spans):
        weights = level_ref[0, :, columns].astype(f32)
        for head in range(heads):
            cumulative = cum_ref[head, local : local + 1, :]
            weight = weights[head * levels : (head + 1) * levels]
            decay = decay_ref[head, local * padded : local * padded + levels, :]
            decay = jnp.concatenate([decay] * (Q // N), axis=1)
            factor_ref[head, :levels, columns] = weight * jnp.exp(cumulative + decay)
            own = cumulative + jnp.log(weight[:1])
            own_ref[head, :1, columns] = own
            across = jnp.exp(own - cumulative[:, HALF - 1 : HALF])
            factor_ref[head, :1, columns] = jnp.where(right, across, 0.0)

    for local, columns in enumerate(spans):
        keys = pick(core_ref[0], at, starts, key_pairs, local, group)
        active = [bit for bit in range(bits) if bit >= low_bits or local >> bit & 1]
        states = [low_state(group + local)]
        for bit in active:
            if bit < low_bits:
                states.append(low_state(((local >> bit) << bit) - 1))
            else:
                states.append(high_ref[high_slots[bit - low_bits]])
        result = dot(jnp.concatenate([keys] + states, axis=0), query_ref[:, columns])
        for half in halves:
            score_ref[local, half] = jnp.where(causal, result[half, half], 0.0)
        for head, rows in enumerate(head_rows):
            total = None
            for place, row in enumerate([0] + [bit + 1 for bit in active]):
                first_row = Q + place * heads * width + rows.start
                term = result[first_row : first_row + width] * factor_ref[head, row : row + 1, columns]
                total = term if total is None else total + term
            sum_ref[rows, columns] = total

    for local, columns in enumerate(spans):
        for head in range(heads):
            own = own_ref[head, :1, columns]
            column = offsets[head][:, local : local + 1]
            for half in halves:
                gaps = jnp.minimum(own[:, half] - column[half], 64.0)
                mixing_ref[local, head, half] = (score_ref[local, half] * jnp.exp(gaps)).astype(bf16)

    for local, columns in enumerate(spans):
        for head, rows in enumerate(head_rows):
            for half in halves:
                here = slice(columns.start + half.start, columns.start + half.stop)
                values = x_ref[rows, here]
                result = dot(values, mixing_ref[local, head, half]) + sum_ref[rows, here]
                out_ref[rows, here] = (result + skip_ref[head] * values.astype(f32)).astype(bf16)


def exchange(value, axis, distance):
    pairs = [(place, place ^ distance) for place in range(lax.axis_size(axis))]
    return lax.ppermute(value, axis, pairs)


def along_z(own):
    pieces = [own]
    for distance in range(1, lax.axis_size("z")):
        low = distance & -distance
        pieces.append(exchange(pieces[distance ^ low], "z", low))
    return pieces[1:]


def places():
    both = [(y, x) for y in range(lax.axis_size("y")) for x in range(lax.axis_size("x"))]
    return sorted(both, key=lambda place: ((place[0] > 0) + (place[1] > 0), place))


def straight(piece):
    near = {(0, 0): piece}
    for y, x in places():
        if (y > 0) != (x > 0):
            near[y, x] = exchange(piece, "x", x) if x else exchange(piece, "y", y)
    return near


def diagonal(near, by_x, by_y, cuts=None):
    far = {}
    cuts = [] if cuts is None else cuts
    for y, x in places():
        if y and x:
            parts = []
            if by_x is not None:
                cuts.append(near[0, x][by_x])
                parts.append(exchange(cuts[-1], "y", y))
            if by_y is not None:
                cuts.append(near[y, 0][by_y])
                parts.append(exchange(cuts[-1], "x", x))
            far[y, x] = parts
    return far


def join(parts):
    return jnp.concatenate(parts, axis=0) if len(parts) > 1 else parts[0]


def with_core(piece):
    return piece, exchange(piece, "core", 1)


def after(value, *others):
    return lax.optimization_barrier((value, *others))[0]


def on_device(x_heads, b_proj, c_proj, log_gate, step_size, level_weight, skip):
    rows, tokens = x_heads.shape
    head_count, tok_dev = log_gate.shape
    levels = level_weight.shape[1]
    bits = levels - 1
    shards = lax.axis_size(("z", "y"))
    span_rows = tok_dev // Q
    spans = tokens // Q
    heads = max(rows // P_SIZE, 1)
    width = rows // heads
    sharing = P_SIZE // width
    block = b_proj.shape[0]
    group = CORES * block // Q
    padded = -(-levels // 8) * 8
    steps = spans // group
    per_shard = span_rows // group

    def to_owners(value):
        value = jnp.repeat(value, sharing, axis=0) if sharing > 1 else value
        value = value.reshape((shards, heads) + value.shape[1:])
        return value.reshape((shards, -1) + value.shape[3:])

    first_head = lax.axis_index(("z", "y")) * rows // P_SIZE
    own_skip = lax.dynamic_slice_in_dim(skip, first_head, heads, 0)
    core = lax.axis_index("core").astype(jnp.int32).reshape(1)

    def group_ids(place, z=None):
        z = lax.axis_index("z") ^ jnp.arange(1, lax.axis_size("z")) if z is None else z
        y = lax.axis_index("y") ^ place[0]
        x = lax.axis_index("x") ^ place[1]
        return ((z * lax.axis_size("y") + y) * lax.axis_size("x") + x).astype(jnp.int32)

    params = pltpu.CompilerParams(vmem_limit_bytes=VMEM_LIMIT)
    key_near = straight(b_proj)
    key_line = along_z(b_proj)
    gates = jnp.stack(
        [log_gate.reshape(head_count, span_rows, Q), step_size.reshape(head_count, span_rows, Q)], axis=1
    )
    gates = lax.all_to_all(to_owners(gates), ("z", "y"), split_axis=0, concat_axis=0, tiled=True)
    query_near = straight(c_proj)
    crossed = [near[place] for near in (key_near, query_near) for place in places() if place in near and any(place)]
    everything = slice(None)
    key_near.update({place: join(parts) for place, parts in diagonal(key_near, everything, None).items()})
    query_near.update({place: join(parts) for place, parts in diagonal(query_near, None, everything).items()})
    keys_here = with_core(join([key_near[place] for place in places()]))

    params = pltpu.CompilerParams(vmem_limit_bytes=VMEM_LIMIT)
    weight, cumulative, offset, half, decay, merge = pl.pallas_call(
        functools.partial(gates_kernel, heads, levels, padded),
        out_shape=[jax.ShapeDtypeStruct((heads, spans, Q), f32)] * 3
        + [jax.ShapeDtypeStruct((heads, spans, N), f32)]
        + [jax.ShapeDtypeStruct((heads, spans * padded, N), f32)] * 2,
        scratch_shapes=[pltpu.VMEM((spans, N), f32)],
        compiler_params=params,
        name="gates",
    )(gates)
    weight, cumulative, offset = [v.reshape(heads, steps, group, Q) for v in (weight, cumulative, offset)]
    half = half.reshape(heads, steps, group, N)
    last_merge = merge.reshape(heads, steps, group * padded, N)[:, :, -padded:].reshape(heads, steps * padded, N)
    x_spec = pl.BlockSpec((rows, group * Q), lambda i, ids, *_: (0, ids[i]))
    span_spec = pl.BlockSpec((heads, None, group, Q), lambda i, ids, *_: (0, ids[i], 0, 0))
    level_spec = pl.BlockSpec((heads, group * padded, N), lambda i, ids, *_: (0, ids[i], 0))
    half_spec = pl.BlockSpec((heads, None, group, N), lambda i, ids, *_: (0, ids[i], 0, 0))
    low_slots = 2 * group
    vmem = pl.BlockSpec(memory_space=pltpu.VMEM)

    def within(start, count, base, trailing):
        return lambda i, *_: (jnp.clip(i - start, 0, count - 1) + base,) + (0,) * trailing

    def first_steps(id_lists):
        return [sum(ids.shape[0] for ids in id_lists[:at]) for at in range(len(id_lists))]

    totals, all_ids = [], []

    def states(sets):
        starts = first_steps([ids for ids, _ in sets])
        ids = join([ids for ids, _ in sets])
        count = ids.shape[0]
        key_specs = [
            pl.BlockSpec((block, N), within(start, own.shape[0], 0, 1)) for start, (own, _) in zip(starts, sets)
        ]
        low, total = pl.pallas_call(
            functools.partial(states_kernel, heads, width, group, padded, starts),
            grid_spec=pltpu.PrefetchScalarGridSpec(
                num_scalar_prefetch=2,
                grid=(count,),
                in_specs=[x_spec, span_spec, half_spec, level_spec] + [spec for spec in key_specs for _ in range(CORES)],
                out_specs=[
                    pl.BlockSpec((None, low_slots, rows, N), lambda i, *_: (i, 0, 0, 0)),
                    pl.BlockSpec((None, rows, N), lambda i, *_: (i, 0, 0)),
                ],
            ),
            out_shape=[
                jax.ShapeDtypeStruct((count, low_slots, rows, N), bf16),
                jax.ShapeDtypeStruct((count, rows, N), f32),
            ],
            compiler_params=params,
            cost_estimate=pl.CostEstimate(
                flops=2 * rows * count * group * Q * N,
                bytes_accessed=4 * count * group * Q * (rows + N),
                transcendentals=0,
            ),
            name="states",
        )(ids, core, x_heads, weight, half, merge, *[key for _, keys in sets for key in keys])
        totals.append(total)
        all_ids.append(ids)
        return [(low, start) for start in starts]

    def outputs(sets, out):
        starts = first_steps([ids for ids, *_ in sets])
        ids = join([ids for ids, *_ in sets])
        count = ids.shape[0]
        tokens_here = count * group * Q
        set_specs, operands = [], []
        for start, (own, keys, queries, (low, base)) in zip(starts, sets):
            set_specs += [pl.BlockSpec((block, N), within(start, own.shape[0], 0, 1))] * (2 * CORES)
            set_specs.append(pl.BlockSpec((None, low_slots, rows, N), within(start, own.shape[0], base, 3)))
            operands += [*keys, *queries, low]
        before = [] if out is None else [out]
        fixed = [
            pl.BlockSpec(memory_space=pltpu.SMEM),
            x_spec,
            vmem,
            span_spec,
            span_spec,
            level_spec,
            pl.BlockSpec(
                (1, heads * levels, group * Q),
                lambda i, ids, *_: (ids[i] // per_shard, 0, ids[i] % per_shard),
            ),
        ]

        def kernel(*refs):
            last = 2 + len(fixed) + len(set_specs)
            outputs_kernel(
                heads, width, group, bits, padded, starts, *refs[:last], *refs[last + len(before) :]
            )

        return pl.pallas_call(
            kernel,
            grid_spec=pltpu.PrefetchScalarGridSpec(
                num_scalar_prefetch=2,
                grid=(count,),
                in_specs=fixed + set_specs + [pl.BlockSpec(memory_space=pl.ANY)] * len(before),
                out_specs=x_spec,
                scratch_shapes=[
                    pltpu.VMEM((N, group * Q), bf16),
                    pltpu.VMEM((group, Q, HALF), f32),
                    pltpu.VMEM((rows, group * Q), f32),
                    pltpu.VMEM((heads, padded, group * Q), f32),
                    pltpu.VMEM((heads, 8, group * Q), f32),
                    pltpu.VMEM((group, heads, Q, HALF), bf16),
                ],
            ),
            out_shape=jax.ShapeDtypeStruct((rows, tokens), bf16),
            input_output_aliases={2 + len(fixed) + len(set_specs): 0} if before else {},
            compiler_params=params,
            cost_estimate=pl.CostEstimate(
                flops=2 * tokens_here * (Q * N + rows * Q + bits * rows * N),
                bytes_accessed=4 * tokens_here * (rows + N),
                transcendentals=heads * tokens_here * Q,
            ),
            name="outputs",
        )(ids, core, own_skip, x_heads, high, cumulative, offset, decay, level_rows, *operands, *before)

    here = join([group_ids(place, lax.axis_index("z").reshape(1)) for place in places()])
    one = (0, 0)
    sides = [place for place in places() if (place[0] > 0) != (place[1] > 0)]
    corners = [place for place in places() if place[0] and place[1]]
    far_ids = {place: group_ids(place) for place in places()}
    lows, cuts = {}, []
    if key_line:
        cut = block * ((len(key_line) + 1) // 3)
        by_x, by_y = slice(0, cut), slice(cut, None)
        key_far = straight(after(join(key_line), *crossed))
        keys_far = {one: with_core(key_far[one])}
        begun = [key_far[one]]
        low_here, lows[one] = states([(here, keys_here), (far_ids[one], keys_far[one])])
        query_line = along_z(after(c_proj, weight))
        if sides:
            tied = {place: after(key_far[place], totals[0]) for place in sides}
            parts = diagonal(tied, by_x, by_y, cuts)
            begun = [tied[place] for place in sides]
            keys_far.update({place: with_core(key_far[place]) for place in sides})
            lows.update(zip(sides, states([(far_ids[place], keys_far[place]) for place in sides])))
            if corners:
                joined = {place: join([after(part, *totals[:2]) for part in parts[place]]) for place in corners}
                begun = [joined[place] for place in corners]
                keys_far.update({place: with_core(joined[place]) for place in corners})
                lows.update(zip(corners, states([(far_ids[place], keys_far[place]) for place in corners])))
        query_far = straight(after(join(query_line), *begun))
    else:
        (low_here,) = states([(here, keys_here)])
    level_rows = lax.all_to_all(
        to_owners(after(level_weight, totals[0], *cuts).astype(bf16)), ("z", "y"), split_axis=0, concat_axis=0, tiled=True
    )
    queries_here = with_core(join([after(query_near[place], totals[0]) for place in places()]))

    high = pl.pallas_call(
        functools.partial(tree_kernel, width, group, padded),
        grid_spec=pltpu.PrefetchScalarGridSpec(
            num_scalar_prefetch=1,
            in_specs=[vmem] * (1 + len(totals)),
            out_specs=vmem,
            scratch_shapes=[pltpu.VMEM((steps, rows, N), f32)],
        ),
        out_shape=jax.ShapeDtypeStruct((steps, rows, N), bf16),
        compiler_params=params,
        name="tree",
    )(join(all_ids), last_merge, *totals)

    out = outputs([(here, keys_here, queries_here, low_here)], None)
    if key_line:
        tied = {place: after(query_far[place], out) for place in sides}
        parts = diagonal(tied, by_x, by_y)
        queries_far = {place: with_core(query_far[place] if place == one else tied[place]) for place in [one] + sides}
        for place in places():
            if sides and place == sides[-1]:
                for corner in corners:
                    queries_far[corner] = with_core(join([after(part, out) for part in parts[corner]]))
                out = after(out, *[queries_far[corner][0] for corner in corners])
            out = outputs([(far_ids[place], keys_far[place], queries_far[place], lows[place])], out)
    return out


def solution(mesh):
    x = mesh.shape["head"] // CORES
    y = math.gcd(mesh.shape["seq"], x)
    z = mesh.shape["seq"] // y
    split_mesh = jax.sharding.Mesh(mesh.devices.reshape(z, y, x, CORES), ("z", "y", "x", "core"))
    seq = ("z", "y")
    head = ("x", "core")
    in_specs = (
        P((*head, *seq), None),
        P((*seq, *head), None),
        P((*seq, *head), None),
        P(head, seq),
        P(head, seq),
        P(head, None, seq),
        P(head),
    )
    out_specs = P((*head, *seq), None)
    return jax.shard_map(
        on_device, mesh=split_mesh, in_specs=in_specs, out_specs=out_specs, check_vma=False
    )
```

```python
import functools
import math

import jax
import jax.numpy as jnp
from jax import lax
from jax.experimental import pallas as pl
from jax.experimental.pallas import tpu as pltpu
from jax.sharding import PartitionSpec as P

P_SIZE = 64
N = 128
Q = 256
HALF = Q // 2
CORES = 2
NEVER = -1e30
VMEM_LIMIT = 60 * 1024 * 1024

f32 = jnp.float32
bf16 = jnp.bfloat16


def dot(a, b):
    return lax.dot_general(a, b, (((1,), (0,)), ((), ())), preferred_element_type=f32)


def exact_parts(value):
    high = value.astype(bf16)
    rest = value - high.astype(f32)
    middle = rest.astype(bf16)
    low = (rest - middle.astype(f32)).astype(bf16)
    return high, middle, low


def gates_kernel(heads, levels, padded, gates_ref, weight_ref, cum_ref, offset_ref, half_ref, decay_ref,
                 merge_ref, log_scratch):
    shards, _, span_rows, _ = gates_ref.shape
    spans = shards * span_rows
    upper = (
        lax.broadcasted_iota(jnp.int32, (Q, Q), 0) <= lax.broadcasted_iota(jnp.int32, (Q, Q), 1)
    ).astype(f32).astype(bf16)
    chunk = min(spans, 64)
    for head in range(heads):
        for shard in range(shards):
            rows = pl.ds(shard * span_rows, span_rows)
            gate = gates_ref[shard, 2 * head]
            step = gates_ref[shard, 2 * head + 1]
            high, middle, low = exact_parts(gate)
            cumulative = dot(high, upper) + dot(middle, upper) + dot(low, upper)
            span_log = cumulative[:, Q - 1 :]
            cum_ref[head, rows, :] = cumulative
            offset_ref[head, rows, :] = cumulative - jnp.log(step)
            half_log = cumulative[:, HALF - 1 : HALF]
            weight_ref[head, rows, :HALF] = jnp.exp(half_log - cumulative[:, :HALF]) * step[:, :HALF]
            weight_ref[head, rows, HALF:] = jnp.exp(span_log - cumulative[:, HALF:]) * step[:, HALF:]
            half_ref[head, rows, :] = jnp.broadcast_to(jnp.exp(span_log - half_log), (span_rows, N))
            log_scratch[rows, :] = jnp.broadcast_to(span_log, (span_rows, N))
        high, middle, low = exact_parts(log_scratch[...])

        def some_spans(at, carry):
            first = at * chunk
            size = (chunk * padded, spans)
            row = lax.broadcasted_iota(jnp.int32, size, 0)
            span = first + row // padded
            level = row % padded
            other = lax.broadcasted_iota(jnp.int32, size, 1)
            out_rows = pl.ds(pl.multiple_of(first * padded, chunk * padded), chunk * padded)
            bit = jnp.maximum(level - 1, 0)
            before = (other >= (span >> bit) << bit) & (other < span)
            before = before.astype(f32).astype(bf16)
            decay = dot(before, high) + dot(before, middle) + dot(before, low)
            has_bit = ((span >> bit) & 1)[:, :1] == 1
            decay_ref[head, out_rows, :] = jnp.where(has_bit, decay, NEVER)
            right = (other > span - (1 << bit)) & (other <= span)
            right = right.astype(f32).astype(bf16)
            merge_ref[head, out_rows, :] = jnp.exp(
                dot(right, high) + dot(right, middle) + dot(right, low)
            )
            return carry

        lax.fori_loop(0, spans // chunk, some_spans, 0)


def pick_set(step, starts, values):
    value = values[0]
    for start, other in zip(starts[1:], values[1:]):
        value = jnp.where(step >= start, other, value)
    return value


def pick(core, step, starts, pairs, local, group):
    half = group // CORES
    rows = slice(local % half * Q, (local % half + 1) * Q)
    mine = core == local // half
    return pick_set(step, starts, [jnp.where(mine, my_ref[rows, :], other_ref[rows, :]) for my_ref, other_ref in pairs])


def scaled(value, rows, width):
    parts = [value[head * width : (head + 1) * width] * row for head, row in enumerate(rows)]
    return jnp.concatenate(parts, axis=0) if len(parts) > 1 else parts[0]


def merge_blocks(left, right, merge_ref, row, width):
    return scaled(left, [merge_ref[head, row : row + 1, :] for head in range(merge_ref.shape[0])], width) + right


def states_kernel(heads, width, group, padded, starts, groups_ref, core_ref, x_ref, weight_ref, half_ref, merge_ref,
                  *refs):
    *key_refs, low_ref, total_ref = refs
    pairs = list(zip(key_refs[::2], key_refs[1::2]))
    kept = {}
    for local in range(group):
        columns = slice(local * Q, (local + 1) * Q)
        weights = [weight_ref[head, local : local + 1, :] for head in range(heads)]
        weighted = scaled(x_ref[:, columns].astype(f32), weights, width).astype(bf16)
        keys = pick(core_ref[0], pl.program_id(0), starts, pairs, local, group)
        first = dot(weighted[:, :HALF], keys[:HALF])
        low_ref[group + local] = first.astype(bf16)
        halves = [half_ref[head, local : local + 1, :] for head in range(heads)]
        state = scaled(first, halves, width) + dot(weighted[:, HALF:], keys[HALF:])
        bit = 0
        while local >> bit & 1:
            state = merge_blocks(kept[bit], state, merge_ref, local * padded + bit + 1, width)
            bit += 1
        kept[bit] = state
        low_ref[local] = state.astype(bf16)
    total_ref[...] = state


def tree_kernel(width, group, padded, groups_ref, merge_ref, *refs):
    *total_refs, high_ref, order_ref = refs
    steps = order_ref.shape[0]
    low_bits = group.bit_length() - 1
    at = 0
    for total_ref in total_refs:
        for slot in range(total_ref.shape[0]):
            order_ref[groups_ref[at]] = total_ref[slot]
            at += 1
    kept = {}
    for step in range(steps):
        state = order_ref[step]
        bit = 0
        while step >> bit & 1:
            row = step * padded + low_bits + bit + 1
            state = merge_blocks(kept[bit], state, merge_ref, row, width)
            bit += 1
        kept[bit] = state
        high_ref[step] = state.astype(bf16)


def outputs_kernel(heads, width, group, bits, padded, starts, groups_ref, core_ref, skip_ref, x_ref, high_ref,
                   cum_ref, offset_ref, decay_ref, level_ref, *refs):
    *set_refs, out_ref, query_ref, score_ref, sum_ref, factor_ref, own_ref, mixing_ref = refs
    set_refs = [set_refs[5 * at : 5 * at + 5] for at in range(len(starts))]
    key_pairs = [refs[0:2] for refs in set_refs]
    query_pairs = [refs[2:4] for refs in set_refs]
    low_refs = [refs[4] for refs in set_refs]
    at = pl.program_id(0)
    step = groups_ref[at]
    low_bits = group.bit_length() - 1
    levels = bits + 1
    causal = lax.broadcasted_iota(jnp.int32, (HALF, HALF), 0) <= lax.broadcasted_iota(
        jnp.int32, (HALF, HALF), 1
    )
    halves = slice(0, HALF), slice(HALF, Q)
    spans = [slice(local * Q, (local + 1) * Q) for local in range(group)]
    head_rows = [slice(head * width, (head + 1) * width) for head in range(heads)]
    high_slots = [
        jnp.maximum((step >> (bit - low_bits) << (bit - low_bits)) - 1, 0) for bit in range(low_bits, bits)
    ]
    offsets = [jnp.transpose(offset_ref[head]) for head in range(heads)]

    def low_state(slot):
        return pick_set(at, starts, [low_ref[slot] for low_ref in low_refs])

    for local, columns in enumerate(spans):
        query_ref[:, columns] = jnp.transpose(pick(core_ref[0], at, starts, query_pairs, local, group))
    right = lax.broadcasted_iota(jnp.int32, (1, Q), 1) >= HALF
    for local, columns in enumerate(spans):
        weights = level_ref[0, :, columns].astype(f32)
        for head in range(heads):
            cumulative = cum_ref[head, local : local + 1, :]
            weight = weights[head * levels : (head + 1) * levels]
            decay = decay_ref[head, local * padded : local * padded + levels, :]
            decay = jnp.concatenate([decay] * (Q // N), axis=1)
            factor_ref[head, :levels, columns] = weight * jnp.exp(cumulative + decay)
            own = cumulative + jnp.log(weight[:1])
            own_ref[head, :1, columns] = own
            across = jnp.exp(own - cumulative[:, HALF - 1 : HALF])
            factor_ref[head, :1, columns] = jnp.where(right, across, 0.0)

    for local, columns in enumerate(spans):
        keys = pick(core_ref[0], at, starts, key_pairs, local, group)
        active = [bit for bit in range(bits) if bit >= low_bits or local >> bit & 1]
        states = [low_state(group + local)]
        for bit in active:
            if bit < low_bits:
                states.append(low_state(((local >> bit) << bit) - 1))
            else:
                states.append(high_ref[high_slots[bit - low_bits]])
        result = dot(jnp.concatenate([keys] + states, axis=0), query_ref[:, columns])
        for half in halves:
            score_ref[local, half] = jnp.where(causal, result[half, half], 0.0)
        for head, rows in enumerate(head_rows):
            total = None
            for place, row in enumerate([0] + [bit + 1 for bit in active]):
                first_row = Q + place * heads * width + rows.start
                term = result[first_row : first_row + width] * factor_ref[head, row : row + 1, columns]
                total = term if total is None else total + term
            sum_ref[rows, columns] = total

    for local, columns in enumerate(spans):
        for head in range(heads):
            own = own_ref[head, :1, columns]
            column = offsets[head][:, local : local + 1]
            for half in halves:
                gaps = jnp.minimum(own[:, half] - column[half], 64.0)
                mixing_ref[local, head, half] = (score_ref[local, half] * jnp.exp(gaps)).astype(bf16)

    for local, columns in enumerate(spans):
        for head, rows in enumerate(head_rows):
            for half in halves:
                here = slice(columns.start + half.start, columns.start + half.stop)
                values = x_ref[rows, here]
                result = dot(values, mixing_ref[local, head, half]) + sum_ref[rows, here]
                out_ref[rows, here] = (result + skip_ref[head] * values.astype(f32)).astype(bf16)


def exchange(value, axis, distance):
    pairs = [(place, place ^ distance) for place in range(lax.axis_size(axis))]
    return lax.ppermute(value, axis, pairs)


def along_z(own):
    pieces = [own]
    for distance in range(1, lax.axis_size("z")):
        low = distance & -distance
        pieces.append(exchange(pieces[distance ^ low], "z", low))
    return pieces[1:]


def along_z_at_once(own):
    return [exchange(own, "z", distance) for distance in range(1, lax.axis_size("z"))]


def places():
    both = [(y, x) for y in range(lax.axis_size("y")) for x in range(lax.axis_size("x"))]
    return sorted(both, key=lambda place: ((place[0] > 0) + (place[1] > 0), place))


def straight(piece):
    near = {(0, 0): piece}
    for y, x in places():
        if (y > 0) != (x > 0):
            near[y, x] = exchange(piece, "x", x) if x else exchange(piece, "y", y)
    return near


def diagonal(near, by_x, by_y):
    far = {}
    for y, x in places():
        if y and x:
            parts = []
            if by_x is not None:
                parts.append(exchange(near[0, x][by_x], "y", y))
            if by_y is not None:
                parts.append(exchange(near[y, 0][by_y], "x", x))
            far[y, x] = parts
    return far


def join(parts):
    return jnp.concatenate(parts, axis=0) if len(parts) > 1 else parts[0]


def with_core(piece):
    return piece, exchange(piece, "core", 1)


def after(value, *others):
    return lax.optimization_barrier((value, *others))[0]


def on_device(x_heads, b_proj, c_proj, log_gate, step_size, level_weight, skip):
    rows, tokens = x_heads.shape
    head_count, tok_dev = log_gate.shape
    levels = level_weight.shape[1]
    bits = levels - 1
    shards = lax.axis_size(("z", "y"))
    span_rows = tok_dev // Q
    spans = tokens // Q
    heads = max(rows // P_SIZE, 1)
    width = rows // heads
    sharing = P_SIZE // width
    block = b_proj.shape[0]
    group = CORES * block // Q
    padded = -(-levels // 8) * 8
    steps = spans // group
    per_shard = span_rows // group

    def to_owners(value):
        value = jnp.repeat(value, sharing, axis=0) if sharing > 1 else value
        value = value.reshape((shards, heads) + value.shape[1:])
        return value.reshape((shards, -1) + value.shape[3:])

    first_head = lax.axis_index(("z", "y")) * rows // P_SIZE
    own_skip = lax.dynamic_slice_in_dim(skip, first_head, heads, 0)
    core = lax.axis_index("core").astype(jnp.int32).reshape(1)

    def group_ids(place, z=None):
        z = lax.axis_index("z") ^ jnp.arange(1, lax.axis_size("z")) if z is None else z
        y = lax.axis_index("y") ^ place[0]
        x = lax.axis_index("x") ^ place[1]
        return ((z * lax.axis_size("y") + y) * lax.axis_size("x") + x).astype(jnp.int32)

    params = pltpu.CompilerParams(vmem_limit_bytes=VMEM_LIMIT)
    key_near = straight(b_proj)
    key_line = along_z(b_proj)
    gates = jnp.stack(
        [log_gate.reshape(head_count, span_rows, Q), step_size.reshape(head_count, span_rows, Q)], axis=1
    )
    gates = lax.all_to_all(to_owners(gates), ("z", "y"), split_axis=0, concat_axis=0, tiled=True)
    query_near = straight(c_proj)
    crossed = [near[place] for near in (key_near, query_near) for place in places() if place in near and any(place)]
    everything = slice(None)
    key_near.update({place: join(parts) for place, parts in diagonal(key_near, everything, None).items()})
    query_near.update({place: join(parts) for place, parts in diagonal(query_near, None, everything).items()})
    keys_here = with_core(join([key_near[place] for place in places()]))

    params = pltpu.CompilerParams(vmem_limit_bytes=VMEM_LIMIT)
    weight, cumulative, offset, half, decay, merge = pl.pallas_call(
        functools.partial(gates_kernel, heads, levels, padded),
        out_shape=[jax.ShapeDtypeStruct((heads, spans, Q), f32)] * 3
        + [jax.ShapeDtypeStruct((heads, spans, N), f32)]
        + [jax.ShapeDtypeStruct((heads, spans * padded, N), f32)] * 2,
        scratch_shapes=[pltpu.VMEM((spans, N), f32)],
        compiler_params=params,
        name="gates",
    )(gates)
    weight, cumulative, offset = [v.reshape(heads, steps, group, Q) for v in (weight, cumulative, offset)]
    half = half.reshape(heads, steps, group, N)
    last_merge = merge.reshape(heads, steps, group * padded, N)[:, :, -padded:].reshape(heads, steps * padded, N)
    level_rows = lax.all_to_all(
        to_owners(level_weight.astype(bf16)), ("z", "y"), split_axis=0, concat_axis=0, tiled=True
    )

    x_spec = pl.BlockSpec((rows, group * Q), lambda i, ids, *_: (0, ids[i]))
    span_spec = pl.BlockSpec((heads, None, group, Q), lambda i, ids, *_: (0, ids[i], 0, 0))
    level_spec = pl.BlockSpec((heads, group * padded, N), lambda i, ids, *_: (0, ids[i], 0))
    half_spec = pl.BlockSpec((heads, None, group, N), lambda i, ids, *_: (0, ids[i], 0, 0))
    low_slots = 2 * group
    vmem = pl.BlockSpec(memory_space=pltpu.VMEM)

    def within(start, count, base, trailing):
        return lambda i, *_: (jnp.clip(i - start, 0, count - 1) + base,) + (0,) * trailing

    def first_steps(id_lists):
        return [sum(ids.shape[0] for ids in id_lists[:at]) for at in range(len(id_lists))]

    totals, all_ids = [], []

    def states(sets, *needs):
        starts = first_steps([ids for ids, _ in sets])
        ids = join([ids for ids, _ in sets])
        count = ids.shape[0]
        key_specs = [
            pl.BlockSpec((block, N), within(start, own.shape[0], 0, 1)) for start, (own, _) in zip(starts, sets)
        ]
        low, total = pl.pallas_call(
            functools.partial(states_kernel, heads, width, group, padded, starts),
            grid_spec=pltpu.PrefetchScalarGridSpec(
                num_scalar_prefetch=2,
                grid=(count,),
                in_specs=[x_spec, span_spec, half_spec, level_spec] + [spec for spec in key_specs for _ in range(CORES)],
                out_specs=[
                    pl.BlockSpec((None, low_slots, rows, N), lambda i, *_: (i, 0, 0, 0)),
                    pl.BlockSpec((None, rows, N), lambda i, *_: (i, 0, 0)),
                ],
            ),
            out_shape=[
                jax.ShapeDtypeStruct((count, low_slots, rows, N), bf16),
                jax.ShapeDtypeStruct((count, rows, N), f32),
            ],
            compiler_params=params,
            cost_estimate=pl.CostEstimate(
                flops=2 * rows * count * group * Q * N,
                bytes_accessed=4 * count * group * Q * (rows + N),
                transcendentals=0,
            ),
            name="states",
        )(ids, core, x_heads, after(weight, *needs), half, merge, *[key for _, keys in sets for key in keys])
        totals.append(total)
        all_ids.append(ids)
        return [(low, start) for start in starts]

    def outputs(sets, out):
        starts = first_steps([ids for ids, *_ in sets])
        ids = join([ids for ids, *_ in sets])
        count = ids.shape[0]
        tokens_here = count * group * Q
        set_specs, operands = [], []
        for start, (own, keys, queries, (low, base)) in zip(starts, sets):
            set_specs += [pl.BlockSpec((block, N), within(start, own.shape[0], 0, 1))] * (2 * CORES)
            set_specs.append(pl.BlockSpec((None, low_slots, rows, N), within(start, own.shape[0], base, 3)))
            operands += [*keys, *queries, low]
        before = [] if out is None else [out]
        fixed = [
            pl.BlockSpec(memory_space=pltpu.SMEM),
            x_spec,
            vmem,
            span_spec,
            span_spec,
            level_spec,
            pl.BlockSpec(
                (1, heads * levels, group * Q),
                lambda i, ids, *_: (ids[i] // per_shard, 0, ids[i] % per_shard),
            ),
        ]

        def kernel(*refs):
            last = 2 + len(fixed) + len(set_specs)
            outputs_kernel(
                heads, width, group, bits, padded, starts, *refs[:last], *refs[last + len(before) :]
            )

        return pl.pallas_call(
            kernel,
            grid_spec=pltpu.PrefetchScalarGridSpec(
                num_scalar_prefetch=2,
                grid=(count,),
                in_specs=fixed + set_specs + [pl.BlockSpec(memory_space=pl.ANY)] * len(before),
                out_specs=x_spec,
                scratch_shapes=[
                    pltpu.VMEM((N, group * Q), bf16),
                    pltpu.VMEM((group, Q, HALF), f32),
                    pltpu.VMEM((rows, group * Q), f32),
                    pltpu.VMEM((heads, padded, group * Q), f32),
                    pltpu.VMEM((heads, 8, group * Q), f32),
                    pltpu.VMEM((group, heads, Q, HALF), bf16),
                ],
            ),
            out_shape=jax.ShapeDtypeStruct((rows, tokens), bf16),
            input_output_aliases={2 + len(fixed) + len(set_specs): 0} if before else {},
            compiler_params=params,
            cost_estimate=pl.CostEstimate(
                flops=2 * tokens_here * (Q * N + rows * Q + bits * rows * N),
                bytes_accessed=4 * tokens_here * (rows + N),
                transcendentals=heads * tokens_here * Q,
            ),
            name="outputs",
        )(ids, core, own_skip, x_heads, high, cumulative, offset, decay, level_rows, *operands, *before)

    here = join([group_ids(place, lax.axis_index("z").reshape(1)) for place in places()])
    one = (0, 0)
    sides = [place for place in places() if (place[0] > 0) != (place[1] > 0)]
    corners = [place for place in places() if place[0] and place[1]]
    far_ids = {place: group_ids(place) for place in places()}
    lows = {}
    if key_line:
        cut = block * ((len(key_line) + 1) // 3)
        by_x, by_y = slice(0, cut), slice(cut, None)
        key_far = straight(after(join(key_line), *crossed))
        keys_far = {one: with_core(key_far[one])}
        low_here, lows[one] = states([(here, keys_here), (far_ids[one], keys_far[one])])
        query_line = along_z_at_once(after(c_proj, *key_line))
        if sides:
            tied = {place: after(key_far[place], totals[0]) for place in sides}
            parts = diagonal(tied, by_x, by_y)
            keys_far.update({place: with_core(key_far[place]) for place in sides})
            lows.update(zip(sides, states([(far_ids[place], keys_far[place]) for place in sides], level_rows)))
            if corners:
                joined = {place: join([after(part, *totals[:2]) for part in parts[place]]) for place in corners}
                keys_far.update({place: with_core(joined[place]) for place in corners})
                lows.update(zip(corners, states([(far_ids[place], keys_far[place]) for place in corners])))
        query_far = straight(join([after(piece, *totals) for piece in query_line]))
    else:
        (low_here,) = states([(here, keys_here)])
    queries_here = with_core(join([after(query_near[place], totals[0]) for place in places()]))

    high = pl.pallas_call(
        functools.partial(tree_kernel, width, group, padded),
        grid_spec=pltpu.PrefetchScalarGridSpec(
            num_scalar_prefetch=1,
            in_specs=[vmem] * (1 + len(totals)),
            out_specs=vmem,
            scratch_shapes=[pltpu.VMEM((steps, rows, N), f32)],
        ),
        out_shape=jax.ShapeDtypeStruct((steps, rows, N), bf16),
        compiler_params=params,
        name="tree",
    )(join(all_ids), last_merge, *totals)

    out = outputs([(here, keys_here, queries_here, low_here)], None)
    if key_line:
        tied = {place: after(query_far[place], out) for place in sides}
        parts = diagonal(tied, by_x, by_y)
        queries_far = {place: with_core(query_far[place] if place == one else tied[place]) for place in [one] + sides}
        for place in places():
            if sides and place == sides[-1]:
                for corner in corners:
                    queries_far[corner] = with_core(join([after(part, out) for part in parts[corner]]))
                out = after(out, *[queries_far[corner][0] for corner in corners])
            out = outputs([(far_ids[place], keys_far[place], queries_far[place], lows[place])], out)
    return out


def solution(mesh):
    x = mesh.shape["head"] // CORES
    y = math.gcd(mesh.shape["seq"], x)
    z = mesh.shape["seq"] // y
    split_mesh = jax.sharding.Mesh(mesh.devices.reshape(z, y, x, CORES), ("z", "y", "x", "core"))
    seq = ("z", "y")
    head = ("x", "core")
    in_specs = (
        P((*head, *seq), None),
        P((*seq, *head), None),
        P((*seq, *head), None),
        P(head, seq),
        P(head, seq),
        P(head, None, seq),
        P(head),
    )
    out_specs = P((*head, *seq), None)
    return jax.shard_map(
        on_device, mesh=split_mesh, in_specs=in_specs, out_specs=out_specs, check_vma=False
    )
```

```python
import functools
import math

import jax
import jax.numpy as jnp
from jax import lax
from jax.experimental import pallas as pl
from jax.experimental.pallas import tpu as pltpu
from jax.sharding import PartitionSpec as P

P_SIZE = 64
N = 128
Q = 256
HALF = Q // 2
CORES = 2
NEVER = -1e30
VMEM_LIMIT = 60 * 1024 * 1024

f32 = jnp.float32
bf16 = jnp.bfloat16


def dot(a, b):
    return lax.dot_general(a, b, (((1,), (0,)), ((), ())), preferred_element_type=f32)


def exact_parts(value):
    high = value.astype(bf16)
    rest = value - high.astype(f32)
    middle = rest.astype(bf16)
    low = (rest - middle.astype(f32)).astype(bf16)
    return high, middle, low


def gates_kernel(heads, levels, padded, gates_ref, weight_ref, cum_ref, offset_ref, half_ref, decay_ref,
                 merge_ref, log_scratch):
    shards, _, span_rows, _ = gates_ref.shape
    spans = shards * span_rows
    upper = (
        lax.broadcasted_iota(jnp.int32, (Q, Q), 0) <= lax.broadcasted_iota(jnp.int32, (Q, Q), 1)
    ).astype(f32).astype(bf16)
    chunk = min(spans, 64)
    for head in range(heads):
        for shard in range(shards):
            rows = pl.ds(shard * span_rows, span_rows)
            gate = gates_ref[shard, 2 * head]
            step = gates_ref[shard, 2 * head + 1]
            high, middle, low = exact_parts(gate)
            cumulative = dot(high, upper) + dot(middle, upper) + dot(low, upper)
            span_log = cumulative[:, Q - 1 :]
            cum_ref[head, rows, :] = cumulative
            offset_ref[head, rows, :] = cumulative - jnp.log(step)
            half_log = cumulative[:, HALF - 1 : HALF]
            weight_ref[head, rows, :HALF] = jnp.exp(half_log - cumulative[:, :HALF]) * step[:, :HALF]
            weight_ref[head, rows, HALF:] = jnp.exp(span_log - cumulative[:, HALF:]) * step[:, HALF:]
            half_ref[head, rows, :] = jnp.broadcast_to(jnp.exp(span_log - half_log), (span_rows, N))
            log_scratch[rows, :] = jnp.broadcast_to(span_log, (span_rows, N))
        high, middle, low = exact_parts(log_scratch[...])

        def some_spans(at, carry):
            first = at * chunk
            size = (chunk * padded, spans)
            row = lax.broadcasted_iota(jnp.int32, size, 0)
            span = first + row // padded
            level = row % padded
            other = lax.broadcasted_iota(jnp.int32, size, 1)
            out_rows = pl.ds(pl.multiple_of(first * padded, chunk * padded), chunk * padded)
            bit = jnp.maximum(level - 1, 0)
            before = (other >= (span >> bit) << bit) & (other < span)
            before = before.astype(f32).astype(bf16)
            decay = dot(before, high) + dot(before, middle) + dot(before, low)
            has_bit = ((span >> bit) & 1)[:, :1] == 1
            decay_ref[head, out_rows, :] = jnp.where(has_bit, decay, NEVER)
            right = (other > span - (1 << bit)) & (other <= span)
            right = right.astype(f32).astype(bf16)
            merge_ref[head, out_rows, :] = jnp.exp(
                dot(right, high) + dot(right, middle) + dot(right, low)
            )
            return carry

        lax.fori_loop(0, spans // chunk, some_spans, 0)


def pick_set(step, starts, values):
    value = values[0]
    for start, other in zip(starts[1:], values[1:]):
        value = jnp.where(step >= start, other, value)
    return value


def pick(core, step, starts, pairs, local, group):
    half = group // CORES
    rows = slice(local % half * Q, (local % half + 1) * Q)
    mine = core == local // half
    return pick_set(step, starts, [jnp.where(mine, my_ref[rows, :], other_ref[rows, :]) for my_ref, other_ref in pairs])


def scaled(value, rows, width):
    parts = [value[head * width : (head + 1) * width] * row for head, row in enumerate(rows)]
    return jnp.concatenate(parts, axis=0) if len(parts) > 1 else parts[0]


def merge_blocks(left, right, merge_ref, row, width):
    return scaled(left, [merge_ref[head, row : row + 1, :] for head in range(merge_ref.shape[0])], width) + right


def states_kernel(heads, width, group, padded, starts, groups_ref, core_ref, x_ref, weight_ref, half_ref, merge_ref,
                  *refs):
    *key_refs, low_ref, total_ref = refs
    pairs = list(zip(key_refs[::2], key_refs[1::2]))
    kept = {}
    for local in range(group):
        columns = slice(local * Q, (local + 1) * Q)
        weights = [weight_ref[head, local : local + 1, :] for head in range(heads)]
        weighted = scaled(x_ref[:, columns].astype(f32), weights, width).astype(bf16)
        keys = pick(core_ref[0], pl.program_id(0), starts, pairs, local, group)
        first = dot(weighted[:, :HALF], keys[:HALF])
        low_ref[group + local] = first.astype(bf16)
        halves = [half_ref[head, local : local + 1, :] for head in range(heads)]
        state = scaled(first, halves, width) + dot(weighted[:, HALF:], keys[HALF:])
        bit = 0
        while local >> bit & 1:
            state = merge_blocks(kept[bit], state, merge_ref, local * padded + bit + 1, width)
            bit += 1
        kept[bit] = state
        low_ref[local] = state.astype(bf16)
    total_ref[...] = state


def tree_kernel(width, group, padded, groups_ref, merge_ref, *refs):
    *total_refs, high_ref, order_ref = refs
    steps = order_ref.shape[0]
    low_bits = group.bit_length() - 1
    at = 0
    for total_ref in total_refs:
        for slot in range(total_ref.shape[0]):
            order_ref[groups_ref[at]] = total_ref[slot]
            at += 1
    kept = {}
    for step in range(steps):
        state = order_ref[step]
        bit = 0
        while step >> bit & 1:
            row = step * padded + low_bits + bit + 1
            state = merge_blocks(kept[bit], state, merge_ref, row, width)
            bit += 1
        kept[bit] = state
        high_ref[step] = state.astype(bf16)


def outputs_kernel(heads, width, group, bits, padded, starts, groups_ref, core_ref, skip_ref, x_ref, high_ref,
                   cum_ref, offset_ref, decay_ref, level_ref, *refs):
    *set_refs, out_ref, query_ref, score_ref, sum_ref, factor_ref, own_ref, mixing_ref = refs
    set_refs = [set_refs[5 * at : 5 * at + 5] for at in range(len(starts))]
    key_pairs = [refs[0:2] for refs in set_refs]
    query_pairs = [refs[2:4] for refs in set_refs]
    low_refs = [refs[4] for refs in set_refs]
    at = pl.program_id(0)
    step = groups_ref[at]
    low_bits = group.bit_length() - 1
    levels = bits + 1
    causal = lax.broadcasted_iota(jnp.int32, (HALF, HALF), 0) <= lax.broadcasted_iota(
        jnp.int32, (HALF, HALF), 1
    )
    halves = slice(0, HALF), slice(HALF, Q)
    spans = [slice(local * Q, (local + 1) * Q) for local in range(group)]
    head_rows = [slice(head * width, (head + 1) * width) for head in range(heads)]
    high_slots = [
        jnp.maximum((step >> (bit - low_bits) << (bit - low_bits)) - 1, 0) for bit in range(low_bits, bits)
    ]
    offsets = [jnp.transpose(offset_ref[head]) for head in range(heads)]

    def low_state(slot):
        return pick_set(at, starts, [low_ref[slot] for low_ref in low_refs])

    for local, columns in enumerate(spans):
        query_ref[:, columns] = jnp.transpose(pick(core_ref[0], at, starts, query_pairs, local, group))
    right = lax.broadcasted_iota(jnp.int32, (1, Q), 1) >= HALF
    for local, columns in enumerate(spans):
        weights = level_ref[0, :, columns].astype(f32)
        for head in range(heads):
            cumulative = cum_ref[head, local : local + 1, :]
            weight = weights[head * levels : (head + 1) * levels]
            decay = decay_ref[head, local * padded : local * padded + levels, :]
            decay = jnp.concatenate([decay] * (Q // N), axis=1)
            factor_ref[head, :levels, columns] = weight * jnp.exp(cumulative + decay)
            own = cumulative + jnp.log(weight[:1])
            own_ref[head, :1, columns] = own
            across = jnp.exp(own - cumulative[:, HALF - 1 : HALF])
            factor_ref[head, :1, columns] = jnp.where(right, across, 0.0)

    for local, columns in enumerate(spans):
        keys = pick(core_ref[0], at, starts, key_pairs, local, group)
        active = [bit for bit in range(bits) if bit >= low_bits or local >> bit & 1]
        states = [low_state(group + local)]
        for bit in active:
            if bit < low_bits:
                states.append(low_state(((local >> bit) << bit) - 1))
            else:
                states.append(high_ref[high_slots[bit - low_bits]])
        result = dot(jnp.concatenate([keys] + states, axis=0), query_ref[:, columns])
        for half in halves:
            score_ref[local, half] = jnp.where(causal, result[half, half], 0.0)
        for head, rows in enumerate(head_rows):
            total = None
            for place, row in enumerate([0] + [bit + 1 for bit in active]):
                first_row = Q + place * heads * width + rows.start
                term = result[first_row : first_row + width] * factor_ref[head, row : row + 1, columns]
                total = term if total is None else total + term
            sum_ref[rows, columns] = total

    for local, columns in enumerate(spans):
        for head in range(heads):
            own = own_ref[head, :1, columns]
            column = offsets[head][:, local : local + 1]
            for half in halves:
                gaps = jnp.minimum(own[:, half] - column[half], 64.0)
                mixing_ref[local, head, half] = (score_ref[local, half] * jnp.exp(gaps)).astype(bf16)

    for local, columns in enumerate(spans):
        for head, rows in enumerate(head_rows):
            for half in halves:
                here = slice(columns.start + half.start, columns.start + half.stop)
                values = x_ref[rows, here]
                result = dot(values, mixing_ref[local, head, half]) + sum_ref[rows, here]
                out_ref[rows, here] = (result + skip_ref[head] * values.astype(f32)).astype(bf16)


def exchange(value, axis, distance):
    pairs = [(place, place ^ distance) for place in range(lax.axis_size(axis))]
    return lax.ppermute(value, axis, pairs)


def along_z(own):
    pieces = [own]
    for distance in range(1, lax.axis_size("z")):
        low = distance & -distance
        pieces.append(exchange(pieces[distance ^ low], "z", low))
    return pieces[1:]


def places():
    both = [(y, x) for y in range(lax.axis_size("y")) for x in range(lax.axis_size("x"))]
    return sorted(both, key=lambda place: ((place[0] > 0) + (place[1] > 0), place))


def straight(piece):
    near = {(0, 0): piece}
    for y, x in places():
        if (y > 0) != (x > 0):
            near[y, x] = exchange(piece, "x", x) if x else exchange(piece, "y", y)
    return near


def diagonal(near, by_x, by_y):
    far = {}
    for y, x in places():
        if y and x:
            parts = []
            if by_x is not None:
                parts.append(exchange(near[0, x][by_x], "y", y))
            if by_y is not None:
                parts.append(exchange(near[y, 0][by_y], "x", x))
            far[y, x] = parts
    return far


def join(parts):
    return jnp.concatenate(parts, axis=0) if len(parts) > 1 else parts[0]


def with_core(piece):
    return piece, exchange(piece, "core", 1)


def after(value, *others):
    return lax.optimization_barrier((value, *others))[0]


def on_device(x_heads, b_proj, c_proj, log_gate, step_size, level_weight, skip):
    rows, tokens = x_heads.shape
    head_count, tok_dev = log_gate.shape
    levels = level_weight.shape[1]
    bits = levels - 1
    shards = lax.axis_size(("z", "y"))
    span_rows = tok_dev // Q
    spans = tokens // Q
    heads = max(rows // P_SIZE, 1)
    width = rows // heads
    sharing = P_SIZE // width
    block = b_proj.shape[0]
    group = CORES * block // Q
    padded = -(-levels // 8) * 8
    steps = spans // group
    per_shard = span_rows // group

    def to_owners(value):
        value = jnp.repeat(value, sharing, axis=0) if sharing > 1 else value
        value = value.reshape((shards, heads) + value.shape[1:])
        return value.reshape((shards, -1) + value.shape[3:])

    first_head = lax.axis_index(("z", "y")) * rows // P_SIZE
    own_skip = lax.dynamic_slice_in_dim(skip, first_head, heads, 0)
    core = lax.axis_index("core").astype(jnp.int32).reshape(1)

    def group_ids(place, z=None):
        z = lax.axis_index("z") ^ jnp.arange(1, lax.axis_size("z")) if z is None else z
        y = lax.axis_index("y") ^ place[0]
        x = lax.axis_index("x") ^ place[1]
        return ((z * lax.axis_size("y") + y) * lax.axis_size("x") + x).astype(jnp.int32)

    params = pltpu.CompilerParams(vmem_limit_bytes=VMEM_LIMIT)
    key_near = straight(b_proj)
    key_line = along_z(b_proj)
    gates = jnp.stack(
        [log_gate.reshape(head_count, span_rows, Q), step_size.reshape(head_count, span_rows, Q)], axis=1
    )
    gates = lax.all_to_all(to_owners(gates), ("z", "y"), split_axis=0, concat_axis=0, tiled=True)
    query_near = straight(c_proj)
    query_line = along_z(after(c_proj, *key_line))
    crossed = [near[place] for near in (key_near, query_near) for place in places() if place in near and any(place)]
    everything = slice(None)
    key_near.update({place: join(parts) for place, parts in diagonal(key_near, everything, None).items()})
    query_near.update({place: join(parts) for place, parts in diagonal(query_near, None, everything).items()})
    keys_here = with_core(join([key_near[place] for place in places()]))

    params = pltpu.CompilerParams(vmem_limit_bytes=VMEM_LIMIT)
    weight, cumulative, offset, half, decay, merge = pl.pallas_call(
        functools.partial(gates_kernel, heads, levels, padded),
        out_shape=[jax.ShapeDtypeStruct((heads, spans, Q), f32)] * 3
        + [jax.ShapeDtypeStruct((heads, spans, N), f32)]
        + [jax.ShapeDtypeStruct((heads, spans * padded, N), f32)] * 2,
        scratch_shapes=[pltpu.VMEM((spans, N), f32)],
        compiler_params=params,
        name="gates",
    )(gates)
    weight, cumulative, offset = [v.reshape(heads, steps, group, Q) for v in (weight, cumulative, offset)]
    half = half.reshape(heads, steps, group, N)
    last_merge = merge.reshape(heads, steps, group * padded, N)[:, :, -padded:].reshape(heads, steps * padded, N)
    x_spec = pl.BlockSpec((rows, group * Q), lambda i, ids, *_: (0, ids[i]))
    span_spec = pl.BlockSpec((heads, None, group, Q), lambda i, ids, *_: (0, ids[i], 0, 0))
    level_spec = pl.BlockSpec((heads, group * padded, N), lambda i, ids, *_: (0, ids[i], 0))
    half_spec = pl.BlockSpec((heads, None, group, N), lambda i, ids, *_: (0, ids[i], 0, 0))
    low_slots = 2 * group
    vmem = pl.BlockSpec(memory_space=pltpu.VMEM)

    def within(start, count, base, trailing):
        return lambda i, *_: (jnp.clip(i - start, 0, count - 1) + base,) + (0,) * trailing

    def first_steps(id_lists):
        return [sum(ids.shape[0] for ids in id_lists[:at]) for at in range(len(id_lists))]

    totals, all_ids = [], []

    def states(sets):
        starts = first_steps([ids for ids, _ in sets])
        ids = join([ids for ids, _ in sets])
        count = ids.shape[0]
        key_specs = [
            pl.BlockSpec((block, N), within(start, own.shape[0], 0, 1)) for start, (own, _) in zip(starts, sets)
        ]
        low, total = pl.pallas_call(
            functools.partial(states_kernel, heads, width, group, padded, starts),
            grid_spec=pltpu.PrefetchScalarGridSpec(
                num_scalar_prefetch=2,
                grid=(count,),
                in_specs=[x_spec, span_spec, half_spec, level_spec] + [spec for spec in key_specs for _ in range(CORES)],
                out_specs=[
                    pl.BlockSpec((None, low_slots, rows, N), lambda i, *_: (i, 0, 0, 0)),
                    pl.BlockSpec((None, rows, N), lambda i, *_: (i, 0, 0)),
                ],
            ),
            out_shape=[
                jax.ShapeDtypeStruct((count, low_slots, rows, N), bf16),
                jax.ShapeDtypeStruct((count, rows, N), f32),
            ],
            compiler_params=params,
            cost_estimate=pl.CostEstimate(
                flops=2 * rows * count * group * Q * N,
                bytes_accessed=4 * count * group * Q * (rows + N),
                transcendentals=0,
            ),
            name="states",
        )(ids, core, x_heads, weight, half, merge, *[key for _, keys in sets for key in keys])
        totals.append(total)
        all_ids.append(ids)
        return [(low, start) for start in starts]

    def outputs(sets, out):
        starts = first_steps([ids for ids, *_ in sets])
        ids = join([ids for ids, *_ in sets])
        count = ids.shape[0]
        tokens_here = count * group * Q
        set_specs, operands = [], []
        for start, (own, keys, queries, (low, base)) in zip(starts, sets):
            set_specs += [pl.BlockSpec((block, N), within(start, own.shape[0], 0, 1))] * (2 * CORES)
            set_specs.append(pl.BlockSpec((None, low_slots, rows, N), within(start, own.shape[0], base, 3)))
            operands += [*keys, *queries, low]
        before = [] if out is None else [out]
        fixed = [
            pl.BlockSpec(memory_space=pltpu.SMEM),
            x_spec,
            vmem,
            span_spec,
            span_spec,
            level_spec,
            pl.BlockSpec(
                (1, heads * levels, group * Q),
                lambda i, ids, *_: (ids[i] // per_shard, 0, ids[i] % per_shard),
            ),
        ]

        def kernel(*refs):
            last = 2 + len(fixed) + len(set_specs)
            outputs_kernel(
                heads, width, group, bits, padded, starts, *refs[:last], *refs[last + len(before) :]
            )

        return pl.pallas_call(
            kernel,
            grid_spec=pltpu.PrefetchScalarGridSpec(
                num_scalar_prefetch=2,
                grid=(count,),
                in_specs=fixed + set_specs + [pl.BlockSpec(memory_space=pl.ANY)] * len(before),
                out_specs=x_spec,
                scratch_shapes=[
                    pltpu.VMEM((N, group * Q), bf16),
                    pltpu.VMEM((group, Q, HALF), f32),
                    pltpu.VMEM((rows, group * Q), f32),
                    pltpu.VMEM((heads, padded, group * Q), f32),
                    pltpu.VMEM((heads, 8, group * Q), f32),
                    pltpu.VMEM((group, heads, Q, HALF), bf16),
                ],
            ),
            out_shape=jax.ShapeDtypeStruct((rows, tokens), bf16),
            input_output_aliases={2 + len(fixed) + len(set_specs): 0} if before else {},
            compiler_params=params,
            cost_estimate=pl.CostEstimate(
                flops=2 * tokens_here * (Q * N + rows * Q + bits * rows * N),
                bytes_accessed=4 * tokens_here * (rows + N),
                transcendentals=heads * tokens_here * Q,
            ),
            name="outputs",
        )(ids, core, own_skip, x_heads, high, cumulative, offset, decay, level_rows, *operands, *before)

    here = join([group_ids(place, lax.axis_index("z").reshape(1)) for place in places()])
    one = (0, 0)
    sides = [place for place in places() if (place[0] > 0) != (place[1] > 0)]
    corners = [place for place in places() if place[0] and place[1]]
    far_ids = {place: group_ids(place) for place in places()}
    lows = {}
    if key_line:
        cut = block * ((len(key_line) + 1) // 3)
        by_x, by_y = slice(0, cut), slice(cut, None)
        key_far = straight(after(join(key_line), *crossed))
        keys_far = {one: with_core(key_far[one])}
        begun = [key_far[one]]
        low_here, lows[one] = states([(here, keys_here), (far_ids[one], keys_far[one])])
        if sides:
            tied = {place: after(key_far[place], totals[0]) for place in sides}
            parts = diagonal(tied, by_x, by_y)
            begun = [tied[place] for place in sides]
            keys_far.update({place: with_core(key_far[place]) for place in sides})
            lows.update(zip(sides, states([(far_ids[place], keys_far[place]) for place in sides])))
            if corners:
                joined = {place: join([after(part, *totals[:2]) for part in parts[place]]) for place in corners}
                begun = [joined[place] for place in corners]
                keys_far.update({place: with_core(joined[place]) for place in corners})
                lows.update(zip(corners, states([(far_ids[place], keys_far[place]) for place in corners])))
        query_far = straight(after(join(query_line), *begun))
    else:
        (low_here,) = states([(here, keys_here)])
    level_rows = lax.all_to_all(
        to_owners(after(level_weight, *totals[:2]).astype(bf16)), ("z", "y"), split_axis=0, concat_axis=0, tiled=True
    )
    queries_here = with_core(join([after(query_near[place], totals[0]) for place in places()]))

    high = pl.pallas_call(
        functools.partial(tree_kernel, width, group, padded),
        grid_spec=pltpu.PrefetchScalarGridSpec(
            num_scalar_prefetch=1,
            in_specs=[vmem] * (1 + len(totals)),
            out_specs=vmem,
            scratch_shapes=[pltpu.VMEM((steps, rows, N), f32)],
        ),
        out_shape=jax.ShapeDtypeStruct((steps, rows, N), bf16),
        compiler_params=params,
        name="tree",
    )(join(all_ids), last_merge, *totals)

    out = outputs([(here, keys_here, queries_here, low_here)], None)
    if key_line:
        tied = {place: after(query_far[place], out) for place in sides}
        parts = diagonal(tied, by_x, by_y)
        queries_far = {place: with_core(query_far[place] if place == one else tied[place]) for place in [one] + sides}
        for place in places():
            if sides and place == sides[-1]:
                for corner in corners:
                    queries_far[corner] = with_core(join([after(part, out) for part in parts[corner]]))
                out = after(out, *[queries_far[corner][0] for corner in corners])
            out = outputs([(far_ids[place], keys_far[place], queries_far[place], lows[place])], out)
    return out


def solution(mesh):
    x = mesh.shape["head"] // CORES
    y = math.gcd(mesh.shape["seq"], x)
    z = mesh.shape["seq"] // y
    split_mesh = jax.sharding.Mesh(mesh.devices.reshape(z, y, x, CORES), ("z", "y", "x", "core"))
    seq = ("z", "y")
    head = ("x", "core")
    in_specs = (
        P((*head, *seq), None),
        P((*seq, *head), None),
        P((*seq, *head), None),
        P(head, seq),
        P(head, seq),
        P(head, None, seq),
        P(head),
    )
    out_specs = P((*head, *seq), None)
    return jax.shard_map(
        on_device, mesh=split_mesh, in_specs=in_specs, out_specs=out_specs, check_vma=False
    )
```

```python
import functools
import math

import jax
import jax.numpy as jnp
from jax import lax
from jax.experimental import pallas as pl
from jax.experimental.pallas import tpu as pltpu
from jax.sharding import PartitionSpec as P

P_SIZE = 64
N = 128
Q = 256
HALF = Q // 2
CORES = 2
NEVER = -1e30
VMEM_LIMIT = 60 * 1024 * 1024

f32 = jnp.float32
bf16 = jnp.bfloat16


def dot(a, b):
    return lax.dot_general(a, b, (((1,), (0,)), ((), ())), preferred_element_type=f32)


def exact_parts(value):
    high = value.astype(bf16)
    rest = value - high.astype(f32)
    middle = rest.astype(bf16)
    low = (rest - middle.astype(f32)).astype(bf16)
    return high, middle, low


def gates_kernel(heads, levels, padded, gates_ref, weight_ref, cum_ref, offset_ref, half_ref, decay_ref,
                 merge_ref, log_scratch):
    shards, _, span_rows, _ = gates_ref.shape
    spans = shards * span_rows
    upper = (
        lax.broadcasted_iota(jnp.int32, (Q, Q), 0) <= lax.broadcasted_iota(jnp.int32, (Q, Q), 1)
    ).astype(f32).astype(bf16)
    chunk = min(spans, 64)
    for head in range(heads):
        for shard in range(shards):
            rows = pl.ds(shard * span_rows, span_rows)
            gate = gates_ref[shard, 2 * head]
            step = gates_ref[shard, 2 * head + 1]
            high, middle, low = exact_parts(gate)
            cumulative = dot(high, upper) + dot(middle, upper) + dot(low, upper)
            span_log = cumulative[:, Q - 1 :]
            cum_ref[head, rows, :] = cumulative
            offset_ref[head, rows, :] = cumulative - jnp.log(step)
            half_log = cumulative[:, HALF - 1 : HALF]
            weight_ref[head, rows, :HALF] = jnp.exp(half_log - cumulative[:, :HALF]) * step[:, :HALF]
            weight_ref[head, rows, HALF:] = jnp.exp(span_log - cumulative[:, HALF:]) * step[:, HALF:]
            half_ref[head, rows, :] = jnp.broadcast_to(jnp.exp(span_log - half_log), (span_rows, N))
            log_scratch[rows, :] = jnp.broadcast_to(span_log, (span_rows, N))
        high, middle, low = exact_parts(log_scratch[...])

        def some_spans(at, carry):
            first = at * chunk
            size = (chunk * padded, spans)
            row = lax.broadcasted_iota(jnp.int32, size, 0)
            span = first + row // padded
            level = row % padded
            other = lax.broadcasted_iota(jnp.int32, size, 1)
            out_rows = pl.ds(pl.multiple_of(first * padded, chunk * padded), chunk * padded)
            bit = jnp.maximum(level - 1, 0)
            before = (other >= (span >> bit) << bit) & (other < span)
            before = before.astype(f32).astype(bf16)
            decay = dot(before, high) + dot(before, middle) + dot(before, low)
            has_bit = ((span >> bit) & 1)[:, :1] == 1
            decay_ref[head, out_rows, :] = jnp.where(has_bit, decay, NEVER)
            right = (other > span - (1 << bit)) & (other <= span)
            right = right.astype(f32).astype(bf16)
            merge_ref[head, out_rows, :] = jnp.exp(
                dot(right, high) + dot(right, middle) + dot(right, low)
            )
            return carry

        lax.fori_loop(0, spans // chunk, some_spans, 0)


def pick_set(step, starts, values):
    value = values[0]
    for start, other in zip(starts[1:], values[1:]):
        value = jnp.where(step >= start, other, value)
    return value


def pick(core, step, starts, pairs, local, group):
    half = group // CORES
    rows = slice(local % half * Q, (local % half + 1) * Q)
    mine = core == local // half
    return pick_set(step, starts, [jnp.where(mine, my_ref[rows, :], other_ref[rows, :]) for my_ref, other_ref in pairs])


def scaled(value, rows, width):
    parts = [value[head * width : (head + 1) * width] * row for head, row in enumerate(rows)]
    return jnp.concatenate(parts, axis=0) if len(parts) > 1 else parts[0]


def merge_blocks(left, right, merge_ref, row, width):
    return scaled(left, [merge_ref[head, row : row + 1, :] for head in range(merge_ref.shape[0])], width) + right


def states_kernel(heads, width, group, padded, starts, groups_ref, core_ref, x_ref, weight_ref, half_ref, merge_ref,
                  *refs):
    *key_refs, low_ref, total_ref = refs
    pairs = list(zip(key_refs[::2], key_refs[1::2]))
    kept = {}
    for local in range(group):
        columns = slice(local * Q, (local + 1) * Q)
        weights = [weight_ref[head, local : local + 1, :] for head in range(heads)]
        weighted = scaled(x_ref[:, columns].astype(f32), weights, width).astype(bf16)
        keys = pick(core_ref[0], pl.program_id(0), starts, pairs, local, group)
        first = dot(weighted[:, :HALF], keys[:HALF])
        low_ref[group + local] = first.astype(bf16)
        halves = [half_ref[head, local : local + 1, :] for head in range(heads)]
        state = scaled(first, halves, width) + dot(weighted[:, HALF:], keys[HALF:])
        bit = 0
        while local >> bit & 1:
            state = merge_blocks(kept[bit], state, merge_ref, local * padded + bit + 1, width)
            bit += 1
        kept[bit] = state
        low_ref[local] = state.astype(bf16)
    total_ref[...] = state


def tree_kernel(width, group, padded, groups_ref, merge_ref, *refs):
    *total_refs, high_ref, order_ref = refs
    steps = order_ref.shape[0]
    low_bits = group.bit_length() - 1
    at = 0
    for total_ref in total_refs:
        for slot in range(total_ref.shape[0]):
            order_ref[groups_ref[at]] = total_ref[slot]
            at += 1
    kept = {}
    for step in range(steps):
        state = order_ref[step]
        bit = 0
        while step >> bit & 1:
            row = step * padded + low_bits + bit + 1
            state = merge_blocks(kept[bit], state, merge_ref, row, width)
            bit += 1
        kept[bit] = state
        high_ref[step] = state.astype(bf16)


def outputs_kernel(heads, width, group, bits, padded, starts, groups_ref, core_ref, skip_ref, x_ref, high_ref,
                   cum_ref, offset_ref, decay_ref, level_ref, *refs):
    *set_refs, out_ref, query_ref, score_ref, sum_ref, factor_ref, own_ref, mixing_ref = refs
    set_refs = [set_refs[5 * at : 5 * at + 5] for at in range(len(starts))]
    key_pairs = [refs[0:2] for refs in set_refs]
    query_pairs = [refs[2:4] for refs in set_refs]
    low_refs = [refs[4] for refs in set_refs]
    at = pl.program_id(0)
    step = groups_ref[at]
    low_bits = group.bit_length() - 1
    levels = bits + 1
    causal = lax.broadcasted_iota(jnp.int32, (HALF, HALF), 0) <= lax.broadcasted_iota(
        jnp.int32, (HALF, HALF), 1
    )
    halves = slice(0, HALF), slice(HALF, Q)
    spans = [slice(local * Q, (local + 1) * Q) for local in range(group)]
    head_rows = [slice(head * width, (head + 1) * width) for head in range(heads)]
    high_slots = [
        jnp.maximum((step >> (bit - low_bits) << (bit - low_bits)) - 1, 0) for bit in range(low_bits, bits)
    ]
    offsets = [jnp.transpose(offset_ref[head]) for head in range(heads)]

    def low_state(slot):
        return pick_set(at, starts, [low_ref[slot] for low_ref in low_refs])

    for local, columns in enumerate(spans):
        query_ref[:, columns] = jnp.transpose(pick(core_ref[0], at, starts, query_pairs, local, group))
    right = lax.broadcasted_iota(jnp.int32, (1, Q), 1) >= HALF
    for local, columns in enumerate(spans):
        weights = level_ref[0, :, columns].astype(f32)
        for head in range(heads):
            cumulative = cum_ref[head, local : local + 1, :]
            weight = weights[head * levels : (head + 1) * levels]
            decay = decay_ref[head, local * padded : local * padded + levels, :]
            decay = jnp.concatenate([decay] * (Q // N), axis=1)
            factor_ref[head, :levels, columns] = weight * jnp.exp(cumulative + decay)
            own = cumulative + jnp.log(weight[:1])
            own_ref[head, :1, columns] = own
            across = jnp.exp(own - cumulative[:, HALF - 1 : HALF])
            factor_ref[head, :1, columns] = jnp.where(right, across, 0.0)

    for local, columns in enumerate(spans):
        keys = pick(core_ref[0], at, starts, key_pairs, local, group)
        active = [bit for bit in range(bits) if bit >= low_bits or local >> bit & 1]
        states = [low_state(group + local)]
        for bit in active:
            if bit < low_bits:
                states.append(low_state(((local >> bit) << bit) - 1))
            else:
                states.append(high_ref[high_slots[bit - low_bits]])
        result = dot(jnp.concatenate([keys] + states, axis=0), query_ref[:, columns])
        for half in halves:
            score_ref[local, half] = jnp.where(causal, result[half, half], 0.0)
        for head, rows in enumerate(head_rows):
            total = None
            for place, row in enumerate([0] + [bit + 1 for bit in active]):
                first_row = Q + place * heads * width + rows.start
                term = result[first_row : first_row + width] * factor_ref[head, row : row + 1, columns]
                total = term if total is None else total + term
            sum_ref[rows, columns] = total

    for local, columns in enumerate(spans):
        for head in range(heads):
            own = own_ref[head, :1, columns]
            column = offsets[head][:, local : local + 1]
            for half in halves:
                gaps = jnp.minimum(own[:, half] - column[half], 64.0)
                mixing_ref[local, head, half] = (score_ref[local, half] * jnp.exp(gaps)).astype(bf16)

    for local, columns in enumerate(spans):
        for head, rows in enumerate(head_rows):
            for half in halves:
                here = slice(columns.start + half.start, columns.start + half.stop)
                values = x_ref[rows, here]
                result = dot(values, mixing_ref[local, head, half]) + sum_ref[rows, here]
                out_ref[rows, here] = (result + skip_ref[head] * values.astype(f32)).astype(bf16)


def exchange(value, axis, distance):
    pairs = [(place, place ^ distance) for place in range(lax.axis_size(axis))]
    return lax.ppermute(value, axis, pairs)


def along_z(own):
    pieces = [own]
    for distance in range(1, lax.axis_size("z")):
        low = distance & -distance
        pieces.append(exchange(pieces[distance ^ low], "z", low))
    return pieces[1:]


def places():
    both = [(y, x) for y in range(lax.axis_size("y")) for x in range(lax.axis_size("x"))]
    return sorted(both, key=lambda place: ((place[0] > 0) + (place[1] > 0), place))


def straight(piece):
    near = {(0, 0): piece}
    for y, x in places():
        if (y > 0) != (x > 0):
            near[y, x] = exchange(piece, "x", x) if x else exchange(piece, "y", y)
    return near


def diagonal(near, by_x, by_y):
    far = {}
    for y, x in places():
        if y and x:
            parts = []
            if by_x is not None:
                parts.append(exchange(near[0, x][by_x], "y", y))
            if by_y is not None:
                parts.append(exchange(near[y, 0][by_y], "x", x))
            far[y, x] = parts
    return far


def join(parts):
    return jnp.concatenate(parts, axis=0) if len(parts) > 1 else parts[0]


def with_core(piece):
    return piece, exchange(piece, "core", 1)


def after(value, *others):
    return lax.optimization_barrier((value, *others))[0]


def on_device(x_heads, b_proj, c_proj, log_gate, step_size, level_weight, skip):
    rows, tokens = x_heads.shape
    head_count, tok_dev = log_gate.shape
    levels = level_weight.shape[1]
    bits = levels - 1
    shards = lax.axis_size(("z", "y"))
    span_rows = tok_dev // Q
    spans = tokens // Q
    heads = max(rows // P_SIZE, 1)
    width = rows // heads
    sharing = P_SIZE // width
    block = b_proj.shape[0]
    group = CORES * block // Q
    padded = -(-levels // 8) * 8
    steps = spans // group
    per_shard = span_rows // group

    def to_owners(value):
        value = jnp.repeat(value, sharing, axis=0) if sharing > 1 else value
        value = value.reshape((shards, heads) + value.shape[1:])
        return value.reshape((shards, -1) + value.shape[3:])

    gates = jnp.stack(
        [log_gate.reshape(head_count, span_rows, Q), step_size.reshape(head_count, span_rows, Q)], axis=1
    )
    gates = lax.all_to_all(to_owners(gates), ("z", "y"), split_axis=0, concat_axis=0, tiled=True)
    first_head = lax.axis_index(("z", "y")) * rows // P_SIZE
    own_skip = lax.dynamic_slice_in_dim(skip, first_head, heads, 0)
    core = lax.axis_index("core").astype(jnp.int32).reshape(1)

    def group_ids(place, z=None):
        z = lax.axis_index("z") ^ jnp.arange(1, lax.axis_size("z")) if z is None else z
        y = lax.axis_index("y") ^ place[0]
        x = lax.axis_index("x") ^ place[1]
        return ((z * lax.axis_size("y") + y) * lax.axis_size("x") + x).astype(jnp.int32)

    params = pltpu.CompilerParams(vmem_limit_bytes=VMEM_LIMIT)
    key_near = straight(b_proj)
    key_line = along_z(b_proj)
    query_near = straight(c_proj)
    crossed = [near[place] for near in (key_near, query_near) for place in places() if place in near and any(place)]
    everything = slice(None)
    key_near.update({place: join(parts) for place, parts in diagonal(key_near, everything, None).items()})
    query_near.update({place: join(parts) for place, parts in diagonal(query_near, None, everything).items()})
    query_line = along_z(after(c_proj, *key_line))
    keys_here = with_core(join([key_near[place] for place in places()]))
    queries_here = with_core(join([query_near[place] for place in places()]))

    params = pltpu.CompilerParams(vmem_limit_bytes=VMEM_LIMIT)
    weight, cumulative, offset, half, decay, merge = pl.pallas_call(
        functools.partial(gates_kernel, heads, levels, padded),
        out_shape=[jax.ShapeDtypeStruct((heads, spans, Q), f32)] * 3
        + [jax.ShapeDtypeStruct((heads, spans, N), f32)]
        + [jax.ShapeDtypeStruct((heads, spans * padded, N), f32)] * 2,
        scratch_shapes=[pltpu.VMEM((spans, N), f32)],
        compiler_params=params,
        name="gates",
    )(gates)
    weight, cumulative, offset = [v.reshape(heads, steps, group, Q) for v in (weight, cumulative, offset)]
    half = half.reshape(heads, steps, group, N)
    last_merge = merge.reshape(heads, steps, group * padded, N)[:, :, -padded:].reshape(heads, steps * padded, N)
    level_rows = lax.all_to_all(
        to_owners(after(level_weight, gates).astype(bf16)), ("z", "y"), split_axis=0, concat_axis=0, tiled=True
    )

    x_spec = pl.BlockSpec((rows, group * Q), lambda i, ids, *_: (0, ids[i]))
    span_spec = pl.BlockSpec((heads, None, group, Q), lambda i, ids, *_: (0, ids[i], 0, 0))
    level_spec = pl.BlockSpec((heads, group * padded, N), lambda i, ids, *_: (0, ids[i], 0))
    half_spec = pl.BlockSpec((heads, None, group, N), lambda i, ids, *_: (0, ids[i], 0, 0))
    low_slots = 2 * group
    vmem = pl.BlockSpec(memory_space=pltpu.VMEM)

    def within(start, count, base, trailing):
        return lambda i, *_: (jnp.clip(i - start, 0, count - 1) + base,) + (0,) * trailing

    def first_steps(id_lists):
        return [sum(ids.shape[0] for ids in id_lists[:at]) for at in range(len(id_lists))]

    totals, all_ids = [], []

    def states(sets):
        starts = first_steps([ids for ids, _ in sets])
        ids = join([ids for ids, _ in sets])
        count = ids.shape[0]
        key_specs = [
            pl.BlockSpec((block, N), within(start, own.shape[0], 0, 1)) for start, (own, _) in zip(starts, sets)
        ]
        low, total = pl.pallas_call(
            functools.partial(states_kernel, heads, width, group, padded, starts),
            grid_spec=pltpu.PrefetchScalarGridSpec(
                num_scalar_prefetch=2,
                grid=(count,),
                in_specs=[x_spec, span_spec, half_spec, level_spec] + [spec for spec in key_specs for _ in range(CORES)],
                out_specs=[
                    pl.BlockSpec((None, low_slots, rows, N), lambda i, *_: (i, 0, 0, 0)),
                    pl.BlockSpec((None, rows, N), lambda i, *_: (i, 0, 0)),
                ],
            ),
            out_shape=[
                jax.ShapeDtypeStruct((count, low_slots, rows, N), bf16),
                jax.ShapeDtypeStruct((count, rows, N), f32),
            ],
            compiler_params=params,
            cost_estimate=pl.CostEstimate(
                flops=2 * rows * count * group * Q * N,
                bytes_accessed=4 * count * group * Q * (rows + N),
                transcendentals=0,
            ),
            name="states",
        )(ids, core, x_heads, weight, half, merge, *[key for _, keys in sets for key in keys])
        totals.append(total)
        all_ids.append(ids)
        return [(low, start) for start in starts]

    def outputs(sets, out):
        starts = first_steps([ids for ids, *_ in sets])
        ids = join([ids for ids, *_ in sets])
        count = ids.shape[0]
        tokens_here = count * group * Q
        set_specs, operands = [], []
        for start, (own, keys, queries, (low, base)) in zip(starts, sets):
            set_specs += [pl.BlockSpec((block, N), within(start, own.shape[0], 0, 1))] * (2 * CORES)
            set_specs.append(pl.BlockSpec((None, low_slots, rows, N), within(start, own.shape[0], base, 3)))
            operands += [*keys, *queries, low]
        before = [] if out is None else [out]
        fixed = [
            pl.BlockSpec(memory_space=pltpu.SMEM),
            x_spec,
            vmem,
            span_spec,
            span_spec,
            level_spec,
            pl.BlockSpec(
                (1, heads * levels, group * Q),
                lambda i, ids, *_: (ids[i] // per_shard, 0, ids[i] % per_shard),
            ),
        ]

        def kernel(*refs):
            last = 2 + len(fixed) + len(set_specs)
            outputs_kernel(
                heads, width, group, bits, padded, starts, *refs[:last], *refs[last + len(before) :]
            )

        return pl.pallas_call(
            kernel,
            grid_spec=pltpu.PrefetchScalarGridSpec(
                num_scalar_prefetch=2,
                grid=(count,),
                in_specs=fixed + set_specs + [pl.BlockSpec(memory_space=pl.ANY)] * len(before),
                out_specs=x_spec,
                scratch_shapes=[
                    pltpu.VMEM((N, group * Q), bf16),
                    pltpu.VMEM((group, Q, HALF), f32),
                    pltpu.VMEM((rows, group * Q), f32),
                    pltpu.VMEM((heads, padded, group * Q), f32),
                    pltpu.VMEM((heads, 8, group * Q), f32),
                    pltpu.VMEM((group, heads, Q, HALF), bf16),
                ],
            ),
            out_shape=jax.ShapeDtypeStruct((rows, tokens), bf16),
            input_output_aliases={2 + len(fixed) + len(set_specs): 0} if before else {},
            compiler_params=params,
            cost_estimate=pl.CostEstimate(
                flops=2 * tokens_here * (Q * N + rows * Q + bits * rows * N),
                bytes_accessed=4 * tokens_here * (rows + N),
                transcendentals=heads * tokens_here * Q,
            ),
            name="outputs",
        )(ids, core, own_skip, x_heads, high, cumulative, offset, decay, level_rows, *operands, *before)

    here = join([group_ids(place, lax.axis_index("z").reshape(1)) for place in places()])
    one = (0, 0)
    sides = [place for place in places() if (place[0] > 0) != (place[1] > 0)]
    corners = [place for place in places() if place[0] and place[1]]
    far_ids = {place: group_ids(place) for place in places()}
    lows = {}
    if key_line:
        cut = block * ((len(key_line) + 1) // 3)
        by_x, by_y = slice(0, cut), slice(cut, None)
        key_far = straight(after(join(key_line), *crossed))
        keys_far = {one: with_core(key_far[one])}
        low_here, lows[one] = states([(here, keys_here), (far_ids[one], keys_far[one])])
        query_own = join(query_line)
        ready = (totals[0], query_own, queries_here[0])
        query_far = straight(after(query_own, *[key_far[place] for place in sides]))
        if sides:
            tied = {place: after(key_far[place], *ready) for place in sides}
            parts = diagonal(tied, by_x, by_y)
            keys_far.update({place: with_core(key_far[place]) for place in sides})
            lows.update(zip(sides, states([(far_ids[place], keys_far[place]) for place in sides])))
            if corners:
                joined = {place: join([after(part, totals[1]) for part in parts[place]]) for place in corners}
                keys_far.update({place: with_core(joined[place]) for place in corners})
                lows.update(zip(corners, states([(far_ids[place], keys_far[place]) for place in corners])))
    else:
        (low_here,) = states([(here, keys_here)])

    high = pl.pallas_call(
        functools.partial(tree_kernel, width, group, padded),
        grid_spec=pltpu.PrefetchScalarGridSpec(
            num_scalar_prefetch=1,
            in_specs=[vmem] * (1 + len(totals)),
            out_specs=vmem,
            scratch_shapes=[pltpu.VMEM((steps, rows, N), f32)],
        ),
        out_shape=jax.ShapeDtypeStruct((steps, rows, N), bf16),
        compiler_params=params,
        name="tree",
    )(join(all_ids), last_merge, *totals)

    out = outputs([(here, keys_here, queries_here, low_here)], None)
    if key_line:
        tied = {place: after(query_far[place], out) for place in sides}
        parts = diagonal(tied, by_x, by_y)
        queries_far = {place: with_core(query_far[place] if place == one else tied[place]) for place in [one] + sides}

        def far_sets(some):
            return [(far_ids[place], keys_far[place], queries_far[place], lows[place]) for place in some]

        early = [one] + sides[: len(sides) // 2]
        late = sides[len(sides) // 2 :]
        out = outputs(far_sets(early), out)
        for place in corners:
            queries_far[place] = with_core(join([after(part, out) for part in parts[place]]))
        if late or corners:
            out = outputs(far_sets(late + corners), out)
    return out


def solution(mesh):
    x = mesh.shape["head"] // CORES
    y = math.gcd(mesh.shape["seq"], x)
    z = mesh.shape["seq"] // y
    split_mesh = jax.sharding.Mesh(mesh.devices.reshape(z, y, x, CORES), ("z", "y", "x", "core"))
    seq = ("z", "y")
    head = ("x", "core")
    in_specs = (
        P((*head, *seq), None),
        P((*seq, *head), None),
        P((*seq, *head), None),
        P(head, seq),
        P(head, seq),
        P(head, None, seq),
        P(head),
    )
    out_specs = P((*head, *seq), None)
    return jax.shard_map(
        on_device, mesh=split_mesh, in_specs=in_specs, out_specs=out_specs, check_vma=False
    )
```
